32 devices in a mesh: dp: 8 (over z, core), tensor: 4 (over y, x).
Axes of the slice: x: 2, y: 2, z: 4, core: 2. Of those that a mesh axis runs over, the one named last changes fastest.
Arguments:
- attn_out: bfloat16 [2048, 8192], P('dp', 'tensor'), parts along dimension 0, may hold values from -6 to 6
- head_signs: int32 [64], replicated, may hold values from 0 to 1
- w_out: bfloat16 [8192, 8192], P('tensor'), may hold values from -0.09375 to 0.09375
- out_exp: int32 [8192], P('tensor'), may hold values from -2 to 1
- residual: bfloat16 [2048, 8192], P('dp', 'tensor'), parts along dimension 0, may hold values from -60 to 60
- norm_gain: bfloat16 [8192], P('tensor'), may hold values from 0.25 to 1.75
- w_kv: bfloat16 [8192, 2048], P(None, 'tensor'), may hold values from -0.0625 to 0.0625
- kv_exp: int32 [2048], P('tensor'), may hold values from -2 to 1
Outputs:
- resid_out: bfloat16 [2048, 8192], P('dp', 'tensor'), parts along dimension 0
- kv: bfloat16 [2048, 2048], P('dp', 'tensor'), parts along dimension 0
The draws below stay inside these ranges and needn't reach their ends.
There are 8 independent parts, one for each index of `dp`. The reference program is written for one: setup_inputs(seed, part) draws one part's arguments, and reference() takes and returns one part's arrays. A program takes and returns all parts, laid end to end along the dimension named above; an argument that names none is the same for every part. Nothing has to cross between parts.
Inputs may be any that keep to these rules, and one draw needn't show every extreme that they name: The sign of head h is 2 head_signs[h] - 1.
All inputs are finite; a program needn't handle non-finite values.
Results may differ from the reference program's by a relative error of at most 0.025.
Values may be sent and summed in bfloat16 or wider, within the bound.
No kernel may reach another device: no remote copies, remote signals or barrier semaphores. Data moves between devices by JAX's collectives and lax.ppermute only.
A program may use at most 128 MiB of HBM per device.

```python
import jax
import jax.numpy as jnp
from jax import lax

HEADS = 64
HD = 128
D = 8192
TOK = 256
KV_COLS = 2048
N_TENSOR = 4


def draw_residual(key, part):
    key = jax.random.fold_in(key, 7)
    key_base, key_cols, key_rows = jax.random.split(key, 3)
    col_ramp = 10.0 ** (jnp.arange(D, dtype=jnp.float32) / D - 0.5)
    col_rough = jax.random.uniform(key_cols, (D,), jnp.float32, 0.6, 1.4)
    row_scale = 10.0 ** jax.random.uniform(key_rows, (TOK, 1), jnp.float32, -0.5, 0.5)
    base = jax.random.truncated_normal(key_base, -5.0, 5.0, (TOK, D), jnp.float32)
    return (0.5 * base * row_scale * col_ramp[None, :] * col_rough[None, :]).astype(jnp.bfloat16)


def touch_ends(entries, rng, low, top_value):
    longest = entries.shape.index(max(entries.shape))
    spots = []
    for shift in (0, 1):
        where = [jax.random.randint(jax.random.fold_in(rng, axis), (), 0, length) for axis, length in enumerate(entries.shape)]
        where[longest] = (where[longest] + shift) % entries.shape[longest]
        spots.append(tuple(where))
    return entries.at[spots[0]].set(low).at[spots[1]].set(top_value)


def strengthened(entries, own_key, source, target, shards_of, factor):
    owner, partner = [(jnp.arange(entries.shape[axis_at]) // (entries.shape[axis_at] // shards_of)).reshape([-1 if axis == axis_at else 1 for axis in range(entries.ndim)]) for axis_at in (source, target)]
    chosen = jax.random.permutation(own_key, shards_of)[partner]
    strong = (owner == chosen) | (owner == (partner + shards_of // 2) % shards_of)
    return jnp.where(strong, factor * entries, entries)


def shard_levels(key, dims, cuts, least, top_value):
    factor_of = 1.0
    for position, parts in cuts:
        steps = jax.random.uniform(jax.random.fold_in(jax.random.fold_in(key, 6), position), (parts,), jnp.float32, least / len(cuts), top_value / len(cuts))
        factor_of = factor_of * jnp.repeat(jnp.exp(steps), dims[position] // parts).reshape((-1,) + (1,) * (len(dims) - 1 - position))
    return factor_of


def gaussian(rng, shape, spread, bound, cuts=(), kind=jnp.bfloat16):
    loudness = shard_levels(rng, shape, cuts, -0.22, 0.18) if cuts else 1.0
    result = jax.random.normal(rng, shape, jnp.float32) * spread * loudness
    return jnp.minimum(jnp.maximum(result, -bound), bound).astype(kind)


def bell_draw_with(stream_key, dims, scale, most, shards, heavy, kind=jnp.bfloat16):
    array = scale * jax.random.normal(stream_key, dims, jnp.float32)
    if shards:
        array = array * shard_levels(stream_key, dims, shards, -0.22, 0.18)
    return jnp.clip(strengthened(array, jax.random.fold_in(stream_key, 3), *heavy), -most, most).astype(kind)


def setup_inputs(seed: int = 0, part: int = 0) -> dict:
    keys = jax.random.split(jax.random.key(seed), 9)
    part_splits = jax.random.split(jax.random.fold_in(keys[8], part), 9)
    return {
        "attn_out": gaussian(part_splits[0], (TOK, HEADS * HD), 1.0, 6.0, ((1, 4),)),
        "head_signs": touch_ends(jax.random.randint(keys[1], (HEADS,), 0, 2), jax.random.fold_in(keys[1], 1), 0, 1).astype(jnp.int32),
        "w_out": bell_draw_with(keys[2], (HEADS * HD, D), (HEADS * HD) ** -0.5, 0.09375, ((0, 4),), (0, 1, 4, 2.0)),
        "out_exp": touch_ends(jax.random.randint(keys[3], (D,), -2, 2), jax.random.fold_in(keys[3], 1), -2, 1).astype(jnp.int32),
        "residual": draw_residual(jax.random.fold_in(jax.random.fold_in(keys[8], part), 71), part),
        "norm_gain": jnp.clip(1.0 + 0.15 * jax.random.normal(keys[5], (D,), jnp.float32), 0.25, 1.75).astype(jnp.bfloat16),
        "w_kv": gaussian(keys[6], (D, KV_COLS), D ** -0.5, 0.0625, ((1, 4),)),
        "kv_exp": touch_ends(jax.random.randint(keys[7], (KV_COLS,), -2, 2), jax.random.fold_in(keys[7], 1), -2, 1).astype(jnp.int32),
    }


def sylvester(order):
    row_ids = jnp.arange(order, dtype=jnp.int32)
    parity = jnp.zeros((order, order), jnp.int32)
    for bit_level in range(order.bit_length() - 1):
        parity = parity ^ row_ids[:, None] >> bit_level & row_ids[None, :] >> bit_level & 1
    return (1 - 2 * parity).astype(jnp.float32)

def reference(attn_out, head_signs, w_out, out_exp, residual, norm_gain, w_kv, kv_exp):
    tok_rows = attn_out.shape[0]
    sign_values = (2 * head_signs - 1).astype(jnp.float32)
    signed = attn_out.astype(jnp.float32).reshape(tok_rows, HEADS, HD) * sign_values[None, :, None]
    blended = jnp.einsum('thd,hg->tgd', signed, sylvester(HEADS), precision=lax.Precision.HIGHEST)
    rotated = (blended * HEADS ** (-0.5)).astype(jnp.bfloat16).reshape(tok_rows, HEADS * HD)
    group_rows = HEADS * HD // N_TENSOR
    pieces = rotated.reshape(tok_rows, N_TENSOR, group_rows).transpose(1, 0, 2)
    weights = w_out.reshape(N_TENSOR, group_rows, D)

    def accumulate(running, operands):
        dev_term = jnp.dot(operands[0], operands[1], preferred_element_type=jnp.float32)
        rounded = lax.optimization_barrier(dev_term.astype(jnp.bfloat16))
        return (running + rounded.astype(jnp.float32), None)
    summed, _ = lax.scan(accumulate, jnp.zeros((tok_rows, D), jnp.float32), (pieces, weights))
    projected = summed * jnp.exp2(out_exp.astype(jnp.float32))[None, :]
    resid_out = (residual.astype(jnp.float32) + projected).astype(jnp.bfloat16)
    hidden_f = resid_out.astype(jnp.float32)
    mean_sq = lax.optimization_barrier(jnp.mean(hidden_f * hidden_f, axis=1))
    normed = (hidden_f * lax.rsqrt(mean_sq + 1e-05)[:, None] * norm_gain.astype(jnp.float32)[None, :]).astype(jnp.bfloat16)
    kv_acc = jnp.dot(normed, w_kv, preferred_element_type=jnp.float32)
    kv = (kv_acc * jnp.exp2(kv_exp.astype(jnp.float32))[None, :]).astype(jnp.bfloat16)
    return (resid_out, kv)
```

```python
import functools

import jax
import jax.numpy as jnp
from jax import lax
from jax.experimental import pallas as pl
from jax.experimental.pallas import tpu as pltpu
from jax.sharding import PartitionSpec as P

HD = 128
EPS = 1e-05
PARTS = 2
ROWS = 16
VMEM = 24 * 1024 * 1024
PROJECT_FLOPS = 1e6


def cost(flops, nbytes):
    return pl.CostEstimate(flops=int(flops), bytes_accessed=int(nbytes), transcendentals=0)


def call(kernel, grid, scalars, in_specs, args, outs, estimate, scratch=()):
    return pl.pallas_call(
        kernel,
        grid_spec=pltpu.PrefetchScalarGridSpec(
            num_scalar_prefetch=len(scalars),
            grid=(grid,),
            in_specs=in_specs,
            out_specs=[spec for _, _, spec in outs],
            scratch_shapes=[pltpu.VMEM(shape, dtype) for shape, dtype in scratch],
        ),
        out_shape=[jax.ShapeDtypeStruct(shape, dtype) for shape, dtype, _ in outs],
        compiler_params=pltpu.CompilerParams(vmem_limit_bytes=VMEM),
        cost_estimate=estimate,
    )(*scalars, *args)


def whole(shape):
    return pl.BlockSpec(shape, lambda *_: (0,) * len(shape))


def swap(block, bit, count):
    return lax.ppermute(block, "tensor", [(i, i ^ 1 << bit) for i in range(count)])


def mix_kernel(part, heads, me_ref, signs_ref, attn, *outs):
    me = me_ref[0]
    half = heads // PARTS
    size = outs[0].shape[0]
    for c in range(len(outs) // 2):
        full, sent = outs[2 * c : 2 * c + 2]

        @pl.loop(0, size // ROWS)
        def _(i):
            at = pl.ds(pl.multiple_of(c * size + i * ROWS, ROWS), ROWS)
            rows = pl.ds(pl.multiple_of(i * ROWS, ROWS), ROWS)

            def head(h):
                sign = (2 * signs_ref[me * heads + h] - 1).astype(jnp.float32)
                return attn[at, pl.ds(h * HD, HD)].astype(jnp.float32) * sign

            v = []
            for h in range(half):
                a, b = head(h), head(h + half)
                v.append(a - b if part else a + b)
            step = 1
            while step < half:
                for lo in range(half):
                    if not lo & step:
                        a, b = v[lo], v[lo | step]
                        v[lo], v[lo | step] = a + b, a - b
                step *= 2
            for h in range(half):
                cols = pl.ds(h * HD, HD)
                full[rows, cols] = v[h]
                sent[rows, cols] = v[h].astype(sent.dtype)


def mix(attn, me, signs, part, colors):
    rows, cols = attn.shape
    shape = (rows // colors, cols // PARTS)
    return call(
        functools.partial(mix_kernel, part, cols // HD),
        1,
        [me, signs],
        [whole(attn.shape)],
        [attn],
        [(shape, d, whole(shape)) for _ in range(colors) for d in (jnp.float32, jnp.bfloat16)],
        cost(6 * attn.size, 5 * attn.size),
    )


def combine(order, me, own, recvs, rows):
    v = own[rows, :]
    for bit, recv in zip(order, recvs):
        flip = (1 - 2 * (me >> bit & 1)).astype(jnp.float32)
        v = recv[rows, :].astype(jnp.float32) + flip * v
    return v


def stage_kernel(orders, scale, me_ref, *refs):
    ins, out = refs[:-1], refs[-1]
    me = me_ref[0]
    per = len(ins) // len(orders)
    for c, order in enumerate(orders):
        own, *recvs = ins[c * per : (c + 1) * per]
        size = own.shape[0]

        @pl.loop(0, size // ROWS)
        def _(i):
            rows = pl.ds(pl.multiple_of(i * ROWS, ROWS), ROWS)
            to = pl.ds(pl.multiple_of(c * size + i * ROWS, ROWS), ROWS)
            out[to, :] = (combine(order, me, own, recvs, rows) * scale).astype(out.dtype)


def stage(blocks, orders, me, scale):
    flat = [b for block in blocks for b in block]
    rows, cols = flat[0].shape
    shape = (rows * len(blocks), cols)
    return call(
        functools.partial(stage_kernel, orders, scale),
        1,
        [me],
        [whole(f.shape) for f in flat],
        flat,
        [(shape, jnp.bfloat16, whole(shape))],
        cost(4 * rows * cols * len(flat), 2 * rows * cols * (len(flat) + 2)),
    )[0]


def send_lists(order):
    lists = []
    for s, bit in enumerate(order):
        members = [1 << bit]
        for later in reversed(order[s + 1 :]):
            members = members + [m | 1 << later for m in members]
        lists.append(members)
    return lists + [[0]]


def project_kernel(plan, parts, extras, tbl_ref, *refs):
    rots, ws, refs = refs[:parts], refs[parts : 2 * parts], refs[2 * parts :]
    adds, outs = refs[:extras], refs[extras:]
    i = pl.program_id(0)
    acc = jnp.dot(rots[0][...], ws[0][...], preferred_element_type=jnp.float32)
    for rot, w in zip(rots[1:], ws[1:]):
        acc = acc + jnp.dot(rot[...], w[...], preferred_element_type=jnp.float32)
    for step, (out, add, lead) in enumerate(plan):

        @pl.when(i == step)
        def _():
            total = acc if add is None else acc + adds[add][lead].astype(jnp.float32)
            outs[out][0] = total.astype(outs[out].dtype)


def project(rots, parts, w_out, tbl, spans, shift, width, dtypes, adds=(), plan=None):
    rows, depth = rots[0].shape
    steps = sum(count for _, count in spans)
    if plan is None:
        plan = [
            (k, k if adds else None, n) for k, (_, count) in enumerate(spans) for n in range(count)
        ]

    def w_map(k):
        return lambda i, t: (k, t[i] + shift)

    def out_map(first, count):
        return lambda i, t: (jnp.clip(i - first, 0, count - 1), 0, 0)

    return call(
        functools.partial(project_kernel, plan, len(parts), len(adds)),
        steps,
        [tbl],
        [whole((rows, depth)) for _ in parts]
        + [pl.BlockSpec((depth, width), w_map(k)) for k in parts]
        + [whole(add.shape) for add in adds],
        [*[rots[k] for k in parts], *[w_out] * len(parts), *adds],
        [
            ((n, rows, width), dtype, pl.BlockSpec((1, rows, width), out_map(at, n)))
            for (at, n), dtype in zip(spans, dtypes)
        ],
        cost(PROJECT_FLOPS, 0),
    )


def close_kernel(colors, residual, exps, *refs):
    terms, out = refs[:-1], refs[-1]
    per = len(terms) // colors
    width = residual.shape[1] // colors
    for c in range(colors):
        cols = pl.ds(c * width, width)
        own, *recvs = terms[c * per : (c + 1) * per]
        acc = own[0].astype(jnp.float32)
        for recv in recvs:
            acc = acc + recv[0].astype(jnp.float32)
        acc = acc * jnp.exp2(exps[:, cols].astype(jnp.float32))
        out[c] = (residual[:, cols].astype(jnp.float32) + acc).astype(jnp.bfloat16)


def close(residual, exps, terms, at):
    colors = len(terms)
    _, rows, width = terms[0][0].shape
    span = width * colors
    flat = [t for color in terms for t in color]
    shape = (colors, rows, width)
    return call(
        functools.partial(close_kernel, colors),
        1,
        [],
        [
            pl.BlockSpec((rows, span), lambda i: (0, at)),
            pl.BlockSpec((1, span), lambda i: (0, at)),
        ]
        + [whole((1, rows, width))] * len(flat),
        [residual, exps, *flat],
        [(shape, jnp.bfloat16, whole(shape))],
        cost(10 * rows * span, 2 * rows * width * (len(flat) + 2 * colors)),
    )[0]


def kv_kernel(plan, count, has_prev, channels, tbl_ref, w, *refs):
    xs, gains, rest = refs[:count], refs[count : count + len(plan)], refs[count + len(plan) :]
    prev, rest = (rest[:2], rest[2:]) if has_prev else (None, rest)
    acc, total = rest[-2:]
    i = pl.program_id(0)

    @pl.when(i == 0)
    def _():
        acc[...] = prev[0][...] if has_prev else jnp.zeros_like(acc)
        total[...] = prev[1][...] if has_prev else jnp.zeros_like(total)

    for step, blocks in enumerate(plan):

        @pl.when(i == step)
        def _():
            product, square = acc[...], total[...]
            for k, at, c in blocks:
                hidden = xs[k][at].astype(jnp.float32)
                depth = hidden.shape[1]
                cols = pl.ds(c * depth, depth)
                scaled = (hidden * gains[step][:, cols].astype(jnp.float32)).astype(jnp.bfloat16)
                product = product + jnp.dot(
                    scaled, w[cols, :], preferred_element_type=jnp.float32
                )
                hidden = hidden * hidden
                for b in range(depth // HD):
                    square = square + hidden[:, b * HD : (b + 1) * HD]
            acc[...], total[...] = product, square

    if channels:
        exps, out = rest[0], rest[1]

        @pl.when(i == len(plan) - 1)
        def _():
            mean = jnp.sum(total[...], axis=1, keepdims=True) / channels
            scale = jnp.exp2(exps[...].astype(jnp.float32))
            out[...] = (acc[...] * lax.rsqrt(mean + EPS) * scale).astype(out.dtype)


def kv_step(plan, arrays, gains, w_kv, tbl, at, span, prev, exps, channels):
    used = sorted({k for blocks in plan for k, _, _ in blocks})
    xs = [arrays[k] for k in used]
    plan = [[(used.index(k), lead, c) for k, lead, c in blocks] for blocks in plan]
    rows = xs[0].shape[1]
    cols = w_kv.shape[1]
    extra = list(prev or ())
    running = [((rows, cols), jnp.float32), ((rows, HD), jnp.float32)]
    if channels:
        extra.append(exps)
        outs, scratch = [((rows, cols), jnp.bfloat16)], running
    else:
        outs, scratch = running, []
    return call(
        functools.partial(kv_kernel, plan, len(xs), prev is not None, channels),
        len(plan),
        [tbl],
        [pl.BlockSpec((span, cols), lambda i, t: (t[i] + at, 0))]
        + [whole(x.shape) for x in xs]
        + [pl.BlockSpec((1, span), lambda i, t: (0, at))] * len(gains)
        + [whole(e.shape) for e in extra],
        [w_kv, *xs, *gains, *extra],
        [(shape, dtype, whole(shape)) for shape, dtype in outs],
        cost(
            2 * rows * span * cols * len(plan), 2 * span * (rows + cols) * len(plan) + 4 * rows * cols
        ),
        scratch,
    )


def gather(x, orders, count):
    colors = x.shape[0]
    arrays, where = [x], {0: [(0, c) for c in range(colors)]}
    levels = len(orders[0])
    for bit in range(levels):
        arrays.append(swap(x, bit, count))
        where[1 << bit] = [(len(arrays) - 1, c) for c in range(colors)]
    for size in range(2, levels + 1):
        for r in range(count):
            if r.bit_count() == size:
                where[r] = []
                for c, order in enumerate(orders):
                    hop = max((b for b in range(levels) if r >> b & 1), key=order.index)
                    k, at = where[r ^ 1 << hop][c]
                    arrays.append(swap(arrays[k][at : at + 1], hop, count))
                    where[r].append((len(arrays) - 1, 0))
    plan = [[(k, at, c) for c, (k, at) in enumerate(blocks)] for blocks in where.values()]
    return arrays, list(zip(where, plan))


def body(attn_out, head_signs, w_out, out_exp, residual, norm_gain, w_kv, kv_exp):
    count = lax.axis_size("tensor")
    levels = count.bit_length() - 1
    me = lax.axis_index("tensor").astype(jnp.int32)
    me_arr = me.reshape(1)
    local = residual.shape[1]
    channels = local * count
    orders = [list(range(levels))]
    orders.append(orders[0][levels // 2 :] + orders[0][: levels // 2])
    colors = len(orders)

    cuts = (8, 8, 4) if local >= 8 * HD else (4, 4) if local >= 4 * HD else (2,)
    units, first = [], 0
    for cut in cuts:
        units.append((first, local // cut))
        first += colors * local // cut

    lists = [send_lists(order) for order in orders]

    def blocks_of(stages, width):
        spans, rel, color = [], [], []
        for s in stages:
            for c in range(colors):
                spans.append((len(rel), len(lists[c][s])))
                rel += lists[c][s]
                color += [c] * len(lists[c][s])
        tbl = (me ^ jnp.array(rel, jnp.int32)) * (local // width) + jnp.array(color, jnp.int32)
        return tbl, spans

    exps = out_exp.reshape(1, -1)
    kv_exps = kv_exp.reshape(1, -1)
    gains = [norm_gain.reshape(1, -1)]
    for r in range(1, count):
        gains.append(lax.ppermute(gains[0], "tensor", [(i, i ^ r) for i in range(count)]))

    rots, blocks = [], []
    for p in range(PARTS):
        mixed = mix(attn_out, me_arr, head_signs, p, colors)
        blocks.append([])
        for c, order in enumerate(orders):
            own, sent = mixed[2 * c : 2 * c + 2]
            blocks[p].append([own, swap(sent, order[0], count)])
    for s in range(1, levels):
        for p in range(PARTS):
            for c, order in enumerate(orders):
                send = stage([blocks[p][c]], [order], me_arr, 1.0)
                blocks[p][c].append(swap(send, order[s], count))
    for p in range(PARTS):
        rots.append(stage(blocks[p], orders, me_arr, head_signs.shape[0] ** -0.5))

    ahead = 2 if len(units) > 2 else 1
    bf16, f32 = jnp.bfloat16, jnp.float32
    received = []
    for u, (first, width) in enumerate(units):
        tbl, spans = blocks_of([0], width)
        prevs, todo, at = (), list(range(PARTS)), first // width
        if u < ahead:
            prevs = project(rots, todo[:-1], w_out, tbl, spans, at, width, [f32] * colors)
            todo = todo[-1:]
        sends = project(rots, todo, w_out, tbl, spans, at, width, [bf16] * colors, prevs)
        received.append([swap(send, order[0], count) for send, order in zip(sends, orders)])

    later = range(1, levels + 1)
    plan = []
    for s in later:
        for c in range(colors):
            n = len(lists[c][s])
            lead = n if s < levels else 0
            plan += [((s - 1) * colors + c, c, lead + k) for k in range(n)]
    dtypes = [bf16 if s == 1 and levels > 1 else f32 for s in later for _ in range(colors)]

    resids, running = [], None
    for u, (first, width) in enumerate(units):
        tbl, spans = blocks_of(later, width)
        parts = project(
            rots, list(range(PARTS)), w_out, tbl, spans, first // width, width, dtypes,
            received[u], plan,
        )
        terms = []
        for c, order in enumerate(orders):
            recvs = []
            for s in range(1, levels):
                send = parts[(s - 1) * colors + c]
                if recvs:
                    size = send.shape[0]
                    for recv in recvs:
                        send = send + recv[size : 2 * size].astype(f32)
                    send = send.astype(bf16)
                recvs.append(swap(send, order[s], count))
            terms.append([parts[(levels - 1) * colors + c], *recvs])
        span = width * colors
        out = close(residual, exps, terms, first // span)
        resids += list(out)
        arrays, found = gather(out, orders, count)
        last = u == len(units) - 1
        near = [b for b in found if b[0].bit_count() < 2]
        far = [b for b in found if b[0].bit_count() >= 2]
        runs = [near, far] if last and far else [found]
        for k, run in enumerate(runs):
            tbl = (me ^ jnp.array([r for r, _ in run], jnp.int32)) * (local // span)
            running = kv_step(
                [plan for _, plan in run],
                arrays,
                [gains[r] for r, _ in run],
                w_kv,
                tbl,
                first // span,
                span,
                running,
                kv_exps,
                channels * (last and k == len(runs) - 1),
            )
    return jnp.concatenate(resids, axis=1), running[0]


def solution(mesh):
    placed = (
        P("dp", "tensor"),
        P(),
        P("tensor", None),
        P("tensor"),
        P("dp", "tensor"),
        P("tensor"),
        P(None, "tensor"),
        P("tensor"),
    )
    return jax.shard_map(
        body,
        mesh=mesh,
        in_specs=placed,
        out_specs=(P("dp", "tensor"), P("dp", "tensor")),
        check_vma=False,
    )
```

```python
import functools

import jax
import jax.numpy as jnp
from jax import lax
from jax.experimental import pallas as pl
from jax.experimental.pallas import tpu as pltpu
from jax.sharding import PartitionSpec as P

HD = 128
EPS = 1e-05
PARTS = 2
ROWS = 16
VMEM = 24 * 1024 * 1024
PROJECT_FLOPS = 1e6
AHEAD = 4


def cost(flops, nbytes):
    return pl.CostEstimate(flops=int(flops), bytes_accessed=int(nbytes), transcendentals=0)


def call(kernel, grid, scalars, in_specs, args, outs, estimate, scratch=()):
    return pl.pallas_call(
        kernel,
        grid_spec=pltpu.PrefetchScalarGridSpec(
            num_scalar_prefetch=len(scalars),
            grid=(grid,),
            in_specs=in_specs,
            out_specs=[spec for _, _, spec in outs],
            scratch_shapes=list(scratch),
        ),
        out_shape=[jax.ShapeDtypeStruct(shape, dtype) for shape, dtype, _ in outs],
        compiler_params=pltpu.CompilerParams(vmem_limit_bytes=VMEM),
        cost_estimate=estimate,
    )(*scalars, *args)


def whole(shape):
    return pl.BlockSpec(shape, lambda *_: (0,) * len(shape))


def swap(block, bit, count):
    return lax.ppermute(block, "tensor", [(i, i ^ 1 << bit) for i in range(count)])


def mix_kernel(part, heads, me_ref, signs_ref, attn, *outs):
    me = me_ref[0]
    half = heads // PARTS
    size = outs[0].shape[0]
    for c in range(len(outs) // 2):
        full, sent = outs[2 * c : 2 * c + 2]

        @pl.loop(0, size // ROWS)
        def _(i):
            at = pl.ds(pl.multiple_of(c * size + i * ROWS, ROWS), ROWS)
            rows = pl.ds(pl.multiple_of(i * ROWS, ROWS), ROWS)

            def head(h):
                sign = (2 * signs_ref[me * heads + h] - 1).astype(jnp.float32)
                return attn[at, pl.ds(h * HD, HD)].astype(jnp.float32) * sign

            v = []
            for h in range(half):
                a, b = head(h), head(h + half)
                v.append(a - b if part else a + b)
            step = 1
            while step < half:
                for lo in range(half):
                    if not lo & step:
                        a, b = v[lo], v[lo | step]
                        v[lo], v[lo | step] = a + b, a - b
                step *= 2
            for h in range(half):
                cols = pl.ds(h * HD, HD)
                full[rows, cols] = v[h]
                sent[rows, cols] = v[h].astype(sent.dtype)


def mix(attn, me, signs, part, colors):
    rows, cols = attn.shape
    shape = (rows // colors, cols // PARTS)
    return call(
        functools.partial(mix_kernel, part, cols // HD),
        1,
        [me, signs],
        [whole(attn.shape)],
        [attn],
        [(shape, d, whole(shape)) for _ in range(colors) for d in (jnp.float32, jnp.bfloat16)],
        cost(6 * attn.size, 5 * attn.size),
    )


def combine(order, me, own, recvs, rows):
    v = own[rows, :]
    for bit, recv in zip(order, recvs):
        flip = (1 - 2 * (me >> bit & 1)).astype(jnp.float32)
        v = recv[rows, :].astype(jnp.float32) + flip * v
    return v


def stage_kernel(orders, scale, me_ref, *refs):
    ins, out = refs[:-1], refs[-1]
    me = me_ref[0]
    per = len(ins) // len(orders)
    for c, order in enumerate(orders):
        own, *recvs = ins[c * per : (c + 1) * per]
        size = own.shape[0]

        @pl.loop(0, size // ROWS)
        def _(i):
            rows = pl.ds(pl.multiple_of(i * ROWS, ROWS), ROWS)
            to = pl.ds(pl.multiple_of(c * size + i * ROWS, ROWS), ROWS)
            out[to, :] = (combine(order, me, own, recvs, rows) * scale).astype(out.dtype)


def stage(blocks, orders, me, scale):
    flat = [b for block in blocks for b in block]
    rows, cols = flat[0].shape
    shape = (rows * len(blocks), cols)
    return call(
        functools.partial(stage_kernel, orders, scale),
        1,
        [me],
        [whole(f.shape) for f in flat],
        flat,
        [(shape, jnp.bfloat16, whole(shape))],
        cost(4 * rows * cols * len(flat), 2 * rows * cols * (len(flat) + 2)),
    )[0]


def send_lists(order):
    lists = []
    for s, bit in enumerate(order):
        members = [1 << bit]
        for later in reversed(order[s + 1 :]):
            members = members + [m | 1 << later for m in members]
        lists.append(members)
    return lists + [[0]]


def project_kernel(plan, parts, extras, shift, tbl_ref, w_hbm, *refs):
    rots, refs = refs[: len(parts)], refs[len(parts) :]
    adds, outs, (buf, sem) = refs[:extras], refs[extras:-2], refs[-2:]
    slots, depth, width = buf.shape
    step_depth = depth // len(parts)

    def copies(step):
        cols = pl.ds(pl.multiple_of((tbl_ref[step] + shift) * width, width), width)
        slot = step % slots
        return [
            pltpu.make_async_copy(
                w_hbm.at[pl.ds(k * step_depth, step_depth), cols],
                buf.at[slot, pl.ds(n * step_depth, step_depth), :],
                sem.at[slot, n],
            )
            for n, k in enumerate(parts)
        ]

    for step in range(min(slots, len(plan))):
        for copy in copies(step):
            copy.start()
    for step, (out, lead, add, add_lead) in enumerate(plan):
        acc = None
        for n, (rot, copy) in enumerate(zip(rots, copies(step))):
            copy.wait()
            term = jnp.dot(
                rot[...],
                buf[step % slots, pl.ds(n * step_depth, step_depth), :],
                preferred_element_type=jnp.float32,
            )
            acc = term if acc is None else acc + term
        if step + slots < len(plan):
            for copy in copies(step + slots):
                copy.start()
        if add is not None:
            acc = acc + adds[add][add_lead].astype(jnp.float32)
        outs[out][lead] = acc.astype(outs[out].dtype)


def project(rots, parts, w_out, tbl, spans, shift, width, dtypes, adds=(), leads=None):
    rows, depth = rots[0].shape
    plan = [(k, n) for k, (_, count) in enumerate(spans) for n in range(count)]
    if leads is None:
        leads = plan if adds else [(None, None)] * len(plan)
    plan = [(*to, *add) for to, add in zip(plan, leads)]
    slots = min(len(plan), AHEAD)
    return call(
        functools.partial(project_kernel, plan, parts, len(adds), shift),
        1,
        [tbl],
        [pl.BlockSpec(memory_space=pl.ANY)]
        + [whole((rows, depth)) for _ in parts]
        + [whole(add.shape) for add in adds],
        [w_out, *[rots[k] for k in parts], *adds],
        [
            ((n, rows, width), dtype, whole((n, rows, width)))
            for (_, n), dtype in zip(spans, dtypes)
        ],
        cost(PROJECT_FLOPS, 0),
        [
            pltpu.VMEM((slots, depth * len(parts), width), jnp.bfloat16),
            pltpu.SemaphoreType.DMA((slots, len(parts))),
        ],
    )


def close_kernel(colors, residual, exps, *refs):
    terms, out = refs[:-1], refs[-1]
    per = len(terms) // colors
    width = residual.shape[1] // colors
    for c in range(colors):
        cols = pl.ds(c * width, width)
        own, *recvs = terms[c * per : (c + 1) * per]
        acc = own[0].astype(jnp.float32)
        for recv in recvs:
            acc = acc + recv[0].astype(jnp.float32)
        acc = acc * jnp.exp2(exps[:, cols].astype(jnp.float32))
        out[c] = (residual[:, cols].astype(jnp.float32) + acc).astype(jnp.bfloat16)


def close(residual, exps, terms, at):
    colors = len(terms)
    _, rows, width = terms[0][0].shape
    span = width * colors
    flat = [t for color in terms for t in color]
    shape = (colors, rows, width)
    return call(
        functools.partial(close_kernel, colors),
        1,
        [],
        [
            pl.BlockSpec((rows, span), lambda i: (0, at)),
            pl.BlockSpec((1, span), lambda i: (0, at)),
        ]
        + [whole((1, rows, width))] * len(flat),
        [residual, exps, *flat],
        [(shape, jnp.bfloat16, whole(shape))],
        cost(10 * rows * span, 2 * rows * width * (len(flat) + 2 * colors)),
    )[0]


def kv_kernel(plan, count, has_prev, channels, tbl_ref, w, *refs):
    xs, gains, rest = refs[:count], refs[count : count + len(plan)], refs[count + len(plan) :]
    prev, rest = (rest[:2], rest[2:]) if has_prev else (None, rest)
    acc, total = rest[-2:]
    i = pl.program_id(0)

    @pl.when(i == 0)
    def _():
        acc[...] = prev[0][...] if has_prev else jnp.zeros_like(acc)
        total[...] = prev[1][...] if has_prev else jnp.zeros_like(total)

    for step, blocks in enumerate(plan):

        @pl.when(i == step)
        def _():
            product, square = acc[...], total[...]
            for k, at, c in blocks:
                hidden = xs[k][at].astype(jnp.float32)
                depth = hidden.shape[1]
                cols = pl.ds(c * depth, depth)
                scaled = (hidden * gains[step][:, cols].astype(jnp.float32)).astype(jnp.bfloat16)
                product = product + jnp.dot(
                    scaled, w[cols, :], preferred_element_type=jnp.float32
                )
                hidden = hidden * hidden
                for b in range(depth // HD):
                    square = square + hidden[:, b * HD : (b + 1) * HD]
            acc[...], total[...] = product, square

    if channels:
        exps, out = rest[0], rest[1]

        @pl.when(i == len(plan) - 1)
        def _():
            mean = jnp.sum(total[...], axis=1, keepdims=True) / channels
            scale = jnp.exp2(exps[...].astype(jnp.float32))
            out[...] = (acc[...] * lax.rsqrt(mean + EPS) * scale).astype(out.dtype)


def kv_step(plan, arrays, gains, w_kv, tbl, at, span, prev, exps, channels):
    used = sorted({k for blocks in plan for k, _, _ in blocks})
    xs = [arrays[k] for k in used]
    plan = [[(used.index(k), lead, c) for k, lead, c in blocks] for blocks in plan]
    rows = xs[0].shape[1]
    cols = w_kv.shape[1]
    extra = list(prev or ())
    running = [((rows, cols), jnp.float32), ((rows, HD), jnp.float32)]
    if channels:
        extra.append(exps)
        outs, scratch = [((rows, cols), jnp.bfloat16)], [pltpu.VMEM(*r) for r in running]
    else:
        outs, scratch = running, []
    return call(
        functools.partial(kv_kernel, plan, len(xs), prev is not None, channels),
        len(plan),
        [tbl],
        [pl.BlockSpec((span, cols), lambda i, t: (t[i] + at, 0))]
        + [whole(x.shape) for x in xs]
        + [pl.BlockSpec((1, span), lambda i, t: (0, at))] * len(gains)
        + [whole(e.shape) for e in extra],
        [w_kv, *xs, *gains, *extra],
        [(shape, dtype, whole(shape)) for shape, dtype in outs],
        cost(
            2 * rows * span * cols * len(plan), 2 * span * (rows + cols) * len(plan) + 4 * rows * cols
        ),
        scratch,
    )


def gather(x, orders, count):
    colors = x.shape[0]
    arrays, where = [x], {0: [(0, c) for c in range(colors)]}
    levels = len(orders[0])
    for bit in range(levels):
        arrays.append(swap(x, bit, count))
        where[1 << bit] = [(len(arrays) - 1, c) for c in range(colors)]
    for size in range(2, levels + 1):
        for r in range(count):
            if r.bit_count() == size:
                where[r] = []
                for c, order in enumerate(orders):
                    hop = max((b for b in range(levels) if r >> b & 1), key=order.index)
                    k, at = where[r ^ 1 << hop][c]
                    arrays.append(swap(arrays[k][at : at + 1], hop, count))
                    where[r].append((len(arrays) - 1, 0))
    plan = [[(k, at, c) for c, (k, at) in enumerate(blocks)] for blocks in where.values()]
    return arrays, list(zip(where, plan))


def body(attn_out, head_signs, w_out, out_exp, residual, norm_gain, w_kv, kv_exp):
    count = lax.axis_size("tensor")
    levels = count.bit_length() - 1
    me = lax.axis_index("tensor").astype(jnp.int32)
    me_arr = me.reshape(1)
    local = residual.shape[1]
    channels = local * count
    orders = [list(range(levels))]
    orders.append(orders[0][levels // 2 :] + orders[0][: levels // 2])
    colors = len(orders)

    cuts = (8, 8, 4) if local >= 8 * HD else (4, 4) if local >= 4 * HD else (2,)
    units, first = [], 0
    for cut in cuts:
        units.append((first, local // cut))
        first += colors * local // cut

    lists = [send_lists(order) for order in orders]

    def blocks_of(stages, width):
        spans, rel, color = [], [], []
        for s in stages:
            for c in range(colors):
                spans.append((len(rel), len(lists[c][s])))
                rel += lists[c][s]
                color += [c] * len(lists[c][s])
        tbl = (me ^ jnp.array(rel, jnp.int32)) * (local // width) + jnp.array(color, jnp.int32)
        return tbl, spans

    exps = out_exp.reshape(1, -1)
    kv_exps = kv_exp.reshape(1, -1)
    gains = [norm_gain.reshape(1, -1)]
    for r in range(1, count):
        gains.append(lax.ppermute(gains[0], "tensor", [(i, i ^ r) for i in range(count)]))

    rots, blocks = [], []
    for p in range(PARTS):
        mixed = mix(attn_out, me_arr, head_signs, p, colors)
        blocks.append([])
        for c, order in enumerate(orders):
            own, sent = mixed[2 * c : 2 * c + 2]
            blocks[p].append([own, swap(sent, order[0], count)])
    for s in range(1, levels):
        for p in range(PARTS):
            for c, order in enumerate(orders):
                send = stage([blocks[p][c]], [order], me_arr, 1.0)
                blocks[p][c].append(swap(send, order[s], count))
    for p in range(PARTS):
        rots.append(stage(blocks[p], orders, me_arr, head_signs.shape[0] ** -0.5))

    ahead = 2 if len(units) > 2 else 1
    bf16, f32 = jnp.bfloat16, jnp.float32
    received = []
    for u, (first, width) in enumerate(units):
        tbl, spans = blocks_of([0], width)
        prevs, todo, at = (), list(range(PARTS)), first // width
        if u < ahead:
            prevs = project(rots, todo[:-1], w_out, tbl, spans, at, width, [f32] * colors)
            todo = todo[-1:]
        sends = project(rots, todo, w_out, tbl, spans, at, width, [bf16] * colors, prevs)
        received.append([swap(send, order[0], count) for send, order in zip(sends, orders)])

    later = range(1, levels + 1)
    leads = []
    for s in later:
        for c in range(colors):
            n = len(lists[c][s])
            leads += [(c, k + n * (s < levels)) for k in range(n)]
    dtypes = [bf16 if s == 1 and levels > 1 else f32 for s in later for _ in range(colors)]

    resids, running = [], None
    for u, (first, width) in enumerate(units):
        tbl, spans = blocks_of(later, width)
        parts = project(
            rots, list(range(PARTS)), w_out, tbl, spans, first // width, width, dtypes,
            received[u], leads,
        )
        terms = []
        for c, order in enumerate(orders):
            recvs = []
            for s in range(1, levels):
                send = parts[(s - 1) * colors + c]
                if recvs:
                    size = send.shape[0]
                    for recv in recvs:
                        send = send + recv[size : 2 * size].astype(f32)
                    send = send.astype(bf16)
                recvs.append(swap(send, order[s], count))
            terms.append([parts[(levels - 1) * colors + c], *recvs])
        span = width * colors
        out = close(residual, exps, terms, first // span)
        resids += list(out)
        arrays, found = gather(out, orders, count)
        last = u == len(units) - 1
        near = [b for b in found if b[0].bit_count() < 2]
        far = [b for b in found if b[0].bit_count() >= 2]
        runs = [near, far] if last and far else [found]
        for k, run in enumerate(runs):
            tbl = (me ^ jnp.array([r for r, _ in run], jnp.int32)) * (local // span)
            running = kv_step(
                [plan for _, plan in run],
                arrays,
                [gains[r] for r, _ in run],
                w_kv,
                tbl,
                first // span,
                span,
                running,
                kv_exps,
                channels * (last and k == len(runs) - 1),
            )
    return jnp.concatenate(resids, axis=1), running[0]


def solution(mesh):
    placed = (
        P("dp", "tensor"),
        P(),
        P("tensor", None),
        P("tensor"),
        P("dp", "tensor"),
        P("tensor"),
        P(None, "tensor"),
        P("tensor"),
    )
    return jax.shard_map(
        body,
        mesh=mesh,
        in_specs=placed,
        out_specs=(P("dp", "tensor"), P("dp", "tensor")),
        check_vma=False,
    )
```

```python
import functools

import jax
import jax.numpy as jnp
from jax import lax
from jax.experimental import pallas as pl
from jax.experimental.pallas import tpu as pltpu
from jax.sharding import PartitionSpec as P

HD = 128
EPS = 1e-05
PARTS = 2
SLABS = 4
PIECES = 4
ROWS = 16
VMEM = 4 * 1024 * 1024
PROJECT_FLOPS = 1e6
AHEAD = 1


def cost(flops, nbytes):
    return pl.CostEstimate(flops=int(flops), bytes_accessed=int(nbytes), transcendentals=0)


def call(kernel, grid, scalars, in_specs, args, outs, estimate, scratch=(), kinds=None):
    kinds = kinds or [jax.ShapeDtypeStruct] * len(outs)
    return pl.pallas_call(
        kernel,
        grid_spec=pltpu.PrefetchScalarGridSpec(
            num_scalar_prefetch=len(scalars),
            grid=(grid,),
            in_specs=in_specs,
            out_specs=[spec for _, _, spec in outs],
            scratch_shapes=list(scratch),
        ),
        out_shape=[kind(shape, dtype) for (shape, dtype, _), kind in zip(outs, kinds)],
        compiler_params=pltpu.CompilerParams(vmem_limit_bytes=VMEM),
        cost_estimate=estimate,
    )(*scalars, *args)


def whole(shape):
    return pl.BlockSpec(shape, lambda *_: (0,) * len(shape))


IN_PLACE = pl.BlockSpec(memory_space=pl.ANY)
IN_VMEM = pl.BlockSpec(memory_space=pltpu.VMEM)


def in_hbm(array):
    return pltpu.with_memory_space_constraint(array, pltpu.HBM)


def after(value, *others):
    return lax.optimization_barrier((value, *others))[0]


def swap(block, bit, count):
    return lax.ppermute(block, "tensor", [(i, i ^ 1 << bit) for i in range(count)])


def mix_rows(part, heads, c, i, me, signs, attn, full, sent):
    half = heads // PARTS
    at = pl.ds(pl.multiple_of(c * full.shape[0] + i * ROWS, ROWS), ROWS)
    rows = pl.ds(pl.multiple_of(i * ROWS, ROWS), ROWS)

    def head(h):
        sign = (2 * signs[me * heads + h] - 1).astype(jnp.float32)
        return attn[at, pl.ds(h * HD, HD)].astype(jnp.float32) * sign

    v = []
    for h in range(half):
        a, b = head(h), head(h + half)
        v.append(a - b if part else a + b)
    step = 1
    while step < half:
        for lo in range(half):
            if not lo & step:
                a, b = v[lo], v[lo | step]
                v[lo], v[lo | step] = a + b, a - b
        step *= 2
    for h in range(half):
        cols = pl.ds(h * HD, HD)
        full[rows, cols] = v[h]
        sent[rows, cols] = v[h].astype(sent.dtype)


def mix_kernel(part, heads, me_ref, *refs):
    if part == 0:
        attn_hbm, signs_hbm, *outs, attn, signs, sem, signs_sem = refs
    else:
        attn, signs_hbm, *outs, signs, signs_sem = refs
    me = me_ref[0]
    get_signs = pltpu.make_async_copy(signs_hbm, signs, signs_sem)
    get_signs.start()
    size = outs[0].shape[0]
    colors = len(outs) // 2
    step = attn.shape[0] // PIECES
    pieces = []
    if part == 0:
        for k in range(PIECES):
            rows = pl.ds(k * step, step)
            pieces.append(
                pltpu.make_async_copy(attn_hbm.at[rows, :], attn.at[rows, :], sem.at[k])
            )
            pieces[k].start()
    get_signs.wait()
    for k in range(PIECES):
        if pieces:
            pieces[k].wait()
        c, first = k * step // size, k * step % size // ROWS
        full, sent = outs[2 * c : 2 * c + 2]

        @pl.loop(first, first + step // ROWS)
        def _(i):
            mix_rows(part, heads, c, i, me, signs, attn, full, sent)


def mix(attn, me, signs, part, colors):
    rows, cols = attn.shape
    shape = (rows // colors, cols // PARTS)
    outs = [(shape, d, whole(shape)) for _ in range(colors) for d in (jnp.float32, jnp.bfloat16)]
    kinds = [jax.ShapeDtypeStruct] * len(outs)
    scratch = [pltpu.SMEM(signs.shape, signs.dtype), pltpu.SemaphoreType.DMA]
    if part == 0:
        outs.append((attn.shape, attn.dtype, IN_VMEM))
        kinds.append(pltpu.VMEM)
        scratch.insert(1, pltpu.SemaphoreType.DMA((PIECES,)))
    return call(
        functools.partial(mix_kernel, part, cols // HD),
        1,
        [me],
        [IN_VMEM if part else IN_PLACE, IN_PLACE],
        [attn if part else in_hbm(attn), in_hbm(signs)],
        outs,
        cost(6 * attn.size, 5 * attn.size),
        scratch,
        kinds,
    )


def load_kernel(first, gate_ref, w_hbm, out, sem):
    del gate_ref
    step = out.shape[0] // PIECES
    copies = [
        pltpu.make_async_copy(
            w_hbm.at[pl.ds(first + k * step, step), :], out.at[pl.ds(k * step, step), :], sem.at[k]
        )
        for k in range(PIECES)
    ]
    for copy in copies:
        copy.start()
    for copy in copies:
        copy.wait()


def load(w, gate, slab):
    rows = w.shape[0] // SLABS
    shape = (rows, w.shape[1])
    return call(
        functools.partial(load_kernel, slab * rows),
        1,
        [gate],
        [IN_PLACE],
        [in_hbm(w)],
        [(shape, w.dtype, IN_VMEM)],
        cost(0, 4 * rows * w.shape[1]),
        [pltpu.SemaphoreType.DMA((PIECES,))],
        [pltpu.VMEM],
    )[0]


def combine(order, me, own, recvs, rows):
    v = own[rows, :]
    for bit, recv in zip(order, recvs):
        flip = (1 - 2 * (me >> bit & 1)).astype(jnp.float32)
        v = recv[rows, :].astype(jnp.float32) + flip * v
    return v


def stage_kernel(orders, scale, me_ref, *refs):
    ins, out = refs[:-1], refs[-1]
    me = me_ref[0]
    per = len(ins) // len(orders)
    for c, order in enumerate(orders):
        own, *recvs = ins[c * per : (c + 1) * per]
        size = own.shape[0]

        @pl.loop(0, size // ROWS)
        def _(i):
            rows = pl.ds(pl.multiple_of(i * ROWS, ROWS), ROWS)
            to = pl.ds(pl.multiple_of(c * size + i * ROWS, ROWS), ROWS)
            out[to, :] = (combine(order, me, own, recvs, rows) * scale).astype(out.dtype)


def stage(blocks, orders, me, scale):
    flat = [b for block in blocks for b in block]
    rows, cols = flat[0].shape
    shape = (rows * len(blocks), cols)
    return call(
        functools.partial(stage_kernel, orders, scale),
        1,
        [me],
        [whole(f.shape) for f in flat],
        flat,
        [(shape, jnp.bfloat16, whole(shape))],
        cost(4 * rows * cols * len(flat), 2 * rows * cols * (len(flat) + 2)),
    )[0]


def send_lists(order):
    lists = []
    for s, bit in enumerate(order):
        members = [1 << bit]
        for later in reversed(order[s + 1 :]):
            members = members + [m | 1 << later for m in members]
        lists.append(members)
    return lists + [[0]]


def project_kernel(plan, parts, extras, shift, width, tbl_ref, *refs):
    rots, refs = refs[:parts], refs[parts:]
    per = SLABS // PARTS
    slabs, refs = refs[: per * parts], refs[per * parts :]
    adds, outs = refs[:extras], refs[extras:]
    for step, (out, lead, add, add_lead) in enumerate(plan):
        cols = pl.ds(pl.multiple_of((tbl_ref[step] + shift) * width, width), width)
        acc = None
        for k, slab in enumerate(slabs):
            depth = slab.shape[0]
            term = jnp.dot(
                rots[k // per][:, k % per * depth : (k % per + 1) * depth],
                slab[:, cols],
                preferred_element_type=jnp.float32,
            )
            acc = term if acc is None else acc + term
        if add is not None:
            acc = acc + adds[add][add_lead].astype(jnp.float32)
        outs[out][lead] = acc.astype(outs[out].dtype)


def project(rots, slabs, tbl, spans, shift, width, dtypes, adds=(), leads=None):
    rows = rots[0].shape[0]
    plan = [(k, n) for k, (_, count) in enumerate(spans) for n in range(count)]
    if leads is None:
        leads = plan if adds else [(None, None)] * len(plan)
    plan = [(*to, *add) for to, add in zip(plan, leads)]
    return call(
        functools.partial(project_kernel, plan, len(rots), len(adds), shift, width),
        1,
        [tbl],
        [IN_VMEM] * (len(rots) + len(slabs) + len(adds)),
        [*rots, *slabs, *adds],
        [
            ((n, rows, width), dtype, whole((n, rows, width)))
            for (_, n), dtype in zip(spans, dtypes)
        ],
        cost(PROJECT_FLOPS, 0),
    )


def close_kernel(colors, residual, exps, *refs):
    terms, out = refs[:-1], refs[-1]
    per = len(terms) // colors
    width = residual.shape[1] // colors
    for c in range(colors):
        cols = pl.ds(c * width, width)
        own, *recvs = terms[c * per : (c + 1) * per]
        acc = own[0].astype(jnp.float32)
        for recv in recvs:
            acc = acc + recv[0].astype(jnp.float32)
        acc = acc * jnp.exp2(exps[:, cols].astype(jnp.float32))
        out[c] = (residual[:, cols].astype(jnp.float32) + acc).astype(jnp.bfloat16)


def close(residual, exps, terms, at):
    colors = len(terms)
    _, rows, width = terms[0][0].shape
    span = width * colors
    flat = [t for color in terms for t in color]
    shape = (colors, rows, width)
    return call(
        functools.partial(close_kernel, colors),
        1,
        [],
        [
            pl.BlockSpec((rows, span), lambda i: (0, at)),
            pl.BlockSpec((1, span), lambda i: (0, at)),
        ]
        + [whole((1, rows, width))] * len(flat),
        [residual, exps, *flat],
        [(shape, jnp.bfloat16, whole(shape))],
        cost(10 * rows * span, 2 * rows * width * (len(flat) + 2 * colors)),
    )[0]


def kv_kernel(plan, count, has_prev, channels, at, span, tbl_ref, w, *refs):
    xs, gains, rest = refs[:count], refs[count : count + len(plan)], refs[count + len(plan) :]
    rows, cols = xs[0].shape[-2], w.shape[1]
    product = rest[0][...] if has_prev else jnp.zeros((rows, cols), jnp.float32)
    square = rest[1][...] if has_prev else jnp.zeros((rows, HD), jnp.float32)
    rest = rest[2 * has_prev :]
    for step, blocks in enumerate(plan):
        for k, lead, c in blocks:
            hidden = xs[k][lead].astype(jnp.float32)
            depth = hidden.shape[1]
            gain = gains[step][:, at * span + c * depth : at * span + (c + 1) * depth]
            scaled = (hidden * gain.astype(jnp.float32)).astype(jnp.bfloat16)
            first = pl.multiple_of((tbl_ref[step] + at) * span + c * depth, depth)
            product = product + jnp.dot(
                scaled, w[pl.ds(first, depth), :], preferred_element_type=jnp.float32
            )
            hidden = hidden * hidden
            for b in range(depth // HD):
                square = square + hidden[:, b * HD : (b + 1) * HD]
    if channels:
        exps, out = rest
        mean = jnp.sum(square, axis=1, keepdims=True) / channels
        scale = jnp.exp2(exps[...].astype(jnp.float32))
        out[...] = (product * lax.rsqrt(mean + EPS) * scale).astype(out.dtype)
    else:
        rest[0][...], rest[1][...] = product, square


def kv_step(plan, arrays, gains, w_kv, tbl, at, span, prev, exps, channels):
    used = sorted({k for blocks in plan for k, _, _ in blocks})
    xs = [arrays[k] for k in used]
    plan = [[(used.index(k), lead, c) for k, lead, c in blocks] for blocks in plan]
    rows = xs[0].shape[1]
    cols = w_kv.shape[1]
    extra = list(prev or ())
    if channels:
        extra.append(exps)
        outs = [((rows, cols), jnp.bfloat16)]
    else:
        outs = [((rows, cols), jnp.float32), ((rows, HD), jnp.float32)]
    args = [w_kv, *xs, *gains, *extra]
    return call(
        functools.partial(kv_kernel, plan, len(xs), prev is not None, channels, at, span),
        1,
        [tbl],
        [IN_VMEM] * len(args),
        args,
        [(shape, dtype, whole(shape)) for shape, dtype in outs],
        cost(
            2 * rows * span * cols * len(plan), 2 * span * (rows + cols) * len(plan) + 4 * rows * cols
        ),
    )


def gather(x, orders, count):
    colors = x.shape[0]
    arrays, where = [x], {0: [(0, c) for c in range(colors)]}
    levels = len(orders[0])
    for bit in range(levels):
        arrays.append(swap(x, bit, count))
        where[1 << bit] = [(len(arrays) - 1, c) for c in range(colors)]
    for size in range(2, levels + 1):
        for r in range(count):
            if r.bit_count() == size:
                where[r] = []
                for c, order in enumerate(orders):
                    hop = max((b for b in range(levels) if r >> b & 1), key=order.index)
                    k, at = where[r ^ 1 << hop][c]
                    arrays.append(swap(arrays[k][at : at + 1], hop, count))
                    where[r].append((len(arrays) - 1, 0))
    plan = [[(k, at, c) for c, (k, at) in enumerate(blocks)] for blocks in where.values()]
    return arrays, list(zip(where, plan))


def body(attn_out, head_signs, w_out, out_exp, residual, norm_gain, w_kv, kv_exp):
    count = lax.axis_size("tensor")
    levels = count.bit_length() - 1
    me = lax.axis_index("tensor").astype(jnp.int32)
    me_arr = me.reshape(1)
    local = residual.shape[1]
    channels = local * count
    orders = [list(range(levels))]
    orders.append(orders[0][levels // 2 :] + orders[0][: levels // 2])
    colors = len(orders)

    cuts = (8, 8, 4) if local >= 8 * HD else (4, 4) if local >= 4 * HD else (2,)
    units, first = [], 0
    for cut in cuts:
        units.append((first, local // cut))
        first += colors * local // cut

    lists = [send_lists(order) for order in orders]

    def blocks_of(stages, width):
        spans, rel, color = [], [], []
        for s in stages:
            for c in range(colors):
                spans.append((len(rel), len(lists[c][s])))
                rel += lists[c][s]
                color += [c] * len(lists[c][s])
        tbl = (me ^ jnp.array(rel, jnp.int32)) * (local // width) + jnp.array(color, jnp.int32)
        return tbl, spans

    exps = out_exp.reshape(1, -1)
    kv_exps = kv_exp.reshape(1, -1)
    gains = [norm_gain.reshape(1, -1)]
    for r in range(1, count):
        gains.append(lax.ppermute(gains[0], "tensor", [(i, i ^ r) for i in range(count)]))

    rots, blocks, slabs = [], [], []
    attn = attn_out
    for p in range(PARTS):
        mixed = mix(attn, me_arr, head_signs, p, colors)
        if p == 0:
            attn = mixed[-1]
        blocks.append([])
        for c, order in enumerate(orders):
            own, sent = mixed[2 * c : 2 * c + 2]
            blocks[p].append([own, swap(sent, order[0], count)])
    gate = after(me_arr, sent)
    for s in range(1, levels):
        for p in range(PARTS):
            if len(slabs) < SLABS - 2:
                slabs.append(load(w_out, gate, len(slabs)))
            here = after(me_arr, *slabs[-1:])
            for c, order in enumerate(orders):
                send = stage([blocks[p][c]], [order], here, 1.0)
                blocks[p][c].append(swap(send, order[s], count))
            gate = after(me_arr, send)
    for p in range(PARTS):
        while len(slabs) < SLABS - PARTS + 1 + p:
            slabs.append(load(w_out, gate, len(slabs)))
        here = after(me_arr, *slabs[-1:])
        rots.append(stage(blocks[p], orders, here, head_signs.shape[0] ** -0.5))
        gate = after(me_arr, rots[p])

    bf16, f32 = jnp.bfloat16, jnp.float32
    received = []
    for u, (first, width) in enumerate(units):
        tbl, spans = blocks_of([0], width)
        prevs, cut, at = (), 0, first // width
        if u < AHEAD:
            cut = PARTS - 1
            prevs = project(
                rots[:cut], slabs[: cut * SLABS // PARTS], tbl, spans, at, width, [f32] * colors
            )
        sends = project(
            rots[cut:], slabs[cut * SLABS // PARTS :], tbl, spans, at, width, [bf16] * colors, prevs
        )
        received.append([swap(send, order[0], count) for send, order in zip(sends, orders)])

    later = range(1, levels + 1)
    leads = []
    for s in later:
        for c in range(colors):
            n = len(lists[c][s])
            leads += [(c, k + n * (s < levels)) for k in range(n)]
    dtypes = [bf16 if s == 1 and levels > 1 else f32 for s in later for _ in range(colors)]

    resids, running = [], None
    for u, (first, width) in enumerate(units):
        tbl, spans = blocks_of(later, width)
        parts = project(
            rots, slabs, tbl, spans, first // width, width, dtypes, received[u], leads
        )
        terms = []
        for c, order in enumerate(orders):
            recvs = []
            for s in range(1, levels):
                send = parts[(s - 1) * colors + c]
                if recvs:
                    size = send.shape[0]
                    for recv in recvs:
                        send = send + recv[size : 2 * size].astype(f32)
                    send = send.astype(bf16)
                recvs.append(swap(send, order[s], count))
            terms.append([parts[(levels - 1) * colors + c], *recvs])
        span = width * colors
        out = close(residual, exps, terms, first // span)
        resids += list(out)
        arrays, found = gather(out, orders, count)
        last = u == len(units) - 1
        near = [b for b in found if b[0].bit_count() < 2]
        far = [b for b in found if b[0].bit_count() >= 2]
        runs = [near, far] if last and far else [found]
        for k, run in enumerate(runs):
            tbl = (me ^ jnp.array([r for r, _ in run], jnp.int32)) * (local // span)
            running = kv_step(
                [plan for _, plan in run],
                arrays,
                [gains[r] for r, _ in run],
                w_kv,
                tbl,
                first // span,
                span,
                running,
                kv_exps,
                channels * (last and k == len(runs) - 1),
            )
    return jnp.concatenate(resids, axis=1), running[0]


def solution(mesh):
    placed = (
        P("dp", "tensor"),
        P(),
        P("tensor", None),
        P("tensor"),
        P("dp", "tensor"),
        P("tensor"),
        P(None, "tensor"),
        P("tensor"),
    )
    return jax.shard_map(
        body,
        mesh=mesh,
        in_specs=placed,
        out_specs=(P("dp", "tensor"), P("dp", "tensor")),
        check_vma=False,
    )
```

```python
import functools

import jax
import jax.numpy as jnp
from jax import lax
from jax.experimental import pallas as pl
from jax.experimental.pallas import tpu as pltpu
from jax.sharding import PartitionSpec as P

HD = 128
EPS = 1e-05
PARTS = 2
HALVES = 2
PIECES = 4
ROWS = 16
VMEM = 4 * 1024 * 1024
PROJECT_FLOPS = 1e6


def cost(flops, nbytes):
    return pl.CostEstimate(flops=int(flops), bytes_accessed=int(nbytes), transcendentals=0)


def call(kernel, grid, scalars, in_specs, args, outs, estimate, scratch=(), kinds=None):
    kinds = kinds or [jax.ShapeDtypeStruct] * len(outs)
    return pl.pallas_call(
        kernel,
        grid_spec=pltpu.PrefetchScalarGridSpec(
            num_scalar_prefetch=len(scalars),
            grid=(grid,),
            in_specs=in_specs,
            out_specs=[spec for _, _, spec in outs],
            scratch_shapes=list(scratch),
        ),
        out_shape=[kind(shape, dtype) for (shape, dtype, _), kind in zip(outs, kinds)],
        compiler_params=pltpu.CompilerParams(vmem_limit_bytes=VMEM),
        cost_estimate=estimate,
    )(*scalars, *args)


def whole(shape):
    return pl.BlockSpec(shape, lambda *_: (0,) * len(shape))


IN_PLACE = pl.BlockSpec(memory_space=pl.ANY)
IN_VMEM = pl.BlockSpec(memory_space=pltpu.VMEM)


def in_hbm(array):
    return pltpu.with_memory_space_constraint(array, pltpu.HBM)


def after(value, *others):
    return lax.optimization_barrier((value, *others))[0]


def swap(block, bit, count):
    return lax.ppermute(block, "tensor", [(i, i ^ 1 << bit) for i in range(count)])


def mix_rows(part, heads, c, i, me, signs, attn, full, sent):
    half = heads // PARTS
    at = pl.ds(pl.multiple_of(c * full.shape[0] + i * ROWS, ROWS), ROWS)
    rows = pl.ds(pl.multiple_of(i * ROWS, ROWS), ROWS)

    def head(h):
        sign = (2 * signs[me * heads + h] - 1).astype(jnp.float32)
        return attn[at, pl.ds(h * HD, HD)].astype(jnp.float32) * sign

    v = []
    for h in range(half):
        a, b = head(h), head(h + half)
        v.append(a - b if part else a + b)
    step = 1
    while step < half:
        for lo in range(half):
            if not lo & step:
                a, b = v[lo], v[lo | step]
                v[lo], v[lo | step] = a + b, a - b
        step *= 2
    for h in range(half):
        cols = pl.ds(h * HD, HD)
        full[rows, cols] = v[h]
        sent[rows, cols] = v[h].astype(sent.dtype)


def mix_kernel(part, heads, me_ref, *refs):
    if part == 0:
        attn_hbm, signs_hbm, gain_hbm, *outs, attn, signs, gain, sem = refs
    else:
        attn, signs_hbm, *outs, signs, sem = refs
    me = me_ref[0]
    get_signs = pltpu.make_async_copy(signs_hbm, signs, sem.at[0])
    get_signs.start()
    size = outs[0].shape[0]
    step = attn.shape[0] // PIECES
    pieces = []
    if part == 0:
        for k in range(PIECES):
            rows = pl.ds(k * step, step)
            pieces.append(
                pltpu.make_async_copy(attn_hbm.at[rows, :], attn.at[rows, :], sem.at[2 + k])
            )
            pieces[k].start()
        get_gain = pltpu.make_async_copy(gain_hbm, gain, sem.at[1])
        get_gain.start()
        get_gain.wait()
        sent = outs[1]
        width = sent.shape[1]
        row = lax.broadcasted_iota(jnp.int32, (ROWS, width), 0)
        block = jnp.zeros((ROWS, width), jnp.float32)
        for k in range(PARTS):
            piece = gain[pl.ds(k * width, width)].astype(jnp.float32)
            block = jnp.where(row == k, jnp.broadcast_to(piece[None, :], block.shape), block)
        sent[size:, :] = block.astype(sent.dtype)
    get_signs.wait()
    for k in range(PIECES):
        if pieces:
            pieces[k].wait()
        c, first = k * step // size, k * step % size // ROWS
        full, sent = outs[2 * c : 2 * c + 2]

        @pl.loop(first, first + step // ROWS)
        def _(i):
            mix_rows(part, heads, c, i, me, signs, attn, full, sent)


def mix(attn, me, signs, gain, part, colors):
    rows, cols = attn.shape
    shape = (rows // colors, cols // PARTS)
    outs = []
    for c in range(colors):
        sent = (shape[0] + ROWS * (part == 0 and c == 0), shape[1])
        outs += [(shape, jnp.float32, whole(shape)), (sent, jnp.bfloat16, whole(sent))]
    kinds = [jax.ShapeDtypeStruct] * len(outs)
    scratch = [pltpu.SMEM(signs.shape, signs.dtype)]
    if part == 0:
        outs.append((attn.shape, attn.dtype, IN_VMEM))
        kinds.append(pltpu.VMEM)
        scratch.append(pltpu.VMEM(gain.shape, gain.dtype))
    scratch.append(pltpu.SemaphoreType.DMA((2 + PIECES,)))
    return call(
        functools.partial(mix_kernel, part, cols // HD),
        1,
        [me],
        [IN_VMEM, IN_PLACE] if part else [IN_PLACE] * 3,
        [attn, in_hbm(signs)] if part else [in_hbm(attn), in_hbm(signs), in_hbm(gain)],
        outs,
        cost(6 * attn.size, 5 * attn.size),
        scratch,
        kinds,
    )


def load_kernel(part, half, gate_ref, w_hbm, out, sem):
    del gate_ref
    depth, width = out.shape
    count = sem.shape[0]
    step, span = depth // PIECES, width // count
    copies = []
    for d in range(count):
        for k in range(PIECES):
            rows = pl.ds(part * depth + k * step, step)
            cols = pl.ds((d * HALVES + half) * span, span)
            to = out.at[pl.ds(k * step, step), pl.ds(d * span, span)]
            copies.append(pltpu.make_async_copy(w_hbm.at[rows, cols], to, sem.at[d, k]))
    for copy in copies:
        copy.start()
    for copy in copies:
        copy.wait()


def load(w, gate, part, half, count):
    shape = (w.shape[0] // PARTS, w.shape[1] // HALVES)
    return call(
        functools.partial(load_kernel, part, half),
        1,
        [gate],
        [IN_PLACE],
        [in_hbm(w)],
        [(shape, w.dtype, IN_VMEM)],
        cost(0, 0),
        [pltpu.SemaphoreType.DMA((count, PIECES))],
        [pltpu.VMEM],
    )[0]


def combine(order, me, own, recvs, rows):
    v = own[rows, :]
    for bit, recv in zip(order, recvs):
        flip = (1 - 2 * (me >> bit & 1)).astype(jnp.float32)
        v = recv[rows, :].astype(jnp.float32) + flip * v
    return v


def stage_kernel(orders, scale, ride, me_ref, *refs):
    riders, ins, out = refs[:ride], refs[ride:-1], refs[-1]
    me = me_ref[0]
    per = len(ins) // len(orders)
    size = ins[0].shape[0]
    for c, order in enumerate(orders):
        own, *recvs = ins[c * per : (c + 1) * per]

        @pl.loop(0, size // ROWS)
        def _(i):
            rows = pl.ds(pl.multiple_of(i * ROWS, ROWS), ROWS)
            to = pl.ds(pl.multiple_of(c * size + i * ROWS, ROWS), ROWS)
            out[to, :] = (combine(order, me, own, recvs, rows) * scale).astype(out.dtype)

    if ride:
        row = lax.broadcasted_iota(jnp.int32, (ROWS, out.shape[1]), 0)
        known = PARTS
        block = riders[0][size:, :].astype(jnp.float32)
        for rider in riders[1:]:
            more = pltpu.roll(rider[size:, :].astype(jnp.float32), known, 0)
            block = jnp.where(row < known, block, more)
            known *= 2
        out[size:, :] = block.astype(out.dtype)


def stage(blocks, orders, me, scale, riders=()):
    flat = [*riders, *[b for block in blocks for b in block]]
    rows, cols = blocks[0][0].shape
    shape = (rows * len(blocks) + ROWS * bool(riders), cols)
    return call(
        functools.partial(stage_kernel, orders, scale, len(riders)),
        1,
        [me],
        [whole(f.shape) for f in flat],
        flat,
        [(shape, jnp.bfloat16, whole(shape))],
        cost(4 * rows * cols * len(flat), 2 * rows * cols * (len(flat) + 2)),
    )[0]


def send_lists(order):
    lists = []
    for s, bit in enumerate(order):
        members = [1 << bit]
        for later in reversed(order[s + 1 :]):
            members = members + [m | 1 << later for m in members]
        lists.append(members)
    return lists + [[0]]


def project_kernel(plan, parts, adds, width, tbl_ref, *refs):
    rots, slabs, refs = refs[:parts], refs[parts : 2 * parts], refs[2 * parts :]
    outs = refs[sum(adds) :]
    for step, (out, lead, add, add_lead) in enumerate(plan):
        cols = pl.ds(pl.multiple_of(tbl_ref[step] * width, width), width)
        acc = None
        for rot, slab in zip(rots, slabs):
            term = jnp.dot(rot[...], slab[:, cols], preferred_element_type=jnp.float32)
            acc = term if acc is None else acc + term
        if add is not None:
            first = sum(adds[:add])
            more = [a[add_lead].astype(jnp.float32) for a in refs[first : first + adds[add]]]
            acc = acc + (more[0] if len(more) == 1 else jnp.concatenate(more, axis=1))
        outs[out][lead] = acc.astype(outs[out].dtype)


def project(rots, slabs, tbl, spans, width, dtypes, adds=(), leads=None):
    rows = rots[0].shape[0]
    plan = [(k, n) for k, (_, count) in enumerate(spans) for n in range(count)]
    if leads is None:
        leads = plan if adds else [(None, None)] * len(plan)
    plan = [(*to, *add) for to, add in zip(plan, leads)]
    args = [*rots, *slabs, *[a for add in adds for a in add]]
    return call(
        functools.partial(project_kernel, plan, len(rots), [len(add) for add in adds], width),
        1,
        [tbl],
        [IN_VMEM] * len(args),
        args,
        [
            ((n, rows, width), dtype, whole((n, rows, width)))
            for (_, n), dtype in zip(spans, dtypes)
        ],
        cost(PROJECT_FLOPS, 0),
    )


def close_kernel(colors, residual, exps, *refs):
    terms, out = refs[:-1], refs[-1]
    per = len(terms) // colors
    width = residual.shape[1] // colors
    for c in range(colors):
        cols = pl.ds(c * width, width)
        own, *recvs = terms[c * per : (c + 1) * per]
        acc = own[0].astype(jnp.float32)
        for recv in recvs:
            acc = acc + recv[0].astype(jnp.float32)
        acc = acc * jnp.exp2(exps[:, cols].astype(jnp.float32))
        out[c] = (residual[:, cols].astype(jnp.float32) + acc).astype(jnp.bfloat16)


def close(residual, exps, terms, at):
    colors = len(terms)
    _, rows, width = terms[0][0].shape
    span = width * colors
    flat = [t for color in terms for t in color]
    shape = (colors, rows, width)
    return call(
        functools.partial(close_kernel, colors),
        1,
        [],
        [
            pl.BlockSpec((rows, span), lambda i: (0, at)),
            pl.BlockSpec((1, span), lambda i: (0, at)),
        ]
        + [whole((1, rows, width))] * len(flat),
        [residual, exps, *flat],
        [(shape, jnp.bfloat16, whole(shape))],
        cost(10 * rows * span, 2 * rows * width * (len(flat) + 2 * colors)),
    )[0]


def kv_kernel(plan, gain_at, counts, has_prev, channels, at, span, tbl_ref, w, *refs):
    xs, riders, rest = refs[: counts[0]], refs[counts[0] : sum(counts)], refs[sum(counts) :]
    rows, cols = xs[0].shape[-2], w.shape[1]
    product = rest[0][...] if has_prev else jnp.zeros((rows, cols), jnp.float32)
    square = rest[1][...] if has_prev else jnp.zeros((rows, HD), jnp.float32)
    rest = rest[2 * has_prev :]
    for step, blocks in enumerate(plan):
        rider, row = gain_at[step]
        rider = riders[rider]
        for k, lead, c in blocks:
            hidden = xs[k][lead].astype(jnp.float32)
            depth = hidden.shape[1]
            part, col = divmod(at * span + c * depth, rider.shape[1])
            gain = rider[rider.shape[0] - ROWS :, col : col + depth].astype(jnp.float32)
            gain = gain[row + part : row + part + 1]
            scaled = (hidden * gain).astype(jnp.bfloat16)
            first = pl.multiple_of((tbl_ref[step] + at) * span + c * depth, depth)
            product = product + jnp.dot(
                scaled, w[pl.ds(first, depth), :], preferred_element_type=jnp.float32
            )
            hidden = hidden * hidden
            for b in range(depth // HD):
                square = square + hidden[:, b * HD : (b + 1) * HD]
    if channels:
        exps, out = rest
        mean = jnp.sum(square, axis=1, keepdims=True) / channels
        scale = jnp.exp2(exps[...].astype(jnp.float32))
        out[...] = (product * lax.rsqrt(mean + EPS) * scale).astype(out.dtype)
    else:
        rest[0][...], rest[1][...] = product, square


def kv_step(plan, arrays, riders, gain_at, w_kv, tbl, at, span, prev, exps, channels):
    used = sorted({k for blocks in plan for k, _, _ in blocks})
    xs = [arrays[k] for k in used]
    plan = [[(used.index(k), lead, c) for k, lead, c in blocks] for blocks in plan]
    rows = xs[0].shape[1]
    cols = w_kv.shape[1]
    extra = list(prev or ())
    if channels:
        extra.append(exps)
        outs = [((rows, cols), jnp.bfloat16)]
    else:
        outs = [((rows, cols), jnp.float32), ((rows, HD), jnp.float32)]
    args = [w_kv, *xs, *riders, *extra]
    counts = [len(xs), len(riders)]
    return call(
        functools.partial(
            kv_kernel, plan, gain_at, counts, prev is not None, channels, at, span
        ),
        1,
        [tbl],
        [IN_VMEM] * len(args),
        args,
        [(shape, dtype, whole(shape)) for shape, dtype in outs],
        cost(
            2 * rows * span * cols * len(plan), 2 * span * (rows + cols) * len(plan) + 4 * rows * cols
        ),
    )


def gather(x, orders, count):
    colors = x.shape[0]
    arrays, where = [x], {0: [(0, c) for c in range(colors)]}
    levels = len(orders[0])
    for bit in range(levels):
        arrays.append(swap(x, bit, count))
        where[1 << bit] = [(len(arrays) - 1, c) for c in range(colors)]
    for size in range(2, levels + 1):
        for r in range(count):
            if r.bit_count() == size:
                where[r] = []
                for c, order in enumerate(orders):
                    hop = max((b for b in range(levels) if r >> b & 1), key=order.index)
                    k, at = where[r ^ 1 << hop][c]
                    arrays.append(swap(arrays[k][at : at + 1], hop, count))
                    where[r].append((len(arrays) - 1, 0))
    plan = [[(k, at, c) for c, (k, at) in enumerate(blocks)] for blocks in where.values()]
    return arrays, list(zip(where, plan))


def body(attn_out, head_signs, w_out, out_exp, residual, norm_gain, w_kv, kv_exp):
    count = lax.axis_size("tensor")
    levels = count.bit_length() - 1
    me = lax.axis_index("tensor").astype(jnp.int32)
    me_arr = me.reshape(1)
    local = residual.shape[1]
    channels = local * count
    orders = [list(range(levels))]
    orders.append(orders[0][levels // 2 :] + orders[0][: levels // 2])
    colors = len(orders)

    half = local // HALVES
    wide = half // colors
    subs = [1] * HALVES

    lists = [send_lists(order) for order in orders]

    def blocks_of(stages, width, sub):
        spans, rel, color = [], [], []
        for s in stages:
            for c in range(colors):
                spans.append((len(rel), len(lists[c][s])))
                rel += lists[c][s]
                color += [c * (wide // width) + sub] * len(lists[c][s])
        tbl = (me ^ jnp.array(rel, jnp.int32)) * (half // width) + jnp.array(color, jnp.int32)
        return tbl, spans

    exps = out_exp.reshape(1, -1)
    kv_exps = kv_exp.reshape(1, -1)

    rots, blocks, riders = [], [], []
    slabs = [[None] * HALVES for _ in range(PARTS)]
    attn = attn_out
    for p in range(PARTS):
        mixed = mix(attn, me_arr, head_signs, norm_gain, p, colors)
        if p == 0:
            attn = mixed[-1]
        blocks.append([])
        for c, order in enumerate(orders):
            own, sent = mixed[2 * c : 2 * c + 2]
            blocks[p].append([own, swap(sent, order[0], count)])
            if p == c == 0:
                riders += [sent, blocks[0][0][1]]
    gate = after(me_arr, sent)
    for s in range(1, levels):
        for p in range(PARTS):
            if s == 1:
                slabs[p][0] = load(w_out, gate, p, 0, count)
            here = after(me_arr, slabs[p][0])
            sends = []
            for c, order in enumerate(orders):
                ride = p == c == 0
                sends.append(stage([blocks[p][c]], [order], here, 1.0, riders if ride else ()))
                blocks[p][c].append(swap(sends[c], order[s], count))
                if ride:
                    riders.append(blocks[p][c][-1])
            gate = after(me_arr, *sends)
    slabs[0][1] = load(w_out, gate, 0, 1, count)
    here = after(me_arr, slabs[0][1])
    scale = head_signs.shape[0] ** -0.5
    for p in range(PARTS):
        rots.append(stage(blocks[p], orders, here, scale))
        here = after(me_arr, rots[p])

    gain_at, known = {0: (0, 0)}, [0]
    for t, bit in enumerate(orders[0]):
        gain_at.update({r ^ 1 << bit: (t + 1, PARTS * k) for k, r in enumerate(known)})
        known += [r ^ 1 << bit for r in known]

    bf16, f32 = jnp.bfloat16, jnp.float32
    received = []
    for v in range(HALVES):
        width = wide // subs[v]
        received.append([[] for _ in orders])
        if v == 1:
            slabs[1][1] = load(w_out, after(me_arr, sends[0]), 1, 1, count)
        for sub in range(subs[v]):
            tbl, spans = blocks_of([0], width, sub)
            weights = [slabs[p][v] for p in range(PARTS)]
            prevs, cut = (), 0
            if v == 0:
                cut = PARTS - 1
                prevs = project(rots[:cut], weights[:cut], tbl, spans, width, [f32] * colors)
            sends = project(
                rots[cut:], weights[cut:], tbl, spans, width, [bf16] * colors, [[p] for p in prevs]
            )
            for c, order in enumerate(orders):
                received[v][c].append(swap(sends[c], order[0], count))

    later = range(1, levels + 1)
    leads = []
    for s in later:
        for c in range(colors):
            n = len(lists[c][s])
            leads += [(c, k + n * (s < levels)) for k in range(n)]
    dtypes = [bf16 if s == 1 and levels > 1 else f32 for s in later for _ in range(colors)]

    resids, running = [], None
    for v in range(HALVES):
        tbl, spans = blocks_of(later, wide, 0)
        weights = [slabs[p][v] for p in range(PARTS)]
        parts = project(rots, weights, tbl, spans, wide, dtypes, received[v], leads)
        terms = []
        for c, order in enumerate(orders):
            recvs = []
            for s in range(1, levels):
                send = parts[(s - 1) * colors + c]
                if recvs:
                    size = send.shape[0]
                    for recv in recvs:
                        send = send + recv[size : 2 * size].astype(f32)
                    send = send.astype(bf16)
                recvs.append(swap(send, order[s], count))
            terms.append([parts[(levels - 1) * colors + c], *recvs])
        out = close(residual, exps, terms, v)
        resids += list(out)
        arrays, found = gather(out, orders, count)
        last = v == HALVES - 1
        near = [b for b in found if b[0].bit_count() < 2]
        far = [b for b in found if b[0].bit_count() >= 2]
        runs = [near, far] if last and far else [found]
        for k, run in enumerate(runs):
            tbl = (me ^ jnp.array([r for r, _ in run], jnp.int32)) * HALVES
            running = kv_step(
                [plan for _, plan in run],
                arrays,
                riders,
                [gain_at[r] for r, _ in run],
                w_kv,
                tbl,
                v,
                half,
                running,
                kv_exps,
                channels * (last and k == len(runs) - 1),
            )
    return jnp.concatenate(resids, axis=1), running[0]


def solution(mesh):
    placed = (
        P("dp", "tensor"),
        P(),
        P("tensor", None),
        P("tensor"),
        P("dp", "tensor"),
        P("tensor"),
        P(None, "tensor"),
        P("tensor"),
    )
    return jax.shard_map(
        body,
        mesh=mesh,
        in_specs=placed,
        out_specs=(P("dp", "tensor"), P("dp", "tensor")),
        check_vma=False,
    )
```

```python
import functools

import jax
import jax.numpy as jnp
from jax import lax
from jax.experimental import pallas as pl
from jax.experimental.pallas import tpu as pltpu
from jax.sharding import PartitionSpec as P

HD = 128
EPS = 1e-05
QUARTERS = ((0, 1, 2), (3,))
HALVES = 2
SLABS = 2
PIECES = 4
ROWS = 16
VMEM = 4 * 1024 * 1024
PROJECT_FLOPS = 1e6
BUSY = 4e9


def cost(flops, nbytes):
    return pl.CostEstimate(flops=int(flops), bytes_accessed=int(nbytes), transcendentals=0)


def call(kernel, grid, scalars, in_specs, args, outs, estimate, scratch=(), kinds=None):
    kinds = kinds or [jax.ShapeDtypeStruct] * len(outs)
    return pl.pallas_call(
        kernel,
        grid_spec=pltpu.PrefetchScalarGridSpec(
            num_scalar_prefetch=len(scalars),
            grid=(grid,),
            in_specs=in_specs,
            out_specs=[spec for _, _, spec in outs],
            scratch_shapes=list(scratch),
        ),
        out_shape=[kind(shape, dtype) for (shape, dtype, _), kind in zip(outs, kinds)],
        compiler_params=pltpu.CompilerParams(vmem_limit_bytes=VMEM),
        cost_estimate=estimate,
    )(*scalars, *args)


def whole(shape):
    return pl.BlockSpec(shape, lambda *_: (0,) * len(shape))


IN_PLACE = pl.BlockSpec(memory_space=pl.ANY)
IN_VMEM = pl.BlockSpec(memory_space=pltpu.VMEM)


def in_hbm(array):
    return pltpu.with_memory_space_constraint(array, pltpu.HBM)


def after(value, *others):
    return lax.optimization_barrier((value, *others))[0]


def turned(bits, levels):
    by = levels // 2
    return (bits << by | bits >> levels - by) & (1 << levels) - 1


def swap(block, bit, count):
    levels = count.bit_length() - 1
    masks = (1 << bit, turned(1 << bit, levels))
    route = [
        (d * count + i, d * count + (i ^ masks[d % 2]))
        for d in range(lax.axis_size("dp"))
        for i in range(count)
    ]
    return lax.ppermute(block, ("dp", "tensor"), route)


def mix_rows(part, heads, c, i, me, signs, attn, full, sent):
    quarter = heads // 4
    at = pl.ds(pl.multiple_of(c * full.shape[0] + i * ROWS, ROWS), ROWS)
    rows = pl.ds(pl.multiple_of(i * ROWS, ROWS), ROWS)

    def head(h):
        sign = (2 * signs[me * heads + h] - 1).astype(jnp.float32)
        return attn[at, pl.ds(h * HD, HD)].astype(jnp.float32) * sign

    mixed = [[] for _ in QUARTERS[part]]
    for h in range(quarter):
        a, b, c2, d = [head(q * quarter + h) for q in range(4)]
        upper, lower = (a + c2, b + d), (a - c2, b - d)
        for k, q in enumerate(QUARTERS[part]):
            one, two = lower if q & 2 else upper
            mixed[k].append(one - two if q & 1 else one + two)
    for k, v in enumerate(mixed):
        step = 1
        while step < quarter:
            for lo in range(quarter):
                if not lo & step:
                    a, b = v[lo], v[lo | step]
                    v[lo], v[lo | step] = a + b, a - b
            step *= 2
        for h in range(quarter):
            cols = pl.ds((k * quarter + h) * HD, HD)
            full[rows, cols] = v[h]
            sent[rows, cols] = v[h].astype(sent.dtype)


def mix_kernel(part, heads, me_ref, *refs):
    if part == 0:
        attn_hbm, signs_hbm, *outs, attn, signs, sem = refs
    else:
        attn, signs_hbm, gain_hbm, *outs, signs, gain, sem = refs
    me = me_ref[0]
    get_signs = pltpu.make_async_copy(signs_hbm, signs, sem.at[0])
    get_signs.start()
    size = outs[0].shape[0]
    step = attn.shape[0] // PIECES
    pieces = []
    if part == 0:
        for k in range(PIECES):
            rows = pl.ds(k * step, step)
            pieces.append(
                pltpu.make_async_copy(attn_hbm.at[rows, :], attn.at[rows, :], sem.at[2 + k])
            )
            pieces[k].start()
    else:
        get_gain = pltpu.make_async_copy(gain_hbm, gain, sem.at[1])
        get_gain.start()
        get_gain.wait()
        sent = outs[1]
        shape = (sent.shape[0] - size, sent.shape[1])
        row = lax.broadcasted_iota(jnp.int32, shape, 0)
        block = jnp.zeros(shape, jnp.float32)
        for k in range(gain.shape[0] // shape[1]):
            piece = gain[pl.ds(k * shape[1], shape[1])].astype(jnp.float32)
            block = jnp.where(row == k, jnp.broadcast_to(piece[None, :], shape), block)
        sent[size:, :] = block.astype(sent.dtype)
    get_signs.wait()
    for k in range(PIECES):
        if pieces:
            pieces[k].wait()
        c, first = k * step // size, k * step % size // ROWS
        full, sent = outs[2 * c : 2 * c + 2]

        @pl.loop(first, first + step // ROWS)
        def _(i):
            mix_rows(part, heads, c, i, me, signs, attn, full, sent)


def mix(attn, me, signs, gain, part, colors, count):
    rows, cols = attn.shape
    shape = (rows // colors, cols // 4 * len(QUARTERS[part]))
    ride = -(-count // 2 * (gain.shape[0] // shape[1]) // ROWS) * ROWS
    outs = []
    for c in range(colors):
        sent = (shape[0] + ride * (part > 0 and c == 0), shape[1])
        outs += [(shape, jnp.float32, whole(shape)), (sent, jnp.bfloat16, whole(sent))]
    kinds = [jax.ShapeDtypeStruct] * len(outs)
    scratch = [pltpu.SMEM(signs.shape, signs.dtype)]
    if part == 0:
        outs.append((attn.shape, attn.dtype, IN_VMEM))
        kinds.append(pltpu.VMEM)
    else:
        scratch.append(pltpu.VMEM(gain.shape, gain.dtype))
    scratch.append(pltpu.SemaphoreType.DMA((2 + PIECES,)))
    return call(
        functools.partial(mix_kernel, part, cols // HD),
        1,
        [me],
        [IN_VMEM, IN_PLACE, IN_PLACE] if part else [IN_PLACE] * 2,
        [attn, in_hbm(signs), in_hbm(gain)] if part else [in_hbm(attn), in_hbm(signs)],
        outs,
        cost(6 * attn.size, 5 * attn.size),
        scratch,
        kinds,
    )


def load_kernel(slab, half, gate_ref, w_hbm, out, sem):
    del gate_ref
    depth, width = out.shape
    count = sem.shape[0]
    step, span = depth // PIECES, width // count
    copies = []
    for d in range(count):
        for k in range(PIECES):
            rows = pl.ds(slab * depth + k * step, step)
            cols = pl.ds((d * HALVES + half) * span, span)
            to = out.at[pl.ds(k * step, step), pl.ds(d * span, span)]
            copies.append(pltpu.make_async_copy(w_hbm.at[rows, cols], to, sem.at[d, k]))
    for copy in copies:
        copy.start()
    for copy in copies:
        copy.wait()


def load(w, gate, slab, half, count, flops=0):
    shape = (w.shape[0] // SLABS, w.shape[1] // HALVES)
    return call(
        functools.partial(load_kernel, slab, half),
        1,
        [gate],
        [IN_PLACE],
        [in_hbm(w)],
        [(shape, w.dtype, IN_VMEM)],
        cost(flops, 0),
        [pltpu.SemaphoreType.DMA((count, PIECES))],
        [pltpu.VMEM],
    )[0]


def combine(order, me, own, recvs, rows):
    v = own[rows, :]
    for bit, recv in zip(order, recvs):
        flip = (1 - 2 * (me >> bit & 1)).astype(jnp.float32)
        v = recv[rows, :].astype(jnp.float32) + flip * v
    return v


def stage_kernel(orders, scale, ride, ride_rows, me_ref, *refs):
    riders, ins, out = refs[:ride], refs[ride:-1], refs[-1]
    me = me_ref[0]
    per = len(ins) // len(orders)
    size = ins[0].shape[0]
    for c, order in enumerate(orders):
        own, *recvs = ins[c * per : (c + 1) * per]

        @pl.loop(0, size // ROWS)
        def _(i):
            rows = pl.ds(pl.multiple_of(i * ROWS, ROWS), ROWS)
            to = pl.ds(pl.multiple_of(c * size + i * ROWS, ROWS), ROWS)
            out[to, :] = (combine(order, me, own, recvs, rows) * scale).astype(out.dtype)

    if ride:
        shape = (out.shape[0] - size, out.shape[1])
        row = lax.broadcasted_iota(jnp.int32, shape, 0)
        known = ride_rows
        block = riders[0][size:, :].astype(jnp.float32)
        for rider in riders[1:]:
            more = pltpu.roll(rider[size:, :].astype(jnp.float32), known, 0)
            block = jnp.where(row < known, block, more)
            known *= 2
        out[size:, :] = block.astype(out.dtype)


def stage(blocks, orders, me, scale, riders=(), ride_rows=0):
    flat = [*riders, *[b for block in blocks for b in block]]
    rows, cols = blocks[0][0].shape
    shape = (riders[0].shape[0] if riders else rows * len(blocks), cols)
    return call(
        functools.partial(stage_kernel, orders, scale, len(riders), ride_rows),
        1,
        [me],
        [whole(f.shape) for f in flat],
        flat,
        [(shape, jnp.bfloat16, whole(shape))],
        cost(4 * rows * cols * len(flat), 2 * rows * cols * (len(flat) + 2)),
    )[0]


def send_lists(order):
    lists = []
    for s, bit in enumerate(order):
        members = [1 << bit]
        for later in reversed(order[s + 1 :]):
            members = members + [m | 1 << later for m in members]
        lists.append(members)
    return lists + [[0]]


def project_kernel(plan, pieces, counts, adds, width, tbl_ref, *refs):
    rots, slabs = refs[: counts[0]], refs[counts[0] : sum(counts)]
    refs = refs[sum(counts) :]
    outs = refs[sum(adds) :]
    for step, (out, lead, add, add_lead) in enumerate(plan):
        cols = pl.ds(pl.multiple_of(tbl_ref[step] * width, width), width)
        acc = None
        for rot, col, slab, row, depth in pieces:
            term = jnp.dot(
                rots[rot][:, col : col + depth],
                slabs[slab][row : row + depth, cols],
                preferred_element_type=jnp.float32,
            )
            acc = term if acc is None else acc + term
        if add is not None:
            first = sum(adds[:add])
            more = [a[add_lead].astype(jnp.float32) for a in refs[first : first + adds[add]]]
            acc = acc + (more[0] if len(more) == 1 else jnp.concatenate(more, axis=1))
        outs[out][lead] = acc.astype(outs[out].dtype)


def project(rots, slabs, pieces, tbl, spans, width, dtypes, adds=(), leads=None):
    rows = rots[0].shape[0]
    plan = [(k, n) for k, (_, count) in enumerate(spans) for n in range(count)]
    if leads is None:
        leads = plan if adds else [(None, None)] * len(plan)
    plan = [(*to, *add) for to, add in zip(plan, leads)]
    args = [*rots, *slabs, *[a for add in adds for a in add]]
    counts = [len(rots), len(slabs)]
    return call(
        functools.partial(
            project_kernel, plan, pieces, counts, [len(add) for add in adds], width
        ),
        1,
        [tbl],
        [IN_VMEM] * len(args),
        args,
        [
            ((n, rows, width), dtype, whole((n, rows, width)))
            for (_, n), dtype in zip(spans, dtypes)
        ],
        cost(PROJECT_FLOPS, 0),
    )


def close_kernel(colors, residual, exps, *refs):
    terms, out = refs[:-1], refs[-1]
    per = len(terms) // colors
    width = residual.shape[1] // colors
    for c in range(colors):
        cols = pl.ds(c * width, width)
        own, *recvs = terms[c * per : (c + 1) * per]
        acc = own[0].astype(jnp.float32)
        for recv in recvs:
            acc = acc + recv[0].astype(jnp.float32)
        acc = acc * jnp.exp2(exps[:, cols].astype(jnp.float32))
        out[c] = (residual[:, cols].astype(jnp.float32) + acc).astype(jnp.bfloat16)


def close(residual, exps, terms, at):
    colors = len(terms)
    _, rows, width = terms[0][0].shape
    span = width * colors
    flat = [t for color in terms for t in color]
    shape = (colors, rows, width)
    return call(
        functools.partial(close_kernel, colors),
        1,
        [],
        [
            pl.BlockSpec((rows, span), lambda i: (0, at)),
            pl.BlockSpec((1, span), lambda i: (0, at)),
        ]
        + [whole((1, rows, width))] * len(flat),
        [residual, exps, *flat],
        [(shape, jnp.bfloat16, whole(shape))],
        cost(10 * rows * span, 2 * rows * width * (len(flat) + 2 * colors)),
    )[0]


def kv_kernel(plan, gain_at, counts, colors, has_prev, channels, at, span, tbl_ref, w, *refs):
    xs, riders, rest = refs[: counts[0]], refs[counts[0] : sum(counts)], refs[sum(counts) :]
    rows, cols = xs[0].shape[-2], w.shape[1]
    product = rest[0][...] if has_prev else jnp.zeros((rows, cols), jnp.float32)
    square = rest[1][...] if has_prev else jnp.zeros((rows, HD), jnp.float32)
    rest = rest[2 * has_prev :]
    for step, blocks in enumerate(plan):
        rider, row = gain_at[step]
        rider = riders[rider]
        for k, lead, c in blocks:
            hidden = xs[k][lead].astype(jnp.float32)
            depth = hidden.shape[1]
            part, col = divmod(at * span + c * depth, rider.shape[1])
            gain = rider[rows // colors :, col : col + depth].astype(jnp.float32)
            gain = gain[row + part : row + part + 1]
            scaled = (hidden * gain).astype(jnp.bfloat16)
            first = pl.multiple_of((tbl_ref[step] + at) * span + c * depth, depth)
            product = product + jnp.dot(
                scaled, w[pl.ds(first, depth), :], preferred_element_type=jnp.float32
            )
            hidden = hidden * hidden
            for b in range(depth // HD):
                square = square + hidden[:, b * HD : (b + 1) * HD]
    if channels:
        exps, out = rest
        mean = jnp.sum(square, axis=1, keepdims=True) / channels
        scale = jnp.exp2(exps[...].astype(jnp.float32))
        out[...] = (product * lax.rsqrt(mean + EPS) * scale).astype(out.dtype)
    else:
        rest[0][...], rest[1][...] = product, square


def kv_step(plan, arrays, riders, gain_at, colors, w_kv, tbl, at, span, prev, exps, channels):
    used = sorted({k for blocks in plan for k, _, _ in blocks})
    xs = [arrays[k] for k in used]
    plan = [[(used.index(k), lead, c) for k, lead, c in blocks] for blocks in plan]
    rows = xs[0].shape[1]
    cols = w_kv.shape[1]
    extra = list(prev or ())
    if channels:
        extra.append(exps)
        outs = [((rows, cols), jnp.bfloat16)]
    else:
        outs = [((rows, cols), jnp.float32), ((rows, HD), jnp.float32)]
    args = [w_kv, *xs, *riders, *extra]
    counts = [len(xs), len(riders)]
    return call(
        functools.partial(
            kv_kernel, plan, gain_at, counts, colors, prev is not None, channels, at, span
        ),
        1,
        [tbl],
        [IN_VMEM] * len(args),
        args,
        [(shape, dtype, whole(shape)) for shape, dtype in outs],
        cost(
            2 * rows * span * cols * len(plan), 2 * span * (rows + cols) * len(plan) + 4 * rows * cols
        ),
    )


def gather(x, orders, count):
    colors = x.shape[0]
    arrays, where = [x], {0: [(0, c) for c in range(colors)]}
    levels = len(orders[0])
    for bit in range(levels):
        arrays.append(swap(x, bit, count))
        where[1 << bit] = [(len(arrays) - 1, c) for c in range(colors)]
    for size in range(2, levels + 1):
        for r in range(count):
            if r.bit_count() == size:
                where[r] = []
                for c, order in enumerate(orders):
                    hop = max((b for b in range(levels) if r >> b & 1), key=order.index)
                    k, at = where[r ^ 1 << hop][c]
                    arrays.append(swap(arrays[k][at : at + 1], hop, count))
                    where[r].append((len(arrays) - 1, 0))
    plan = [[(k, at, c) for c, (k, at) in enumerate(blocks)] for blocks in where.values()]
    return arrays, list(zip(where, plan))


def body(attn_out, head_signs, w_out, out_exp, residual, norm_gain, w_kv, kv_exp):
    count = lax.axis_size("tensor")
    levels = count.bit_length() - 1
    me = lax.axis_index("tensor").astype(jnp.int32)
    odd = lax.axis_index("dp") % 2 == 1
    me_arr = me.reshape(1)
    by = levels // 2
    unturned = (me >> by | me << levels - by) & count - 1
    logical = jnp.where(odd, unturned, me).reshape(1)
    depth, local = w_out.shape[0], residual.shape[1]
    channels = local * count
    orders = [list(range(levels))]
    orders.append(orders[0][levels // 2 :] + orders[0][: levels // 2])
    colors = len(orders)
    half = local // HALVES
    wide = half // colors

    def devices(rel):
        far = jnp.array([turned(r, levels) for r in rel], jnp.int32)
        return me ^ jnp.where(odd, far, jnp.array(rel, jnp.int32))

    lists = [send_lists(order) for order in orders]

    def blocks_of(stages):
        spans, rel, color = [], [], []
        for s in stages:
            for c in range(colors):
                spans.append((len(rel), len(lists[c][s])))
                rel += lists[c][s]
                color += [c] * len(lists[c][s])
        return devices(rel) * colors + jnp.array(color, jnp.int32), spans

    exps = out_exp.reshape(1, -1)
    kv_exps = kv_exp.reshape(1, -1)

    rots, blocks, riders = [], [], []
    slabs = [[None] * SLABS for _ in range(HALVES)]
    attn = attn_out
    for p in range(len(QUARTERS)):
        mixed = mix(attn, me_arr, head_signs, norm_gain, p, colors, count)
        if p == 0:
            attn = mixed[-1]
        blocks.append([])
        for c, order in enumerate(orders):
            own, sent = mixed[2 * c : 2 * c + 2]
            blocks[p].append([own, swap(sent, order[0], count)])
            if p == 1 and c == 0:
                riders += [sent, blocks[p][c][1]]
    ride_rows = local // riders[0].shape[1]
    slabs[0][0] = load(w_out, after(me_arr, sent), 0, 0, count)
    here = after(logical, slabs[0][0])
    for s in range(1, levels):
        sends = []
        for p in range(len(QUARTERS)):
            for c, order in enumerate(orders):
                ride = p == 1 and c == 0
                send = stage(
                    [blocks[p][c]], [order], here, 1.0, riders if ride else (), ride_rows
                )
                blocks[p][c].append(swap(send, order[s], count))
                sends.append(send)
                if ride:
                    riders.append(blocks[p][c][-1])
            here = after(logical, *sends)
    slabs[0][1] = load(w_out, after(me_arr, *sends), 1, 0, count, BUSY)
    slabs[1][0] = load(w_out, after(me_arr, slabs[0][1]), 0, 1, count, BUSY)
    here = after(logical, slabs[1][0])
    scale = head_signs.shape[0] ** -0.5
    for p in range(len(QUARTERS)):
        rots.append(stage(blocks[p], orders, here, scale))
        here = after(logical, rots[p])

    gain_at, known = {0: (0, 0)}, [0]
    for t, bit in enumerate(orders[0]):
        gain_at.update({r ^ 1 << bit: (t + 1, ride_rows * k) for k, r in enumerate(known)})
        known += [r ^ 1 << bit for r in known]

    cuts = (0, depth // 2, depth // 4 * 3, depth)
    pieces = [(0, 0, 0, 0), (0, cuts[1], 1, 0), (1, 0, 1, cuts[2] - cuts[1])]
    pieces = [(*piece, to - at) for piece, at, to in zip(pieces, cuts, cuts[1:])]
    ready = pieces[:2]
    late = [(0, 0, 0, *pieces[2][3:])]

    bf16, f32 = jnp.bfloat16, jnp.float32
    received = [[] for _ in range(HALVES)]
    tbl, spans = blocks_of([0])
    prevs = project(rots[:1], slabs[0], ready, tbl, spans, wide, [f32] * colors)
    sends = project(
        rots[1:], slabs[0][1:], late, tbl, spans, wide, [bf16] * colors, [[p] for p in prevs]
    )
    received[0] = [swap(send, order[0], count) for send, order in zip(sends, orders)]
    slabs[1][1] = load(w_out, after(me_arr, *sends), 1, 1, count)
    for v in range(1, HALVES):
        tbl, spans = blocks_of([0])
        sends = project(rots, slabs[v], pieces, tbl, spans, wide, [bf16] * colors)
        received[v] = [swap(send, order[0], count) for send, order in zip(sends, orders)]

    later = range(1, levels + 1)
    leads = []
    for s in later:
        for c in range(colors):
            n = len(lists[c][s])
            leads += [(c, k + n * (s < levels)) for k in range(n)]
    dtypes = [bf16 if s == 1 and levels > 1 else f32 for s in later for _ in range(colors)]

    resids, found = [], []
    for v in range(HALVES):
        tbl, spans = blocks_of(later)
        adds = [[r] for r in received[v]]
        parts = project(rots, slabs[v], pieces, tbl, spans, wide, dtypes, adds, leads)
        terms = []
        for c, order in enumerate(orders):
            recvs = []
            for s in range(1, levels):
                send = parts[(s - 1) * colors + c]
                if recvs:
                    size = send.shape[0]
                    for recv in recvs:
                        send = send + recv[size : 2 * size].astype(f32)
                    send = send.astype(bf16)
                recvs.append(swap(send, order[s], count))
            terms.append([parts[(levels - 1) * colors + c], *recvs])
        out = close(residual, exps, terms, v)
        resids += list(out)
        found.append(gather(out, orders, count))

    runs = []
    for far in (False, True):
        for v, (arrays, blocks) in enumerate(found):
            run = [b for b in blocks if (b[0].bit_count() > 1) == far]
            if run:
                runs.append((v, arrays, run))
    running = None
    for k, (v, arrays, run) in enumerate(runs):
        running = kv_step(
            [plan for _, plan in run],
            arrays,
            riders,
            [gain_at[r] for r, _ in run],
            colors,
            w_kv,
            devices([r for r, _ in run]) * HALVES,
            v,
            half,
            running,
            kv_exps,
            channels * (k == len(runs) - 1),
        )
    return jnp.concatenate(resids, axis=1), running[0]


def solution(mesh):
    placed = (
        P("dp", "tensor"),
        P(),
        P("tensor", None),
        P("tensor"),
        P("dp", "tensor"),
        P("tensor"),
        P(None, "tensor"),
        P("tensor"),
    )
    return jax.shard_map(
        body,
        mesh=mesh,
        in_specs=placed,
        out_specs=(P("dp", "tensor"), P("dp", "tensor")),
        check_vma=False,
    )
```

```python
import functools

import jax
import jax.numpy as jnp
from jax import lax
from jax.experimental import pallas as pl
from jax.experimental.pallas import tpu as pltpu
from jax.sharding import PartitionSpec as P

HD = 128
EPS = 1e-05
QUARTERS = ((0, 1, 2), (3,))
HALVES = 2
SLABS = 2
PIECES = 4
ROWS = 16
UNROLL = 4
VMEM = 4 * 1024 * 1024
PROJECT_FLOPS = 1e6
BUSY = 4e9


def cost(flops, nbytes):
    return pl.CostEstimate(flops=int(flops), bytes_accessed=int(nbytes), transcendentals=0)


def call(kernel, grid, scalars, in_specs, args, outs, estimate, scratch=(), kinds=None):
    kinds = kinds or [jax.ShapeDtypeStruct] * len(outs)
    return pl.pallas_call(
        kernel,
        grid_spec=pltpu.PrefetchScalarGridSpec(
            num_scalar_prefetch=len(scalars),
            grid=(grid,),
            in_specs=in_specs,
            out_specs=[spec for _, _, spec in outs],
            scratch_shapes=list(scratch),
        ),
        out_shape=[kind(shape, dtype) for (shape, dtype, _), kind in zip(outs, kinds)],
        compiler_params=pltpu.CompilerParams(vmem_limit_bytes=VMEM),
        cost_estimate=estimate,
    )(*scalars, *args)


def whole(shape):
    return pl.BlockSpec(shape, lambda *_: (0,) * len(shape))


IN_PLACE = pl.BlockSpec(memory_space=pl.ANY)
IN_VMEM = pl.BlockSpec(memory_space=pltpu.VMEM)


def in_hbm(array):
    return pltpu.with_memory_space_constraint(array, pltpu.HBM)


def after(value, *others):
    return lax.optimization_barrier((value, *others))[0]


def turned(bits, levels):
    by = levels // 2
    return (bits << by | bits >> levels - by) & (1 << levels) - 1


def swap(block, bit, count):
    levels = count.bit_length() - 1
    masks = (1 << bit, turned(1 << bit, levels))
    route = [
        (d * count + i, d * count + (i ^ masks[d % 2]))
        for d in range(lax.axis_size("dp"))
        for i in range(count)
    ]
    return lax.ppermute(block, ("dp", "tensor"), route)


def mix_rows(part, heads, c, i, me, signs, attn, full, sent):
    quarter = heads // 4
    at = pl.ds(pl.multiple_of(c * full.shape[0] + i * ROWS, ROWS), ROWS)
    rows = pl.ds(pl.multiple_of(i * ROWS, ROWS), ROWS)

    def head(h):
        sign = (2 * signs[me * heads + h] - 1).astype(jnp.float32)
        return attn[at, pl.ds(h * HD, HD)].astype(jnp.float32) * sign

    mixed = [[] for _ in QUARTERS[part]]
    for h in range(quarter):
        a, b, c2, d = [head(q * quarter + h) for q in range(4)]
        upper, lower = (a + c2, b + d), (a - c2, b - d)
        for k, q in enumerate(QUARTERS[part]):
            one, two = lower if q & 2 else upper
            mixed[k].append(one - two if q & 1 else one + two)
    for k, v in enumerate(mixed):
        step = 1
        while step < quarter:
            for lo in range(quarter):
                if not lo & step:
                    a, b = v[lo], v[lo | step]
                    v[lo], v[lo | step] = a + b, a - b
            step *= 2
        for h in range(quarter):
            cols = pl.ds((k * quarter + h) * HD, HD)
            full[rows, cols] = v[h]
            sent[rows, cols] = v[h].astype(sent.dtype)


def mix_kernel(part, heads, me_ref, *refs):
    if part == 0:
        attn_hbm, signs_hbm, *outs, attn, signs, sem = refs
    else:
        attn, signs_hbm, gain_hbm, *outs, signs, gain, sem = refs
    me = me_ref[0]
    get_signs = pltpu.make_async_copy(signs_hbm, signs, sem.at[0])
    get_signs.start()
    size = outs[0].shape[0]
    step = attn.shape[0] // PIECES
    pieces = []
    if part == 0:
        for k in range(PIECES):
            rows = pl.ds(k * step, step)
            pieces.append(
                pltpu.make_async_copy(attn_hbm.at[rows, :], attn.at[rows, :], sem.at[2 + k])
            )
            pieces[k].start()
    else:
        get_gain = pltpu.make_async_copy(gain_hbm, gain, sem.at[1])
        get_gain.start()
        get_gain.wait()
        sent = outs[1]
        shape = (sent.shape[0] - size, sent.shape[1])
        row = lax.broadcasted_iota(jnp.int32, shape, 0)
        block = jnp.zeros(shape, jnp.float32)
        for k in range(gain.shape[0] // shape[1]):
            piece = gain[pl.ds(k * shape[1], shape[1])].astype(jnp.float32)
            block = jnp.where(row == k, jnp.broadcast_to(piece[None, :], shape), block)
        sent[size:, :] = block.astype(sent.dtype)
    get_signs.wait()
    for k in range(PIECES):
        if pieces:
            pieces[k].wait()
        c, first = k * step // size, k * step % size // ROWS
        full, sent = outs[2 * c : 2 * c + 2]

        @pl.loop(first, first + step // ROWS, unroll=UNROLL)
        def _(i):
            mix_rows(part, heads, c, i, me, signs, attn, full, sent)


def mix(attn, me, signs, gain, part, colors, count):
    rows, cols = attn.shape
    shape = (rows // colors, cols // 4 * len(QUARTERS[part]))
    ride = -(-count // 2 * (gain.shape[0] // shape[1]) // ROWS) * ROWS
    outs = []
    for c in range(colors):
        sent = (shape[0] + ride * (part > 0 and c == 0), shape[1])
        outs += [(shape, jnp.float32, whole(shape)), (sent, jnp.bfloat16, whole(sent))]
    kinds = [jax.ShapeDtypeStruct] * len(outs)
    scratch = [pltpu.SMEM(signs.shape, signs.dtype)]
    if part == 0:
        outs.append((attn.shape, attn.dtype, IN_VMEM))
        kinds.append(pltpu.VMEM)
    else:
        scratch.append(pltpu.VMEM(gain.shape, gain.dtype))
    scratch.append(pltpu.SemaphoreType.DMA((2 + PIECES,)))
    return call(
        functools.partial(mix_kernel, part, cols // HD),
        1,
        [me],
        [IN_VMEM, IN_PLACE, IN_PLACE] if part else [IN_PLACE] * 2,
        [attn, in_hbm(signs), in_hbm(gain)] if part else [in_hbm(attn), in_hbm(signs)],
        outs,
        cost(6 * attn.size, 5 * attn.size),
        scratch,
        kinds,
    )


def load_kernel(slab, half, gate_ref, w_hbm, out, sem):
    del gate_ref
    depth, width = out.shape
    count = sem.shape[0]
    step, span = depth // PIECES, width // count
    copies = []
    for d in range(count):
        for k in range(PIECES):
            rows = pl.ds(slab * depth + k * step, step)
            cols = pl.ds((d * HALVES + half) * span, span)
            to = out.at[pl.ds(k * step, step), pl.ds(d * span, span)]
            copies.append(pltpu.make_async_copy(w_hbm.at[rows, cols], to, sem.at[d, k]))
    for copy in copies:
        copy.start()
    for copy in copies:
        copy.wait()


def load(w, gate, slab, half, count, flops=0):
    shape = (w.shape[0] // SLABS, w.shape[1] // HALVES)
    return call(
        functools.partial(load_kernel, slab, half),
        1,
        [gate],
        [IN_PLACE],
        [in_hbm(w)],
        [(shape, w.dtype, IN_VMEM)],
        cost(flops, 0),
        [pltpu.SemaphoreType.DMA((count, PIECES))],
        [pltpu.VMEM],
    )[0]


def combine(order, me, own, recvs, rows):
    v = own[rows, :]
    for bit, recv in zip(order, recvs):
        flip = (1 - 2 * (me >> bit & 1)).astype(jnp.float32)
        v = recv[rows, :].astype(jnp.float32) + flip * v
    return v


def combine_into(out, orders, scale, me, ins):
    per = len(ins) // len(orders)
    size = ins[0].shape[0]
    for c, order in enumerate(orders):
        own, *recvs = ins[c * per : (c + 1) * per]

        @pl.loop(0, size // ROWS, unroll=UNROLL)
        def _(i):
            rows = pl.ds(pl.multiple_of(i * ROWS, ROWS), ROWS)
            to = pl.ds(pl.multiple_of(c * size + i * ROWS, ROWS), ROWS)
            out[to, :] = (combine(order, me, own, recvs, rows) * scale).astype(out.dtype)


def stage_kernel(order, ride, ride_rows, me_ref, *refs):
    riders, ins, out = refs[:ride], refs[ride:-1], refs[-1]
    size = ins[0].shape[0]
    combine_into(out, [order], 1.0, me_ref[0], ins)
    if ride:
        shape = (out.shape[0] - size, out.shape[1])
        row = lax.broadcasted_iota(jnp.int32, shape, 0)
        known = ride_rows
        block = riders[0][size:, :].astype(jnp.float32)
        for rider in riders[1:]:
            more = pltpu.roll(rider[size:, :].astype(jnp.float32), known, 0)
            block = jnp.where(row < known, block, more)
            known *= 2
        out[size:, :] = block.astype(out.dtype)


def stage(block, order, me, riders=(), ride_rows=0):
    flat = [*riders, *block]
    shape = riders[0].shape if riders else block[0].shape
    return call(
        functools.partial(stage_kernel, order, len(riders), ride_rows),
        1,
        [me],
        [whole(f.shape) for f in flat],
        flat,
        [(shape, jnp.bfloat16, whole(shape))],
        cost(4 * block[0].size * len(flat), 2 * block[0].size * (len(flat) + 2)),
    )[0]


def send_lists(order):
    lists = []
    for s, bit in enumerate(order):
        members = [1 << bit]
        for later in reversed(order[s + 1 :]):
            members = members + [m | 1 << later for m in members]
        lists.append(members)
    return lists + [[0]]


def project_kernel(plan, pieces, counts, adds, width, orders, scale, tbl_ref, me_ref, *refs):
    raws, rots = refs[: counts[0]], refs[counts[0] : sum(counts[:2])]
    slabs, refs = refs[sum(counts[:2]) : sum(counts)], refs[sum(counts) :]
    outs = refs[sum(adds) :]
    if raws:
        combine_into(outs[-1], orders, scale, me_ref[0], raws)
        rots = [outs[-1]]
    for step, (out, lead, add, add_lead) in enumerate(plan):
        cols = pl.ds(pl.multiple_of(tbl_ref[step] * width, width), width)
        acc = None
        for rot, col, slab, row, depth in pieces:
            term = jnp.dot(
                rots[rot][:, col : col + depth],
                slabs[slab][row : row + depth, cols],
                preferred_element_type=jnp.float32,
            )
            acc = term if acc is None else acc + term
        if add is not None:
            first = sum(adds[:add])
            more = [a[add_lead].astype(jnp.float32) for a in refs[first : first + adds[add]]]
            acc = acc + (more[0] if len(more) == 1 else jnp.concatenate(more, axis=1))
        outs[out][lead] = acc.astype(outs[out].dtype)


def project(
    rots, slabs, pieces, tbl, spans, width, dtypes, me, adds=(), leads=None, raws=(), orders=(), scale=1.0
):
    plan = [(k, n) for k, (_, count) in enumerate(spans) for n in range(count)]
    if leads is None:
        leads = plan if adds else [(None, None)] * len(plan)
    plan = [(*to, *add) for to, add in zip(plan, leads)]
    flat = [r for raw in raws for r in raw]
    args = [*flat, *rots, *slabs, *[a for add in adds for a in add]]
    counts = [len(flat), len(rots), len(slabs)]
    rows = rots[0].shape[0] if rots else sum(raw[0].shape[0] for raw in raws)
    shapes = [((n, rows, width), dtype) for (_, n), dtype in zip(spans, dtypes)]
    if raws:
        shapes.append(((rows, flat[0].shape[1]), jnp.bfloat16))
    return call(
        functools.partial(
            project_kernel, plan, pieces, counts, [len(a) for a in adds], width, orders, scale
        ),
        1,
        [tbl, me],
        [IN_VMEM] * len(args),
        args,
        [(shape, dtype, whole(shape)) for shape, dtype in shapes],
        cost(PROJECT_FLOPS, 0),
    )


def close_kernel(colors, residual, exps, *refs):
    terms, out = refs[:-1], refs[-1]
    per = len(terms) // colors
    width = residual.shape[1] // colors
    for c in range(colors):
        cols = pl.ds(c * width, width)
        own, *recvs = terms[c * per : (c + 1) * per]
        acc = own[0].astype(jnp.float32)
        for recv in recvs:
            acc = acc + recv[0].astype(jnp.float32)
        acc = acc * jnp.exp2(exps[:, cols].astype(jnp.float32))
        out[c] = (residual[:, cols].astype(jnp.float32) + acc).astype(jnp.bfloat16)


def close(residual, exps, terms, at):
    colors = len(terms)
    _, rows, width = terms[0][0].shape
    span = width * colors
    flat = [t for color in terms for t in color]
    shape = (colors, rows, width)
    return call(
        functools.partial(close_kernel, colors),
        1,
        [],
        [
            pl.BlockSpec((rows, span), lambda i: (0, at)),
            pl.BlockSpec((1, span), lambda i: (0, at)),
        ]
        + [whole((1, rows, width))] * len(flat),
        [residual, exps, *flat],
        [(shape, jnp.bfloat16, whole(shape))],
        cost(10 * rows * span, 2 * rows * width * (len(flat) + 2 * colors)),
    )[0]


def kv_kernel(plan, gain_at, counts, colors, has_prev, channels, at, span, tbl_ref, w, *refs):
    xs, riders, rest = refs[: counts[0]], refs[counts[0] : sum(counts)], refs[sum(counts) :]
    rows, cols = xs[0].shape[-2], w.shape[1]
    product = rest[0][...] if has_prev else jnp.zeros((rows, cols), jnp.float32)
    square = rest[1][...] if has_prev else jnp.zeros((rows, HD), jnp.float32)
    rest = rest[2 * has_prev :]
    for step, blocks in enumerate(plan):
        rider, row = gain_at[step]
        rider = riders[rider]
        for k, lead, c in blocks:
            hidden = xs[k][lead].astype(jnp.float32)
            depth = hidden.shape[1]
            part, col = divmod(at * span + c * depth, rider.shape[1])
            gain = rider[rows // colors :, col : col + depth].astype(jnp.float32)
            gain = gain[row + part : row + part + 1]
            scaled = (hidden * gain).astype(jnp.bfloat16)
            first = pl.multiple_of((tbl_ref[step] + at) * span + c * depth, depth)
            product = product + jnp.dot(
                scaled, w[pl.ds(first, depth), :], preferred_element_type=jnp.float32
            )
            hidden = hidden * hidden
            for b in range(depth // HD):
                square = square + hidden[:, b * HD : (b + 1) * HD]
    if channels:
        exps, out = rest
        mean = jnp.sum(square, axis=1, keepdims=True) / channels
        scale = jnp.exp2(exps[...].astype(jnp.float32))
        out[...] = (product * lax.rsqrt(mean + EPS) * scale).astype(out.dtype)
    else:
        rest[0][...], rest[1][...] = product, square


def kv_step(plan, arrays, riders, gain_at, colors, w_kv, tbl, at, span, prev, exps, channels):
    used = sorted({k for blocks in plan for k, _, _ in blocks})
    xs = [arrays[k] for k in used]
    plan = [[(used.index(k), lead, c) for k, lead, c in blocks] for blocks in plan]
    rows = xs[0].shape[1]
    cols = w_kv.shape[1]
    extra = list(prev or ())
    if channels:
        extra.append(exps)
        outs = [((rows, cols), jnp.bfloat16)]
    else:
        outs = [((rows, cols), jnp.float32), ((rows, HD), jnp.float32)]
    args = [w_kv, *xs, *riders, *extra]
    counts = [len(xs), len(riders)]
    return call(
        functools.partial(
            kv_kernel, plan, gain_at, counts, colors, prev is not None, channels, at, span
        ),
        1,
        [tbl],
        [IN_VMEM] * len(args),
        args,
        [(shape, dtype, whole(shape)) for shape, dtype in outs],
        cost(
            2 * rows * span * cols * len(plan), 2 * span * (rows + cols) * len(plan) + 4 * rows * cols
        ),
    )


def gather(x, orders, count):
    colors = x.shape[0]
    arrays, where = [x], {0: [(0, c) for c in range(colors)]}
    levels = len(orders[0])
    for bit in range(levels):
        arrays.append(swap(x, bit, count))
        where[1 << bit] = [(len(arrays) - 1, c) for c in range(colors)]
    for size in range(2, levels + 1):
        for r in range(count):
            if r.bit_count() == size:
                where[r] = []
                for c, order in enumerate(orders):
                    hop = max((b for b in range(levels) if r >> b & 1), key=order.index)
                    k, at = where[r ^ 1 << hop][c]
                    arrays.append(swap(arrays[k][at : at + 1], hop, count))
                    where[r].append((len(arrays) - 1, 0))
    plan = [[(k, at, c) for c, (k, at) in enumerate(blocks)] for blocks in where.values()]
    return arrays, list(zip(where, plan))


def body(attn_out, head_signs, w_out, out_exp, residual, norm_gain, w_kv, kv_exp):
    count = lax.axis_size("tensor")
    levels = count.bit_length() - 1
    me = lax.axis_index("tensor").astype(jnp.int32)
    odd = lax.axis_index("dp") % 2 == 1
    me_arr = me.reshape(1)
    by = levels // 2
    unturned = (me >> by | me << levels - by) & count - 1
    logical = jnp.where(odd, unturned, me).reshape(1)
    depth, local = w_out.shape[0], residual.shape[1]
    channels = local * count
    orders = [list(range(levels))]
    orders.append(orders[0][levels // 2 :] + orders[0][: levels // 2])
    colors = len(orders)
    half = local // HALVES
    wide = half // colors

    def devices(rel):
        far = jnp.array([turned(r, levels) for r in rel], jnp.int32)
        return me ^ jnp.where(odd, far, jnp.array(rel, jnp.int32))

    lists = [send_lists(order) for order in orders]

    def blocks_of(stages):
        spans, rel, color = [], [], []
        for s in stages:
            for c in range(colors):
                spans.append((len(rel), len(lists[c][s])))
                rel += lists[c][s]
                color += [c] * len(lists[c][s])
        return devices(rel) * colors + jnp.array(color, jnp.int32), spans

    exps = out_exp.reshape(1, -1)
    kv_exps = kv_exp.reshape(1, -1)

    blocks, riders = [], []
    slabs = [[None] * SLABS for _ in range(HALVES)]
    attn = attn_out
    for p in range(len(QUARTERS)):
        mixed = mix(attn, me_arr, head_signs, norm_gain, p, colors, count)
        if p == 0:
            attn = mixed[-1]
        blocks.append([])
        for c, order in enumerate(orders):
            own, sent = mixed[2 * c : 2 * c + 2]
            blocks[p].append([own, swap(sent, order[0], count)])
            if p == 1 and c == 0:
                riders += [sent, blocks[p][c][1]]
    ride_rows = local // riders[0].shape[1]
    slabs[0][0] = load(w_out, after(me_arr, sent), 0, 0, count)
    here = after(logical, slabs[0][0])
    for s in range(1, levels):
        sends = []
        for p in range(len(QUARTERS)):
            for c, order in enumerate(orders):
                ride = p == 1 and c == 0
                send = stage(blocks[p][c], order, here, riders if ride else (), ride_rows)
                blocks[p][c].append(swap(send, order[s], count))
                sends.append(send)
                if ride:
                    riders.append(blocks[p][c][-1])
            here = after(logical, *sends)
    slabs[0][1] = load(w_out, after(me_arr, *sends), 1, 0, count, BUSY)

    gain_at, known = {0: (0, 0)}, [0]
    for t, bit in enumerate(orders[0]):
        gain_at.update({r ^ 1 << bit: (t + 1, ride_rows * k) for k, r in enumerate(known)})
        known += [r ^ 1 << bit for r in known]

    cuts = (0, depth // 2, depth // 4 * 3, depth)
    pieces = [(0, 0, 0, 0), (0, cuts[1], 1, 0), (1, 0, 1, cuts[2] - cuts[1])]
    pieces = [(*piece, to - at) for piece, at, to in zip(pieces, cuts, cuts[1:])]
    ready = pieces[:2]
    late = [(0, 0, 0, *pieces[2][3:])]

    bf16, f32 = jnp.bfloat16, jnp.float32
    received = [[] for _ in range(HALVES)]
    tbl, spans = blocks_of([0])
    scale = head_signs.shape[0] ** -0.5
    *prevs, rot = project(
        [], slabs[0], ready, tbl, spans, wide, [f32] * colors, logical,
        raws=blocks[0], orders=orders, scale=scale,
    )
    rots = [rot]
    *sends, rot = project(
        [], slabs[0][1:], late, tbl, spans, wide, [bf16] * colors, logical, [[p] for p in prevs],
        raws=blocks[1], orders=orders, scale=scale,
    )
    rots.append(rot)
    received[0] = [swap(send, order[0], count) for send, order in zip(sends, orders)]
    slabs[1][0] = load(w_out, after(me_arr, *sends), 0, 1, count)
    slabs[1][1] = load(w_out, after(me_arr, slabs[1][0]), 1, 1, count)
    for v in range(1, HALVES):
        tbl, spans = blocks_of([0])
        sends = project(rots, slabs[v], pieces, tbl, spans, wide, [bf16] * colors, logical)
        received[v] = [swap(send, order[0], count) for send, order in zip(sends, orders)]

    later = range(1, levels + 1)
    leads = []
    for s in later:
        for c in range(colors):
            n = len(lists[c][s])
            leads += [(c, k + n * (s < levels)) for k in range(n)]
    dtypes = [bf16 if s == 1 and levels > 1 else f32 for s in later for _ in range(colors)]

    resids, found = [], []
    for v in range(HALVES):
        tbl, spans = blocks_of(later)
        adds = [[r] for r in received[v]]
        parts = project(rots, slabs[v], pieces, tbl, spans, wide, dtypes, logical, adds, leads)
        terms = []
        for c, order in enumerate(orders):
            recvs = []
            for s in range(1, levels):
                send = parts[(s - 1) * colors + c]
                if recvs:
                    size = send.shape[0]
                    for recv in recvs:
                        send = send + recv[size : 2 * size].astype(f32)
                    send = send.astype(bf16)
                recvs.append(swap(send, order[s], count))
            terms.append([parts[(levels - 1) * colors + c], *recvs])
        out = close(residual, exps, terms, v)
        resids += list(out)
        found.append(gather(out, orders, count))

    runs = []
    for far in (False, True):
        for v, (arrays, blocks) in enumerate(found):
            run = [b for b in blocks if (b[0].bit_count() > 1) == far]
            if run:
                runs.append((v, arrays, run))
    running = None
    for k, (v, arrays, run) in enumerate(runs):
        running = kv_step(
            [plan for _, plan in run],
            arrays,
            riders,
            [gain_at[r] for r, _ in run],
            colors,
            w_kv,
            devices([r for r, _ in run]) * HALVES,
            v,
            half,
            running,
            kv_exps,
            channels * (k == len(runs) - 1),
        )
    return jnp.concatenate(resids, axis=1), running[0]


def solution(mesh):
    placed = (
        P("dp", "tensor"),
        P(),
        P("tensor", None),
        P("tensor"),
        P("dp", "tensor"),
        P("tensor"),
        P(None, "tensor"),
        P("tensor"),
    )
    return jax.shard_map(
        body,
        mesh=mesh,
        in_specs=placed,
        out_specs=(P("dp", "tensor"), P("dp", "tensor")),
        check_vma=False,
    )
```

```python
import functools

import jax
import jax.numpy as jnp
from jax import lax
from jax.experimental import pallas as pl
from jax.experimental.pallas import tpu as pltpu
from jax.sharding import PartitionSpec as P

HD = 128
EPS = 1e-05
QUARTERS = ((0, 1, 2), (3,))
HALVES = 2
PIECES = 4
LOADS = 4
ROWS = 16
UNROLL = 4
VMEM = 4 * 1024 * 1024
PROJECT_FLOPS = 1e6
BUSY = 4e9


def cost(flops, nbytes):
    return pl.CostEstimate(flops=int(flops), bytes_accessed=int(nbytes), transcendentals=0)


def call(kernel, grid, scalars, in_specs, args, outs, estimate, scratch=(), kinds=None):
    kinds = kinds or [jax.ShapeDtypeStruct] * len(outs)
    return pl.pallas_call(
        kernel,
        grid_spec=pltpu.PrefetchScalarGridSpec(
            num_scalar_prefetch=len(scalars),
            grid=(grid,),
            in_specs=in_specs,
            out_specs=[spec for _, _, spec in outs],
            scratch_shapes=list(scratch),
        ),
        out_shape=[kind(shape, dtype) for (shape, dtype, _), kind in zip(outs, kinds)],
        compiler_params=pltpu.CompilerParams(vmem_limit_bytes=VMEM),
        cost_estimate=estimate,
    )(*scalars, *args)


def whole(shape):
    return pl.BlockSpec(shape, lambda *_: (0,) * len(shape))


IN_PLACE = pl.BlockSpec(memory_space=pl.ANY)
IN_VMEM = pl.BlockSpec(memory_space=pltpu.VMEM)


def in_hbm(array):
    return pltpu.with_memory_space_constraint(array, pltpu.HBM)


def after(value, *others):
    return lax.optimization_barrier((value, *others))[0]


def turned(bits, levels):
    by = levels // 2
    return (bits << by | bits >> levels - by) & (1 << levels) - 1


def swap(block, bit, count):
    levels = count.bit_length() - 1
    masks = (1 << bit, turned(1 << bit, levels))
    route = [
        (d * count + i, d * count + (i ^ masks[d % 2]))
        for d in range(lax.axis_size("dp"))
        for i in range(count)
    ]
    return lax.ppermute(block, ("dp", "tensor"), route)


def mix_rows(part, heads, c, i, me, signs, attn, full, sent):
    quarter = heads // 4
    at = pl.ds(pl.multiple_of(c * full.shape[0] + i * ROWS, ROWS), ROWS)
    rows = pl.ds(pl.multiple_of(i * ROWS, ROWS), ROWS)

    def head(h):
        sign = (2 * signs[me * heads + h] - 1).astype(jnp.float32)
        return attn[at, pl.ds(h * HD, HD)].astype(jnp.float32) * sign

    mixed = [[] for _ in QUARTERS[part]]
    for h in range(quarter):
        a, b, c2, d = [head(q * quarter + h) for q in range(4)]
        upper, lower = (a + c2, b + d), (a - c2, b - d)
        for k, q in enumerate(QUARTERS[part]):
            one, two = lower if q & 2 else upper
            mixed[k].append(one - two if q & 1 else one + two)
    for k, v in enumerate(mixed):
        step = 1
        while step < quarter:
            for lo in range(quarter):
                if not lo & step:
                    a, b = v[lo], v[lo | step]
                    v[lo], v[lo | step] = a + b, a - b
            step *= 2
        for h in range(quarter):
            cols = pl.ds((k * quarter + h) * HD, HD)
            full[rows, cols] = v[h]
            sent[rows, cols] = v[h].astype(sent.dtype)


def mix_kernel(part, heads, me_ref, *refs):
    if part == 0:
        attn_hbm, signs_hbm, *outs, attn, signs, sem = refs
    else:
        attn, signs_hbm, gain_hbm, *outs, signs, gain, sem = refs
    me = me_ref[0]
    get_signs = pltpu.make_async_copy(signs_hbm, signs, sem.at[0])
    get_signs.start()
    size = outs[0].shape[0]
    step = attn.shape[0] // PIECES
    pieces = []
    if part == 0:
        for k in range(PIECES):
            rows = pl.ds(k * step, step)
            pieces.append(
                pltpu.make_async_copy(attn_hbm.at[rows, :], attn.at[rows, :], sem.at[2 + k])
            )
            pieces[k].start()
    else:
        get_gain = pltpu.make_async_copy(gain_hbm, gain, sem.at[1])
        get_gain.start()
        get_gain.wait()
        sent = outs[1]
        shape = (sent.shape[0] - size, sent.shape[1])
        row = lax.broadcasted_iota(jnp.int32, shape, 0)
        block = jnp.zeros(shape, jnp.float32)
        for k in range(gain.shape[0] // shape[1]):
            piece = gain[pl.ds(k * shape[1], shape[1])].astype(jnp.float32)
            block = jnp.where(row == k, jnp.broadcast_to(piece[None, :], shape), block)
        sent[size:, :] = block.astype(sent.dtype)
    get_signs.wait()
    for k in range(PIECES):
        if pieces:
            pieces[k].wait()
        c, first = k * step // size, k * step % size // ROWS
        full, sent = outs[2 * c : 2 * c + 2]

        @pl.loop(first, first + step // ROWS, unroll=UNROLL)
        def _(i):
            mix_rows(part, heads, c, i, me, signs, attn, full, sent)


def mix(attn, me, signs, gain, part, colors, count):
    rows, cols = attn.shape
    shape = (rows // colors, cols // 4 * len(QUARTERS[part]))
    ride = -(-count // 2 * (gain.shape[0] // shape[1]) // ROWS) * ROWS
    outs = []
    for c in range(colors):
        sent = (shape[0] + ride * (part > 0 and c == 0), shape[1])
        outs += [(shape, jnp.float32, whole(shape)), (sent, jnp.bfloat16, whole(sent))]
    kinds = [jax.ShapeDtypeStruct] * len(outs)
    scratch = [pltpu.SMEM(signs.shape, signs.dtype)]
    if part == 0:
        outs.append((attn.shape, attn.dtype, IN_VMEM))
        kinds.append(pltpu.VMEM)
    else:
        scratch.append(pltpu.VMEM(gain.shape, gain.dtype))
    scratch.append(pltpu.SemaphoreType.DMA((2 + PIECES,)))
    return call(
        functools.partial(mix_kernel, part, cols // HD),
        1,
        [me],
        [IN_VMEM, IN_PLACE, IN_PLACE] if part else [IN_PLACE] * 2,
        [attn, in_hbm(signs), in_hbm(gain)] if part else [in_hbm(attn), in_hbm(signs)],
        outs,
        cost(6 * attn.size, 5 * attn.size),
        scratch,
        kinds,
    )


def load_kernel(tbl_ref, w_hbm, out, sem):
    depth, width = out.shape
    count, loads = sem.shape
    step, span = depth // loads, width // count
    copies = []
    for d in range(count):
        cols = pl.ds(pl.multiple_of(tbl_ref[d] * span, span), span)
        for k in range(loads):
            rows = pl.ds(k * step, step)
            to = out.at[rows, pl.ds(d * span, span)]
            copies.append(pltpu.make_async_copy(w_hbm.at[rows, cols], to, sem.at[d, k]))
    for copy in copies:
        copy.start()
    for copy in copies:
        copy.wait()


def load(w, tbl, width, flops=0):
    count = tbl.shape[0]
    return call(
        load_kernel,
        1,
        [tbl],
        [IN_PLACE],
        [in_hbm(w)],
        [((w.shape[0], count * width), w.dtype, IN_VMEM)],
        cost(flops, 0),
        [pltpu.SemaphoreType.DMA((count, LOADS))],
        [pltpu.VMEM],
    )[0]


def combine(order, me, own, recvs, rows):
    v = own[rows, :]
    for bit, recv in zip(order, recvs):
        flip = (1 - 2 * (me >> bit & 1)).astype(jnp.float32)
        v = recv[rows, :].astype(jnp.float32) + flip * v
    return v


def combine_into(out, orders, scale, me, ins):
    per = len(ins) // len(orders)
    size = ins[0].shape[0]
    for c, order in enumerate(orders):
        own, *recvs = ins[c * per : (c + 1) * per]

        @pl.loop(0, size // ROWS, unroll=UNROLL)
        def _(i):
            rows = pl.ds(pl.multiple_of(i * ROWS, ROWS), ROWS)
            to = pl.ds(pl.multiple_of(c * size + i * ROWS, ROWS), ROWS)
            out[to, :] = (combine(order, me, own, recvs, rows) * scale).astype(out.dtype)


def stage_kernel(order, ride, ride_rows, me_ref, *refs):
    riders, ins, out = refs[:ride], refs[ride:-1], refs[-1]
    size = ins[0].shape[0]
    combine_into(out, [order], 1.0, me_ref[0], ins)
    if ride:
        shape = (out.shape[0] - size, out.shape[1])
        row = lax.broadcasted_iota(jnp.int32, shape, 0)
        known = ride_rows
        block = riders[0][size:, :].astype(jnp.float32)
        for rider in riders[1:]:
            more = pltpu.roll(rider[size:, :].astype(jnp.float32), known, 0)
            block = jnp.where(row < known, block, more)
            known *= 2
        out[size:, :] = block.astype(out.dtype)


def stage(block, order, me, riders=(), ride_rows=0):
    flat = [*riders, *block]
    shape = riders[0].shape if riders else block[0].shape
    return call(
        functools.partial(stage_kernel, order, len(riders), ride_rows),
        1,
        [me],
        [whole(f.shape) for f in flat],
        flat,
        [(shape, jnp.bfloat16, whole(shape))],
        cost(4 * block[0].size * len(flat), 2 * block[0].size * (len(flat) + 2)),
    )[0]


def send_lists(order):
    lists = []
    for s, bit in enumerate(order):
        members = [1 << bit]
        for later in reversed(order[s + 1 :]):
            members = members + [m | 1 << later for m in members]
        lists.append(members)
    return lists + [[0]]


def project_kernel(plan, pieces, counts, adds, width, orders, scale, me_ref, *refs):
    raws, rots = refs[: counts[0]], refs[counts[0] : sum(counts)]
    slab, refs = refs[sum(counts)], refs[sum(counts) + 1 :]
    outs = refs[sum(adds) :]
    if raws:
        combine_into(outs[-1], orders, scale, me_ref[0], raws)
        rots = [outs[-1]]
    for step, (out, lead, add, add_lead) in enumerate(plan):
        acc = None
        for rot, (row, depth) in zip(rots, pieces):
            term = jnp.dot(
                rot[...],
                slab[row : row + depth, step * width : (step + 1) * width],
                preferred_element_type=jnp.float32,
            )
            acc = term if acc is None else acc + term
        if add is not None:
            first = sum(adds[:add])
            more = [a[add_lead].astype(jnp.float32) for a in refs[first : first + adds[add]]]
            acc = acc + (more[0] if len(more) == 1 else jnp.concatenate(more, axis=1))
        outs[out][lead] = acc.astype(outs[out].dtype)


def project(
    rots, slab, pieces, spans, width, dtypes, me, adds=(), leads=None, raws=(), orders=(), scale=1.0
):
    plan = [(k, n) for k, (_, count) in enumerate(spans) for n in range(count)]
    if leads is None:
        leads = plan if adds else [(None, None)] * len(plan)
    plan = [(*to, *add) for to, add in zip(plan, leads)]
    flat = [r for raw in raws for r in raw]
    args = [*flat, *rots, slab, *[a for add in adds for a in add]]
    counts = [len(flat), len(rots)]
    rows = rots[0].shape[0] if rots else sum(raw[0].shape[0] for raw in raws)
    shapes = [((n, rows, width), dtype) for (_, n), dtype in zip(spans, dtypes)]
    if raws:
        shapes.append(((rows, flat[0].shape[1]), jnp.bfloat16))
    return call(
        functools.partial(
            project_kernel, plan, pieces, counts, [len(a) for a in adds], width, orders, scale
        ),
        1,
        [me],
        [IN_VMEM] * len(args),
        args,
        [(shape, dtype, whole(shape)) for shape, dtype in shapes],
        cost(PROJECT_FLOPS, 0),
    )


def close_kernel(colors, residual, exps, *refs):
    terms, out = refs[:-1], refs[-1]
    per = len(terms) // colors
    width = residual.shape[1] // colors
    for c in range(colors):
        cols = pl.ds(c * width, width)
        own, *recvs = terms[c * per : (c + 1) * per]
        acc = own[0].astype(jnp.float32)
        for recv in recvs:
            acc = acc + recv[0].astype(jnp.float32)
        acc = acc * jnp.exp2(exps[:, cols].astype(jnp.float32))
        out[c] = (residual[:, cols].astype(jnp.float32) + acc).astype(jnp.bfloat16)


def close(residual, exps, terms, at):
    colors = len(terms)
    _, rows, width = terms[0][0].shape
    span = width * colors
    flat = [t for color in terms for t in color]
    shape = (colors, rows, width)
    return call(
        functools.partial(close_kernel, colors),
        1,
        [],
        [
            pl.BlockSpec((rows, span), lambda i: (0, at)),
            pl.BlockSpec((1, span), lambda i: (0, at)),
        ]
        + [whole((1, rows, width))] * len(flat),
        [residual, exps, *flat],
        [(shape, jnp.bfloat16, whole(shape))],
        cost(10 * rows * span, 2 * rows * width * (len(flat) + 2 * colors)),
    )[0]


def kv_kernel(plan, gain_at, counts, colors, has_prev, channels, at, span, tbl_ref, w, *refs):
    xs, riders, rest = refs[: counts[0]], refs[counts[0] : sum(counts)], refs[sum(counts) :]
    rows, cols = xs[0].shape[-2], w.shape[1]
    product = rest[0][...] if has_prev else jnp.zeros((rows, cols), jnp.float32)
    square = rest[1][...] if has_prev else jnp.zeros((rows, HD), jnp.float32)
    rest = rest[2 * has_prev :]
    for step, blocks in enumerate(plan):
        rider, row = gain_at[step]
        rider = riders[rider]
        for k, lead, c in blocks:
            hidden = xs[k][lead].astype(jnp.float32)
            depth = hidden.shape[1]
            part, col = divmod(at * span + c * depth, rider.shape[1])
            gain = rider[rows // colors :, col : col + depth].astype(jnp.float32)
            gain = gain[row + part : row + part + 1]
            scaled = (hidden * gain).astype(jnp.bfloat16)
            first = pl.multiple_of((tbl_ref[step] + at) * span + c * depth, depth)
            product = product + jnp.dot(
                scaled, w[pl.ds(first, depth), :], preferred_element_type=jnp.float32
            )
            hidden = hidden * hidden
            for b in range(depth // HD):
                square = square + hidden[:, b * HD : (b + 1) * HD]
    if channels:
        exps, out = rest
        mean = jnp.sum(square, axis=1, keepdims=True) / channels
        scale = jnp.exp2(exps[...].astype(jnp.float32))
        out[...] = (product * lax.rsqrt(mean + EPS) * scale).astype(out.dtype)
    else:
        rest[0][...], rest[1][...] = product, square


def kv_step(plan, arrays, riders, gain_at, colors, w_kv, tbl, at, span, prev, exps, channels):
    used = sorted({k for blocks in plan for k, _, _ in blocks})
    xs = [arrays[k] for k in used]
    plan = [[(used.index(k), lead, c) for k, lead, c in blocks] for blocks in plan]
    rows = xs[0].shape[1]
    cols = w_kv.shape[1]
    extra = list(prev or ())
    if channels:
        extra.append(exps)
        outs = [((rows, cols), jnp.bfloat16)]
    else:
        outs = [((rows, cols), jnp.float32), ((rows, HD), jnp.float32)]
    args = [w_kv, *xs, *riders, *extra]
    counts = [len(xs), len(riders)]
    return call(
        functools.partial(
            kv_kernel, plan, gain_at, counts, colors, prev is not None, channels, at, span
        ),
        1,
        [tbl],
        [IN_VMEM] * len(args),
        args,
        [(shape, dtype, whole(shape)) for shape, dtype in outs],
        cost(
            2 * rows * span * cols * len(plan), 2 * span * (rows + cols) * len(plan) + 4 * rows * cols
        ),
    )


def gather(x, orders, count):
    colors = x.shape[0]
    arrays, where = [x], {0: [(0, c) for c in range(colors)]}
    levels = len(orders[0])
    for bit in range(levels):
        arrays.append(swap(x, bit, count))
        where[1 << bit] = [(len(arrays) - 1, c) for c in range(colors)]
    for size in range(2, levels + 1):
        for r in range(count):
            if r.bit_count() == size:
                where[r] = []
                for c, order in enumerate(orders):
                    hop = max((b for b in range(levels) if r >> b & 1), key=order.index)
                    k, at = where[r ^ 1 << hop][c]
                    arrays.append(swap(arrays[k][at : at + 1], hop, count))
                    where[r].append((len(arrays) - 1, 0))
    plan = [[(k, at, c) for c, (k, at) in enumerate(blocks)] for blocks in where.values()]
    return arrays, list(zip(where, plan))


def body(attn_out, head_signs, w_out, out_exp, residual, norm_gain, w_kv, kv_exp):
    count = lax.axis_size("tensor")
    levels = count.bit_length() - 1
    me = lax.axis_index("tensor").astype(jnp.int32)
    odd = lax.axis_index("dp") % 2 == 1
    me_arr = me.reshape(1)
    by = levels // 2
    unturned = (me >> by | me << levels - by) & count - 1
    logical = jnp.where(odd, unturned, me).reshape(1)
    depth, local = w_out.shape[0], residual.shape[1]
    channels = local * count
    orders = [list(range(levels))]
    orders.append(orders[0][levels // 2 :] + orders[0][: levels // 2])
    colors = len(orders)
    half = local // HALVES
    wide = half // colors

    def devices(rel):
        far = jnp.array([turned(r, levels) for r in rel], jnp.int32)
        return me ^ jnp.where(odd, far, jnp.array(rel, jnp.int32))

    lists = [send_lists(order) for order in orders]

    def blocks_of(stages, v):
        spans, rel, color = [], [], []
        for s in stages:
            for c in range(colors):
                spans.append((len(rel), len(lists[c][s])))
                rel += lists[c][s]
                color += [v * colors + c] * len(lists[c][s])
        return devices(rel) * (local // wide) + jnp.array(color, jnp.int32), spans

    later = range(1, levels + 1)
    first_tbls = [blocks_of([0], v)[0] for v in range(HALVES)]
    rest_tbls = [blocks_of(later, v)[0] for v in range(HALVES)]
    first_spans, rest_spans = blocks_of([0], 0)[1], blocks_of(later, 0)[1]

    exps = out_exp.reshape(1, -1)
    kv_exps = kv_exp.reshape(1, -1)

    blocks, riders = [], []
    attn = attn_out
    for p in range(len(QUARTERS)):
        mixed = mix(attn, me_arr, head_signs, norm_gain, p, colors, count)
        if p == 0:
            attn = mixed[-1]
        blocks.append([])
        for c, order in enumerate(orders):
            own, sent = mixed[2 * c : 2 * c + 2]
            blocks[p].append([own, swap(sent, order[0], count)])
            if p == 1 and c == 0:
                riders += [sent, blocks[p][c][1]]
    ride_rows = local // riders[0].shape[1]
    slabs = [load(w_out, after(first_tbls[0], sent), wide)]
    here = after(logical, slabs[0])
    for s in range(1, levels):
        sends = []
        for p in range(len(QUARTERS)):
            for c, order in enumerate(orders):
                ride = p == 1 and c == 0
                send = stage(blocks[p][c], order, here, riders if ride else (), ride_rows)
                blocks[p][c].append(swap(send, order[s], count))
                sends.append(send)
                if ride:
                    riders.append(blocks[p][c][-1])
            here = after(logical, *sends)
    slabs.append(load(w_out, after(first_tbls[1], *sends), wide, BUSY))

    gain_at, known = {0: (0, 0)}, [0]
    for t, bit in enumerate(orders[0]):
        gain_at.update({r ^ 1 << bit: (t + 1, ride_rows * k) for k, r in enumerate(known)})
        known += [r ^ 1 << bit for r in known]

    bf16, f32 = jnp.bfloat16, jnp.float32
    cut = blocks[0][0][0].shape[1]
    pieces = [(0, cut), (cut, depth - cut)]
    scale = head_signs.shape[0] ** -0.5
    *prevs, rot = project(
        [], slabs[0], pieces[:1], first_spans, wide, [f32] * colors, after(logical, slabs[1]),
        raws=blocks[0], orders=orders, scale=scale,
    )
    rots = [rot]
    *sends, rot = project(
        [], slabs[0], pieces[1:], first_spans, wide, [bf16] * colors, logical,
        [[p] for p in prevs], raws=blocks[1], orders=orders, scale=scale,
    )
    rots.append(rot)
    received = []
    for v in range(HALVES):
        if v:
            sends = project(
                rots, slabs[v], pieces, first_spans, wide, [bf16] * colors, logical
            )
        received.append([swap(send, order[0], count) for send, order in zip(sends, orders)])

    leads = []
    for s in later:
        for c in range(colors):
            n = len(lists[c][s])
            leads += [(c, k + n * (s < levels)) for k in range(n)]
    dtypes = [bf16 if s == 1 and levels > 1 else f32 for s in later for _ in range(colors)]

    resids, found = [], []
    for v in range(HALVES):
        adds = [[r] for r in received[v]]
        slab = load(w_out, after(rest_tbls[v], *sends), wide)
        parts = project(
            rots, slab, pieces, rest_spans, wide, dtypes, logical, adds, leads
        )
        sends = parts[:colors]
        terms = []
        for c, order in enumerate(orders):
            recvs = []
            for s in range(1, levels):
                send = parts[(s - 1) * colors + c]
                if recvs:
                    size = send.shape[0]
                    for recv in recvs:
                        send = send + recv[size : 2 * size].astype(f32)
                    send = send.astype(bf16)
                recvs.append(swap(send, order[s], count))
            terms.append([parts[(levels - 1) * colors + c], *recvs])
        out = close(residual, exps, terms, v)
        resids += list(out)
        found.append(gather(out, orders, count))

    runs = []
    for far in (False, True):
        for v, (arrays, blocks) in enumerate(found):
            run = [b for b in blocks if (b[0].bit_count() > 1) == far]
            if run:
                runs.append((v, arrays, run))
    running = None
    for k, (v, arrays, run) in enumerate(runs):
        running = kv_step(
            [plan for _, plan in run],
            arrays,
            riders,
            [gain_at[r] for r, _ in run],
            colors,
            w_kv,
            devices([r for r, _ in run]) * HALVES,
            v,
            half,
            running,
            kv_exps,
            channels * (k == len(runs) - 1),
        )
    return jnp.concatenate(resids, axis=1), running[0]


def solution(mesh):
    placed = (
        P("dp", "tensor"),
        P(),
        P("tensor", None),
        P("tensor"),
        P("dp", "tensor"),
        P("tensor"),
        P(None, "tensor"),
        P("tensor"),
    )
    return jax.shard_map(
        body,
        mesh=mesh,
        in_specs=placed,
        out_specs=(P("dp", "tensor"), P("dp", "tensor")),
        check_vma=False,
    )
```

```python
import functools

import jax
import jax.numpy as jnp
from jax import lax
from jax.experimental import pallas as pl
from jax.experimental.pallas import tpu as pltpu
from jax.sharding import PartitionSpec as P

HD = 128
EPS = 1e-05
QUARTERS = ((0, 1), (2, 3))
RIDE = 0
HALVES = 2
PIECES = 4
LOADS = 4
ROWS = 16
UNROLL = 4
VMEM = 4 * 1024 * 1024
PROJECT_FLOPS = 1e6
BUSY = 4e9


def cost(flops, nbytes):
    return pl.CostEstimate(flops=int(flops), bytes_accessed=int(nbytes), transcendentals=0)


def call(kernel, grid, scalars, in_specs, args, outs, estimate, scratch=(), kinds=None):
    kinds = kinds or [jax.ShapeDtypeStruct] * len(outs)
    return pl.pallas_call(
        kernel,
        grid_spec=pltpu.PrefetchScalarGridSpec(
            num_scalar_prefetch=len(scalars),
            grid=(grid,),
            in_specs=in_specs,
            out_specs=[spec for _, _, spec in outs],
            scratch_shapes=list(scratch),
        ),
        out_shape=[kind(shape, dtype) for (shape, dtype, _), kind in zip(outs, kinds)],
        compiler_params=pltpu.CompilerParams(vmem_limit_bytes=VMEM),
        cost_estimate=estimate,
    )(*scalars, *args)


def whole(shape):
    return pl.BlockSpec(shape, lambda *_: (0,) * len(shape))


IN_PLACE = pl.BlockSpec(memory_space=pl.ANY)
IN_VMEM = pl.BlockSpec(memory_space=pltpu.VMEM)


def in_hbm(array):
    return pltpu.with_memory_space_constraint(array, pltpu.HBM)


def after(value, *others):
    return lax.optimization_barrier((value, *others))[0]


def turned(bits, levels):
    by = levels // 2
    return (bits << by | bits >> levels - by) & (1 << levels) - 1


def swap(block, bit, count):
    levels = count.bit_length() - 1
    masks = (1 << bit, turned(1 << bit, levels))
    route = [
        (d * count + i, d * count + (i ^ masks[d % 2]))
        for d in range(lax.axis_size("dp"))
        for i in range(count)
    ]
    return lax.ppermute(block, ("dp", "tensor"), route)


def mix_rows(part, heads, c, i, signs, attn, full, sent):
    quarter = heads // 4
    at = pl.ds(pl.multiple_of(c * full.shape[0] + i * ROWS, ROWS), ROWS)
    rows = pl.ds(pl.multiple_of(i * ROWS, ROWS), ROWS)

    def head(h):
        return attn[at, pl.ds(h * HD, HD)].astype(jnp.float32) * signs[h]

    mixed = [[] for _ in QUARTERS[part]]
    for h in range(quarter):
        a, b, c2, d = [head(q * quarter + h) for q in range(4)]
        upper, lower = (a + c2, b + d), (a - c2, b - d)
        for k, q in enumerate(QUARTERS[part]):
            one, two = lower if q & 2 else upper
            mixed[k].append(one - two if q & 1 else one + two)
    for k, v in enumerate(mixed):
        step = 1
        while step < quarter:
            for lo in range(quarter):
                if not lo & step:
                    a, b = v[lo], v[lo | step]
                    v[lo], v[lo | step] = a + b, a - b
            step *= 2
        for h in range(quarter):
            cols = pl.ds((k * quarter + h) * HD, HD)
            full[rows, cols] = v[h]
            sent[rows, cols] = v[h].astype(sent.dtype)


def mix_kernel(part, heads, me_ref, *refs):
    ride = part == RIDE
    attn, signs_ref, *refs = refs
    gain_hbm, *refs = refs if ride else (None, *refs)
    *outs, sem = refs
    gain, outs = (outs[-1], outs[:-1]) if ride else (None, outs)
    signs_mem, outs = outs[-1], outs[:-1]
    me = me_ref[0]
    get_signs = pltpu.make_async_copy(signs_ref, signs_mem, sem.at[0])
    get_signs.start()
    size = outs[0].shape[0]
    step = attn.shape[0] // PIECES
    pieces = []
    if part == 0:
        attn_hbm, attn, outs = attn, outs[-1], outs[:-1]
        for k in range(PIECES):
            rows = pl.ds(k * step, step)
            pieces.append(
                pltpu.make_async_copy(attn_hbm.at[rows, :], attn.at[rows, :], sem.at[2 + k])
            )
            pieces[k].start()
    if ride:
        get_gain = pltpu.make_async_copy(gain_hbm, gain, sem.at[1])
        get_gain.start()
        get_gain.wait()
        sent = outs[1]
        shape = (sent.shape[0] - size, sent.shape[1])
        row = lax.broadcasted_iota(jnp.int32, shape, 0)
        block = jnp.zeros(shape, jnp.float32)
        for k in range(gain.shape[0] // shape[1]):
            piece = gain[pl.ds(k * shape[1], shape[1])].astype(jnp.float32)
            block = jnp.where(row == k, jnp.broadcast_to(piece[None, :], shape), block)
        sent[size:, :] = block.astype(sent.dtype)
    get_signs.wait()
    signs = [
        jnp.full((ROWS, HD), 2 * signs_mem[me * heads + h] - 1, jnp.int32).astype(jnp.float32)
        for h in range(heads)
    ]
    for k in range(PIECES):
        if pieces:
            pieces[k].wait()
        c, first = k * step // size, k * step % size // ROWS
        full, sent = outs[2 * c : 2 * c + 2]

        @pl.loop(first, first + step // ROWS, unroll=UNROLL)
        def _(i):
            mix_rows(part, heads, c, i, signs, attn, full, sent)


def mix(attn, me, signs, gain, part, colors, count):
    rows, cols = attn.shape
    shape = (rows // colors, cols // 4 * len(QUARTERS[part]))
    riding = part == RIDE
    ride = -(-count // 2 * (gain.shape[0] // shape[1]) // ROWS) * ROWS
    outs = []
    for c in range(colors):
        sent = (shape[0] + ride * (riding and c == 0), shape[1])
        outs += [(shape, jnp.float32, whole(shape)), (sent, jnp.bfloat16, whole(sent))]
    kinds = [jax.ShapeDtypeStruct] * len(outs)
    specs, args = [IN_VMEM if part else IN_PLACE, IN_PLACE], [attn if part else in_hbm(attn), in_hbm(signs)]
    scratch = [pltpu.SMEM(signs.shape, signs.dtype)]
    if part == 0:
        outs.append((attn.shape, attn.dtype, IN_VMEM))
        kinds.append(pltpu.VMEM)
    if riding:
        specs.append(IN_PLACE)
        args.append(in_hbm(gain))
        scratch.append(pltpu.VMEM(gain.shape, gain.dtype))
    scratch.append(pltpu.SemaphoreType.DMA((2 + PIECES,)))
    return call(
        functools.partial(mix_kernel, part, cols // HD),
        1,
        [me],
        specs,
        args,
        outs,
        cost(6 * attn.size, 5 * attn.size),
        scratch,
        kinds,
    )


def load_kernel(tbl_ref, w_hbm, out, sem):
    depth, width = out.shape
    count, loads = sem.shape
    step, span = depth // loads, width // count
    copies = []
    for d in range(count):
        cols = pl.ds(pl.multiple_of(tbl_ref[d] * span, span), span)
        for k in range(loads):
            rows = pl.ds(k * step, step)
            to = out.at[rows, pl.ds(d * span, span)]
            copies.append(pltpu.make_async_copy(w_hbm.at[rows, cols], to, sem.at[d, k]))
    for copy in copies:
        copy.start()
    for copy in copies:
        copy.wait()


def load(w, tbl, width, flops=0):
    count = tbl.shape[0]
    return call(
        load_kernel,
        1,
        [tbl],
        [IN_PLACE],
        [in_hbm(w)],
        [((w.shape[0], count * width), w.dtype, IN_VMEM)],
        cost(flops, 0),
        [pltpu.SemaphoreType.DMA((count, LOADS))],
        [pltpu.VMEM],
    )[0]


def combine(order, me, own, recvs, rows):
    v = own[rows, :]
    for bit, recv in zip(order, recvs):
        flip = (1 - 2 * (me >> bit & 1)).astype(jnp.float32)
        v = recv[rows, :].astype(jnp.float32) + flip * v
    return v


def combine_into(out, orders, scale, me, ins):
    per = len(ins) // len(orders)
    size = ins[0].shape[0]
    for c, order in enumerate(orders):
        own, *recvs = ins[c * per : (c + 1) * per]

        @pl.loop(0, size // ROWS, unroll=UNROLL)
        def _(i):
            rows = pl.ds(pl.multiple_of(i * ROWS, ROWS), ROWS)
            to = pl.ds(pl.multiple_of(c * size + i * ROWS, ROWS), ROWS)
            out[to, :] = (combine(order, me, own, recvs, rows) * scale).astype(out.dtype)


def stage_kernel(order, ride, ride_rows, me_ref, *refs):
    riders, ins, out = refs[:ride], refs[ride:-1], refs[-1]
    size = ins[0].shape[0]
    combine_into(out, [order], 1.0, me_ref[0], ins)
    if ride:
        shape = (out.shape[0] - size, out.shape[1])
        row = lax.broadcasted_iota(jnp.int32, shape, 0)
        known = ride_rows
        block = riders[0][size:, :].astype(jnp.float32)
        for rider in riders[1:]:
            more = pltpu.roll(rider[size:, :].astype(jnp.float32), known, 0)
            block = jnp.where(row < known, block, more)
            known *= 2
        out[size:, :] = block.astype(out.dtype)


def stage(block, order, me, riders=(), ride_rows=0):
    flat = [*riders, *block]
    shape = riders[0].shape if riders else block[0].shape
    return call(
        functools.partial(stage_kernel, order, len(riders), ride_rows),
        1,
        [me],
        [whole(f.shape) for f in flat],
        flat,
        [(shape, jnp.bfloat16, whole(shape))],
        cost(4 * block[0].size * len(flat), 2 * block[0].size * (len(flat) + 2)),
    )[0]


def send_lists(order):
    lists = []
    for s, bit in enumerate(order):
        members = [1 << bit]
        for later in reversed(order[s + 1 :]):
            members = members + [m | 1 << later for m in members]
        lists.append(members)
    return lists + [[0]]


def project_kernel(plan, pieces, counts, adds, width, orders, scale, me_ref, *refs):
    added, refs = refs[: sum(adds)], refs[sum(adds) :]
    raws, rots = refs[: counts[0]], refs[counts[0] : sum(counts)]
    slab, outs = refs[sum(counts)], refs[sum(counts) + 1 :]
    if raws:
        combine_into(outs[-1], orders, scale, me_ref[0], raws)
        rots = [outs[-1]]
    for step, (out, lead, add, add_lead) in enumerate(plan):
        acc = None
        for rot, (row, depth) in zip(rots, pieces):
            term = jnp.dot(
                rot[...],
                slab[row : row + depth, step * width : (step + 1) * width],
                preferred_element_type=jnp.float32,
            )
            acc = term if acc is None else acc + term
        if add is not None:
            first = sum(adds[:add])
            more = [a[add_lead].astype(jnp.float32) for a in added[first : first + adds[add]]]
            acc = acc + (more[0] if len(more) == 1 else jnp.concatenate(more, axis=1))
        outs[out][lead] = acc.astype(outs[out].dtype)


def project(
    rots, slab, pieces, spans, width, dtypes, me, adds=(), leads=None, raws=(), orders=(), scale=1.0
):
    plan = [(k, n) for k, (_, count) in enumerate(spans) for n in range(count)]
    if leads is None:
        leads = plan if adds else [(None, None)] * len(plan)
    plan = [(*to, *add) for to, add in zip(plan, leads)]
    flat = [r for raw in raws for r in raw]
    args = [*[a for add in adds for a in add], *flat, *rots, slab]
    counts = [len(flat), len(rots)]
    rows = rots[0].shape[0] if rots else sum(raw[0].shape[0] for raw in raws)
    shapes = [((n, rows, width), dtype) for (_, n), dtype in zip(spans, dtypes)]
    if raws:
        shapes.append(((rows, flat[0].shape[1]), jnp.bfloat16))
    return call(
        functools.partial(
            project_kernel, plan, pieces, counts, [len(a) for a in adds], width, orders, scale
        ),
        1,
        [me],
        [IN_VMEM] * len(args),
        args,
        [(shape, dtype, whole(shape)) for shape, dtype in shapes],
        cost(PROJECT_FLOPS, 0),
    )


def close_kernel(colors, residual, exps, *refs):
    terms, out = refs[:-1], refs[-1]
    per = len(terms) // colors
    width = residual.shape[1] // colors
    for c in range(colors):
        cols = pl.ds(c * width, width)
        own, *recvs = terms[c * per : (c + 1) * per]
        acc = own[0].astype(jnp.float32)
        for recv in recvs:
            acc = acc + recv[0].astype(jnp.float32)
        acc = acc * jnp.exp2(exps[:, cols].astype(jnp.float32))
        out[c] = (residual[:, cols].astype(jnp.float32) + acc).astype(jnp.bfloat16)


def close(residual, exps, terms, at):
    colors = len(terms)
    _, rows, width = terms[0][0].shape
    span = width * colors
    flat = [t for color in terms for t in color]
    shape = (colors, rows, width)
    return call(
        functools.partial(close_kernel, colors),
        1,
        [],
        [
            pl.BlockSpec((rows, span), lambda i: (0, at)),
            pl.BlockSpec((1, span), lambda i: (0, at)),
        ]
        + [whole((1, rows, width))] * len(flat),
        [residual, exps, *flat],
        [(shape, jnp.bfloat16, whole(shape))],
        cost(10 * rows * span, 2 * rows * width * (len(flat) + 2 * colors)),
    )[0]


def kv_kernel(plan, gain_at, counts, colors, has_prev, channels, at, span, tbl_ref, *refs):
    prevs, w, refs = refs[: 2 * has_prev], refs[2 * has_prev], refs[2 * has_prev + 1 :]
    xs, riders, rest = refs[: counts[0]], refs[counts[0] : sum(counts)], refs[sum(counts) :]
    rows, cols = xs[0].shape[-2], w.shape[1]
    product = prevs[0][...] if has_prev else jnp.zeros((rows, cols), jnp.float32)
    square = prevs[1][...] if has_prev else jnp.zeros((rows, HD), jnp.float32)
    for step, blocks in enumerate(plan):
        rider, row = gain_at[step]
        rider = riders[rider]
        for k, lead, c in blocks:
            hidden = xs[k][lead].astype(jnp.float32)
            depth = hidden.shape[1]
            part, col = divmod(at * span + c * depth, rider.shape[1])
            gain = rider[rows // colors :, col : col + depth].astype(jnp.float32)
            gain = gain[row + part : row + part + 1]
            scaled = (hidden * gain).astype(jnp.bfloat16)
            first = pl.multiple_of((tbl_ref[step] + at) * span + c * depth, depth)
            product = product + jnp.dot(
                scaled, w[pl.ds(first, depth), :], preferred_element_type=jnp.float32
            )
            hidden = hidden * hidden
            for b in range(depth // HD):
                square = square + hidden[:, b * HD : (b + 1) * HD]
    if channels:
        exps, out = rest
        mean = jnp.sum(square, axis=1, keepdims=True) / channels
        scale = jnp.exp2(exps[...].astype(jnp.float32))
        out[...] = (product * lax.rsqrt(mean + EPS) * scale).astype(out.dtype)
    else:
        rest[0][...], rest[1][...] = product, square


def kv_step(plan, arrays, riders, gain_at, colors, w_kv, tbl, at, span, prev, exps, channels):
    used = sorted({k for blocks in plan for k, _, _ in blocks})
    xs = [arrays[k] for k in used]
    plan = [[(used.index(k), lead, c) for k, lead, c in blocks] for blocks in plan]
    rows = xs[0].shape[1]
    cols = w_kv.shape[1]
    extra = []
    if channels:
        extra.append(exps)
        outs = [((rows, cols), jnp.bfloat16)]
    else:
        outs = [((rows, cols), jnp.float32), ((rows, HD), jnp.float32)]
    args = [*(prev or ()), w_kv, *xs, *riders, *extra]
    counts = [len(xs), len(riders)]
    return call(
        functools.partial(
            kv_kernel, plan, gain_at, counts, colors, prev is not None, channels, at, span
        ),
        1,
        [tbl],
        [IN_VMEM] * len(args),
        args,
        [(shape, dtype, whole(shape)) for shape, dtype in outs],
        cost(
            2 * rows * span * cols * len(plan), 2 * span * (rows + cols) * len(plan) + 4 * rows * cols
        ),
    )


def gather(x, orders, count):
    colors = x.shape[0]
    arrays, where = [x], {0: [(0, c) for c in range(colors)]}
    levels = len(orders[0])
    for bit in range(levels):
        arrays.append(swap(x, bit, count))
        where[1 << bit] = [(len(arrays) - 1, c) for c in range(colors)]
    for size in range(2, levels + 1):
        for r in range(count):
            if r.bit_count() == size:
                where[r] = []
                for c, order in enumerate(orders):
                    hop = max((b for b in range(levels) if r >> b & 1), key=order.index)
                    k, at = where[r ^ 1 << hop][c]
                    arrays.append(swap(arrays[k][at : at + 1], hop, count))
                    where[r].append((len(arrays) - 1, 0))
    plan = [[(k, at, c) for c, (k, at) in enumerate(blocks)] for blocks in where.values()]
    return arrays, list(zip(where, plan))


def body(attn_out, head_signs, w_out, out_exp, residual, norm_gain, w_kv, kv_exp):
    count = lax.axis_size("tensor")
    levels = count.bit_length() - 1
    me = lax.axis_index("tensor").astype(jnp.int32)
    odd = lax.axis_index("dp") % 2 == 1
    me_arr = me.reshape(1)
    by = levels // 2
    unturned = (me >> by | me << levels - by) & count - 1
    logical = jnp.where(odd, unturned, me).reshape(1)
    depth, local = w_out.shape[0], residual.shape[1]
    channels = local * count
    orders = [list(range(levels))]
    orders.append(orders[0][levels // 2 :] + orders[0][: levels // 2])
    colors = len(orders)
    half = local // HALVES
    wide = half // colors

    def devices(rel):
        far = jnp.array([turned(r, levels) for r in rel], jnp.int32)
        return me ^ jnp.where(odd, far, jnp.array(rel, jnp.int32))

    lists = [send_lists(order) for order in orders]

    def blocks_of(stages, v):
        spans, rel, color = [], [], []
        for s in stages:
            for c in range(colors):
                spans.append((len(rel), len(lists[c][s])))
                rel += lists[c][s]
                color += [v * colors + c] * len(lists[c][s])
        return devices(rel) * (local // wide) + jnp.array(color, jnp.int32), spans

    later = range(1, levels + 1)
    first_tbls = [blocks_of([0], v)[0] for v in range(HALVES)]
    rest_tbls = [blocks_of(later, v)[0] for v in range(HALVES)]
    first_spans, rest_spans = blocks_of([0], 0)[1], blocks_of(later, 0)[1]

    exps = out_exp.reshape(1, -1)
    kv_exps = kv_exp.reshape(1, -1)

    blocks, riders = [], []
    attn = attn_out
    for p in range(len(QUARTERS)):
        mixed = mix(attn, me_arr, head_signs, norm_gain, p, colors, count)
        if p == 0:
            attn = mixed[-1]
        blocks.append([])
        for c, order in enumerate(orders):
            own, sent = mixed[2 * c : 2 * c + 2]
            blocks[p].append([own, swap(sent, order[0], count)])
            if p == RIDE and c == 0:
                riders += [sent, blocks[p][c][1]]
    ride_rows = local // riders[0].shape[1]
    slabs = [load(w_out, after(first_tbls[0], sent), wide)]
    here = after(logical, slabs[0])
    for s in range(1, levels):
        sends = []
        for p in range(len(QUARTERS)):
            for c, order in enumerate(orders):
                ride = p == RIDE and c == 0
                send = stage(blocks[p][c], order, here, riders if ride else (), ride_rows)
                blocks[p][c].append(swap(send, order[s], count))
                sends.append(send)
                if ride:
                    riders.append(blocks[p][c][-1])
            here = after(logical, *sends)
    slabs.append(load(w_out, after(first_tbls[1], *sends), wide, BUSY))

    gain_at, known = {0: (0, 0)}, [0]
    for t, bit in enumerate(orders[0]):
        gain_at.update({r ^ 1 << bit: (t + 1, ride_rows * k) for k, r in enumerate(known)})
        known += [r ^ 1 << bit for r in known]

    bf16, f32 = jnp.bfloat16, jnp.float32
    cut = blocks[0][0][0].shape[1]
    pieces = [(0, cut), (cut, depth - cut)]
    scale = head_signs.shape[0] ** -0.5
    *prevs, rot = project(
        [], slabs[0], pieces[:1], first_spans, wide, [f32] * colors, after(logical, slabs[1]),
        raws=blocks[0], orders=orders, scale=scale,
    )
    rots = [rot]
    *sends, rot = project(
        [], slabs[0], pieces[1:], first_spans, wide, [bf16] * colors, logical,
        [[p] for p in prevs], raws=blocks[1], orders=orders, scale=scale,
    )
    rots.append(rot)
    received = []
    for v in range(HALVES):
        if v:
            sends = project(
                rots, slabs[v], pieces, first_spans, wide, [bf16] * colors, logical
            )
        received.append([swap(send, order[0], count) for send, order in zip(sends, orders)])

    leads = []
    for s in later:
        for c in range(colors):
            n = len(lists[c][s])
            leads += [(c, k + n * (s < levels)) for k in range(n)]
    dtypes = [bf16 if s == 1 and levels > 1 else f32 for s in later for _ in range(colors)]

    def keys_and_values(run, running, last):
        v, arrays, run = run
        return kv_step(
            [plan for _, plan in run],
            arrays,
            riders,
            [gain_at[r] for r, _ in run],
            colors,
            w_kv,
            devices([r for r, _ in run]) * HALVES,
            v,
            half,
            running,
            kv_exps,
            channels * last,
        )

    resids, runs, running = [], [], None
    for v in range(HALVES):
        adds = [[r] for r in received[v]]
        slab = load(w_out, after(rest_tbls[v], *sends), wide)
        parts = project(
            rots, slab, pieces, rest_spans, wide, dtypes, logical, adds, leads
        )
        sends = parts[:colors]
        terms = []
        for c, order in enumerate(orders):
            recvs = []
            for s in range(1, levels):
                send = parts[(s - 1) * colors + c]
                if recvs:
                    size = send.shape[0]
                    for recv in recvs:
                        send = send + recv[size : 2 * size].astype(f32)
                    send = send.astype(bf16)
                recvs.append(swap(send, order[s], count))
            terms.append([parts[(levels - 1) * colors + c], *recvs])
        out = close(residual, exps, terms, v)
        resids += list(out)
        arrays, found = gather(out, orders, count)
        for far in (False, True):
            run = [b for b in found if (b[0].bit_count() > 1) == far]
            split = far and v == HALVES - 1
            for wanted in ([c] for c in range(colors)) if split else (range(colors),):
                part = [(r, [b for b in plan if b[2] in wanted]) for r, plan in run]
                if run and not far:
                    running = keys_and_values((v, arrays, part), running, False)
                elif run:
                    runs.append((v, arrays, part))

    for k, run in enumerate(runs):
        running = keys_and_values(run, running, k == len(runs) - 1)
    return jnp.concatenate(resids, axis=1), running[0]


def solution(mesh):
    placed = (
        P("dp", "tensor"),
        P(),
        P("tensor", None),
        P("tensor"),
        P("dp", "tensor"),
        P("tensor"),
        P(None, "tensor"),
        P("tensor"),
    )
    return jax.shard_map(
        body,
        mesh=mesh,
        in_specs=placed,
        out_specs=(P("dp", "tensor"), P("dp", "tensor")),
        check_vma=False,
    )
```

```python
import functools

import jax
import jax.numpy as jnp
from jax import lax
from jax.experimental import pallas as pl
from jax.experimental.pallas import tpu as pltpu
from jax.sharding import PartitionSpec as P

HD = 128
EPS = 1e-05
QUARTERS = ((0, 1), (2, 3))
RIDE = 0
HALVES = 2
PIECES = 4
LOADS = 4
ROWS = 16
UNROLL = 2
VMEM = 4 * 1024 * 1024
PROJECT_FLOPS = 1e6
BUSY = 4e9


def cost(flops, nbytes):
    return pl.CostEstimate(flops=int(flops), bytes_accessed=int(nbytes), transcendentals=0)


def call(kernel, grid, scalars, in_specs, args, outs, estimate, scratch=(), kinds=None):
    kinds = kinds or [jax.ShapeDtypeStruct] * len(outs)
    return pl.pallas_call(
        kernel,
        grid_spec=pltpu.PrefetchScalarGridSpec(
            num_scalar_prefetch=len(scalars),
            grid=(grid,),
            in_specs=in_specs,
            out_specs=[spec for _, _, spec in outs],
            scratch_shapes=list(scratch),
        ),
        out_shape=[kind(shape, dtype) for (shape, dtype, _), kind in zip(outs, kinds)],
        compiler_params=pltpu.CompilerParams(vmem_limit_bytes=VMEM),
        cost_estimate=estimate,
    )(*scalars, *args)


def whole(shape):
    return pl.BlockSpec(shape, lambda *_: (0,) * len(shape))


IN_PLACE = pl.BlockSpec(memory_space=pl.ANY)
IN_VMEM = pl.BlockSpec(memory_space=pltpu.VMEM)


def in_hbm(array):
    return pltpu.with_memory_space_constraint(array, pltpu.HBM)


def after(value, *others):
    return lax.optimization_barrier((value, *others))[0]


def turned(bits, levels):
    by = levels // 2
    return (bits << by | bits >> levels - by) & (1 << levels) - 1


def swap(block, bit, count):
    levels = count.bit_length() - 1
    masks = (1 << bit, turned(1 << bit, levels))
    route = [
        (d * count + i, d * count + (i ^ masks[d % 2]))
        for d in range(lax.axis_size("dp"))
        for i in range(count)
    ]
    return lax.ppermute(block, ("dp", "tensor"), route)


def mix_rows(part, heads, c, i, signs, attn, full, sent):
    quarter = heads // 4
    at = pl.ds(pl.multiple_of(c * full.shape[0] + i * ROWS, ROWS), ROWS)
    rows = pl.ds(pl.multiple_of(i * ROWS, ROWS), ROWS)

    def head(h):
        return attn[at, pl.ds(h * HD, HD)].astype(jnp.float32) * signs[h]

    mixed = [[] for _ in QUARTERS[part]]
    for h in range(quarter):
        a, b, c2, d = [head(q * quarter + h) for q in range(4)]
        upper, lower = (a + c2, b + d), (a - c2, b - d)
        for k, q in enumerate(QUARTERS[part]):
            one, two = lower if q & 2 else upper
            mixed[k].append(one - two if q & 1 else one + two)
    for k, v in enumerate(mixed):
        step = 1
        while step < quarter:
            for lo in range(quarter):
                if not lo & step:
                    a, b = v[lo], v[lo | step]
                    v[lo], v[lo | step] = a + b, a - b
            step *= 2
        for h in range(quarter):
            cols = pl.ds((k * quarter + h) * HD, HD)
            full[rows, cols] = v[h]
            sent[rows, cols] = v[h].astype(sent.dtype)


def mix_kernel(part, heads, me_ref, *refs):
    ride = part == RIDE
    attn, signs_ref, *refs = refs
    gain_hbm, *refs = refs if ride else (None, *refs)
    *outs, sem = refs
    gain, outs = (outs[-1], outs[:-1]) if ride else (None, outs)
    signs_mem, outs = outs[-1], outs[:-1]
    me = me_ref[0]
    get_signs = pltpu.make_async_copy(signs_ref, signs_mem, sem.at[0])
    get_signs.start()
    size = outs[0].shape[0]
    step = attn.shape[0] // PIECES
    pieces = []
    if part == 0:
        attn_hbm, attn, outs = attn, outs[-1], outs[:-1]
        for k in range(PIECES):
            rows = pl.ds(k * step, step)
            pieces.append(
                pltpu.make_async_copy(attn_hbm.at[rows, :], attn.at[rows, :], sem.at[2 + k])
            )
            pieces[k].start()
    if ride:
        get_gain = pltpu.make_async_copy(gain_hbm, gain, sem.at[1])
        get_gain.start()
        get_gain.wait()
        sent = outs[1]
        shape = (sent.shape[0] - size, sent.shape[1])
        row = lax.broadcasted_iota(jnp.int32, shape, 0)
        block = jnp.zeros(shape, jnp.float32)
        for k in range(gain.shape[0] // shape[1]):
            piece = gain[pl.ds(k * shape[1], shape[1])].astype(jnp.float32)
            block = jnp.where(row == k, jnp.broadcast_to(piece[None, :], shape), block)
        sent[size:, :] = block.astype(sent.dtype)
    get_signs.wait()
    signs = [(2 * signs_mem[me * heads + h] - 1).astype(jnp.float32) for h in range(heads)]
    for k in range(PIECES):
        if pieces:
            pieces[k].wait()
        c, first = k * step // size, k * step % size // ROWS
        full, sent = outs[2 * c : 2 * c + 2]

        @pl.loop(first, first + step // ROWS, unroll=UNROLL)
        def _(i):
            mix_rows(part, heads, c, i, signs, attn, full, sent)


def mix(attn, me, signs, gain, part, colors, count):
    rows, cols = attn.shape
    shape = (rows // colors, cols // 4 * len(QUARTERS[part]))
    riding = part == RIDE
    ride = -(-count // 2 * (gain.shape[0] // shape[1]) // ROWS) * ROWS
    outs = []
    for c in range(colors):
        sent = (shape[0] + ride * (riding and c == 0), shape[1])
        outs += [(shape, jnp.float32, whole(shape)), (sent, jnp.bfloat16, whole(sent))]
    kinds = [jax.ShapeDtypeStruct] * len(outs)
    specs, args = [IN_VMEM if part else IN_PLACE, IN_PLACE], [attn if part else in_hbm(attn), in_hbm(signs)]
    scratch = [pltpu.SMEM(signs.shape, signs.dtype)]
    if part == 0:
        outs.append((attn.shape, attn.dtype, IN_VMEM))
        kinds.append(pltpu.VMEM)
    if riding:
        specs.append(IN_PLACE)
        args.append(in_hbm(gain))
        scratch.append(pltpu.VMEM(gain.shape, gain.dtype))
    scratch.append(pltpu.SemaphoreType.DMA((2 + PIECES,)))
    return call(
        functools.partial(mix_kernel, part, cols // HD),
        1,
        [me],
        specs,
        args,
        outs,
        cost(6 * attn.size, 5 * attn.size),
        scratch,
        kinds,
    )


def load_kernel(tbl_ref, w_hbm, out, sem):
    depth, width = out.shape
    count, loads = sem.shape
    step, span = depth // loads, width // count
    copies = []
    for d in range(count):
        cols = pl.ds(pl.multiple_of(tbl_ref[d] * span, span), span)
        for k in range(loads):
            rows = pl.ds(k * step, step)
            to = out.at[rows, pl.ds(d * span, span)]
            copies.append(pltpu.make_async_copy(w_hbm.at[rows, cols], to, sem.at[d, k]))
    for copy in copies:
        copy.start()
    for copy in copies:
        copy.wait()


def load(w, tbl, width, flops=0):
    count = tbl.shape[0]
    return call(
        load_kernel,
        1,
        [tbl],
        [IN_PLACE],
        [in_hbm(w)],
        [((w.shape[0], count * width), w.dtype, IN_VMEM)],
        cost(flops, 0),
        [pltpu.SemaphoreType.DMA((count, LOADS))],
        [pltpu.VMEM],
    )[0]


def combine(order, me, own, recvs, rows):
    v = own[rows, :]
    for bit, recv in zip(order, recvs):
        flip = (1 - 2 * (me >> bit & 1)).astype(jnp.float32)
        v = recv[rows, :].astype(jnp.float32) + flip * v
    return v


def combine_into(out, orders, scale, me, ins):
    per = len(ins) // len(orders)
    size = ins[0].shape[0]
    for c, order in enumerate(orders):
        own, *recvs = ins[c * per : (c + 1) * per]

        @pl.loop(0, size // ROWS, unroll=UNROLL)
        def _(i):
            rows = pl.ds(pl.multiple_of(i * ROWS, ROWS), ROWS)
            to = pl.ds(pl.multiple_of(c * size + i * ROWS, ROWS), ROWS)
            out[to, :] = (combine(order, me, own, recvs, rows) * scale).astype(out.dtype)


def stage_kernel(order, ride, ride_rows, me_ref, *refs):
    riders, ins, out = refs[:ride], refs[ride:-1], refs[-1]
    size = ins[0].shape[0]
    combine_into(out, [order], 1.0, me_ref[0], ins)
    if ride:
        shape = (out.shape[0] - size, out.shape[1])
        row = lax.broadcasted_iota(jnp.int32, shape, 0)
        known = ride_rows
        block = riders[0][size:, :].astype(jnp.float32)
        for rider in riders[1:]:
            more = pltpu.roll(rider[size:, :].astype(jnp.float32), known, 0)
            block = jnp.where(row < known, block, more)
            known *= 2
        out[size:, :] = block.astype(out.dtype)


def stage(block, order, me, riders=(), ride_rows=0):
    flat = [*riders, *block]
    shape = riders[0].shape if riders else block[0].shape
    return call(
        functools.partial(stage_kernel, order, len(riders), ride_rows),
        1,
        [me],
        [whole(f.shape) for f in flat],
        flat,
        [(shape, jnp.bfloat16, whole(shape))],
        cost(4 * block[0].size * len(flat), 2 * block[0].size * (len(flat) + 2)),
    )[0]


def send_lists(order):
    lists = []
    for s, bit in enumerate(order):
        members = [1 << bit]
        for later in reversed(order[s + 1 :]):
            members = members + [m | 1 << later for m in members]
        lists.append(members)
    return lists + [[0]]


def project_kernel(plan, pieces, counts, adds, width, orders, scale, me_ref, *refs):
    added, refs = refs[: sum(adds)], refs[sum(adds) :]
    raws, rots = refs[: counts[0]], refs[counts[0] : sum(counts)]
    slab, outs = refs[sum(counts)], refs[sum(counts) + 1 :]
    if raws:
        combine_into(outs[-1], orders, scale, me_ref[0], raws)
        rots = [outs[-1]]
    for step, (out, lead, add, add_lead) in enumerate(plan):
        acc = None
        for rot, (row, depth) in zip(rots, pieces):
            term = jnp.dot(
                rot[...],
                slab[row : row + depth, step * width : (step + 1) * width],
                preferred_element_type=jnp.float32,
            )
            acc = term if acc is None else acc + term
        if add is not None:
            first = sum(adds[:add])
            more = [a[add_lead].astype(jnp.float32) for a in added[first : first + adds[add]]]
            acc = acc + (more[0] if len(more) == 1 else jnp.concatenate(more, axis=1))
        outs[out][lead] = acc.astype(outs[out].dtype)


def project(
    rots, slab, pieces, spans, width, dtypes, me, adds=(), leads=None, raws=(), orders=(), scale=1.0
):
    plan = [(k, n) for k, (_, count) in enumerate(spans) for n in range(count)]
    if leads is None:
        leads = plan if adds else [(None, None)] * len(plan)
    plan = [(*to, *add) for to, add in zip(plan, leads)]
    flat = [r for raw in raws for r in raw]
    args = [*[a for add in adds for a in add], *flat, *rots, slab]
    counts = [len(flat), len(rots)]
    rows = rots[0].shape[0] if rots else sum(raw[0].shape[0] for raw in raws)
    shapes = [((n, rows, width), dtype) for (_, n), dtype in zip(spans, dtypes)]
    if raws:
        shapes.append(((rows, flat[0].shape[1]), jnp.bfloat16))
    return call(
        functools.partial(
            project_kernel, plan, pieces, counts, [len(a) for a in adds], width, orders, scale
        ),
        1,
        [me],
        [IN_VMEM] * len(args),
        args,
        [(shape, dtype, whole(shape)) for shape, dtype in shapes],
        cost(PROJECT_FLOPS, 0),
    )


def close_kernel(colors, residual, exps, *refs):
    terms, out = refs[:-1], refs[-1]
    per = len(terms) // colors
    width = residual.shape[1] // colors
    for c in range(colors):
        cols = pl.ds(c * width, width)
        own, *recvs = terms[c * per : (c + 1) * per]
        acc = own[0].astype(jnp.float32)
        for recv in recvs:
            acc = acc + recv[0].astype(jnp.float32)
        acc = acc * jnp.exp2(exps[:, cols].astype(jnp.float32))
        out[c] = (residual[:, cols].astype(jnp.float32) + acc).astype(jnp.bfloat16)


def close(residual, exps, terms, at):
    colors = len(terms)
    _, rows, width = terms[0][0].shape
    span = width * colors
    flat = [t for color in terms for t in color]
    shape = (colors, rows, width)
    return call(
        functools.partial(close_kernel, colors),
        1,
        [],
        [
            pl.BlockSpec((rows, span), lambda i: (0, at)),
            pl.BlockSpec((1, span), lambda i: (0, at)),
        ]
        + [whole((1, rows, width))] * len(flat),
        [residual, exps, *flat],
        [(shape, jnp.bfloat16, whole(shape))],
        cost(10 * rows * span, 2 * rows * width * (len(flat) + 2 * colors)),
    )[0]


def kv_kernel(plan, gain_at, counts, colors, has_prev, channels, at, span, tbl_ref, *refs):
    prevs, w, refs = refs[: 2 * has_prev], refs[2 * has_prev], refs[2 * has_prev + 1 :]
    xs, riders, rest = refs[: counts[0]], refs[counts[0] : sum(counts)], refs[sum(counts) :]
    rows, cols = xs[0].shape[-2], w.shape[1]
    product = prevs[0][...] if has_prev else jnp.zeros((rows, cols), jnp.float32)
    square = prevs[1][...] if has_prev else jnp.zeros((rows, HD), jnp.float32)
    for step, blocks in enumerate(plan):
        rider, row = gain_at[step]
        rider = riders[rider]
        for k, lead, c in blocks:
            hidden = xs[k][lead].astype(jnp.float32)
            depth = hidden.shape[1]
            part, col = divmod(at * span + c * depth, rider.shape[1])
            gain = rider[rows // colors :, col : col + depth].astype(jnp.float32)
            gain = gain[row + part : row + part + 1]
            scaled = (hidden * gain).astype(jnp.bfloat16)
            first = pl.multiple_of((tbl_ref[step] + at) * span + c * depth, depth)
            product = product + jnp.dot(
                scaled, w[pl.ds(first, depth), :], preferred_element_type=jnp.float32
            )
            hidden = hidden * hidden
            for b in range(depth // HD):
                square = square + hidden[:, b * HD : (b + 1) * HD]
    if channels:
        exps, out = rest
        mean = jnp.sum(square, axis=1, keepdims=True) / channels
        scale = jnp.exp2(exps[...].astype(jnp.float32))
        out[...] = (product * lax.rsqrt(mean + EPS) * scale).astype(out.dtype)
    else:
        rest[0][...], rest[1][...] = product, square


def kv_step(plan, arrays, riders, gain_at, colors, w_kv, tbl, at, span, prev, exps, channels):
    used = sorted({k for blocks in plan for k, _, _ in blocks})
    xs = [arrays[k] for k in used]
    plan = [[(used.index(k), lead, c) for k, lead, c in blocks] for blocks in plan]
    rows = xs[0].shape[1]
    cols = w_kv.shape[1]
    extra = []
    if channels:
        extra.append(exps)
        outs = [((rows, cols), jnp.bfloat16)]
    else:
        outs = [((rows, cols), jnp.float32), ((rows, HD), jnp.float32)]
    args = [*(prev or ()), w_kv, *xs, *riders, *extra]
    counts = [len(xs), len(riders)]
    return call(
        functools.partial(
            kv_kernel, plan, gain_at, counts, colors, prev is not None, channels, at, span
        ),
        1,
        [tbl],
        [IN_VMEM] * len(args),
        args,
        [(shape, dtype, whole(shape)) for shape, dtype in outs],
        cost(
            2 * rows * span * cols * len(plan), 2 * span * (rows + cols) * len(plan) + 4 * rows * cols
        ),
    )


def gather(x, orders, count):
    colors = x.shape[0]
    arrays, where = [x], {0: [(0, c) for c in range(colors)]}
    levels = len(orders[0])
    for bit in range(levels):
        arrays.append(swap(x, bit, count))
        where[1 << bit] = [(len(arrays) - 1, c) for c in range(colors)]
    for size in range(2, levels + 1):
        for r in range(count):
            if r.bit_count() == size:
                where[r] = []
                for c, order in enumerate(orders):
                    hop = max((b for b in range(levels) if r >> b & 1), key=order.index)
                    k, at = where[r ^ 1 << hop][c]
                    arrays.append(swap(arrays[k][at : at + 1], hop, count))
                    where[r].append((len(arrays) - 1, 0))
    plan = [[(k, at, c) for c, (k, at) in enumerate(blocks)] for blocks in where.values()]
    return arrays, list(zip(where, plan))


def body(attn_out, head_signs, w_out, out_exp, residual, norm_gain, w_kv, kv_exp):
    count = lax.axis_size("tensor")
    levels = count.bit_length() - 1
    me = lax.axis_index("tensor").astype(jnp.int32)
    odd = lax.axis_index("dp") % 2 == 1
    me_arr = me.reshape(1)
    by = levels // 2
    unturned = (me >> by | me << levels - by) & count - 1
    logical = jnp.where(odd, unturned, me).reshape(1)
    depth, local = w_out.shape[0], residual.shape[1]
    channels = local * count
    orders = [list(range(levels))]
    orders.append(orders[0][levels // 2 :] + orders[0][: levels // 2])
    colors = len(orders)
    half = local // HALVES
    wide = half // colors

    def devices(rel):
        far = jnp.array([turned(r, levels) for r in rel], jnp.int32)
        return me ^ jnp.where(odd, far, jnp.array(rel, jnp.int32))

    lists = [send_lists(order) for order in orders]

    def blocks_of(stages, v):
        spans, rel, color = [], [], []
        for s in stages:
            for c in range(colors):
                spans.append((len(rel), len(lists[c][s])))
                rel += lists[c][s]
                color += [v * colors + c] * len(lists[c][s])
        return devices(rel) * (local // wide) + jnp.array(color, jnp.int32), spans

    later = range(1, levels + 1)
    first_tbls = [blocks_of([0], v)[0] for v in range(HALVES)]
    rest_tbls = [blocks_of(later, v)[0] for v in range(HALVES)]
    first_spans, rest_spans = blocks_of([0], 0)[1], blocks_of(later, 0)[1]

    exps = out_exp.reshape(1, -1)
    kv_exps = kv_exp.reshape(1, -1)

    blocks, riders = [], []
    attn = attn_out
    for p in range(len(QUARTERS)):
        mixed = mix(attn, me_arr, head_signs, norm_gain, p, colors, count)
        if p == 0:
            attn = mixed[-1]
        blocks.append([])
        for c, order in enumerate(orders):
            own, sent = mixed[2 * c : 2 * c + 2]
            blocks[p].append([own, swap(sent, order[0], count)])
            if p == RIDE and c == 0:
                riders += [sent, blocks[p][c][1]]
    ride_rows = local // riders[0].shape[1]
    slabs = [load(w_out, after(first_tbls[0], sent), wide)]
    here = after(logical, slabs[0])
    for s in range(1, levels):
        sends = []
        for p in range(len(QUARTERS)):
            for c, order in enumerate(orders):
                ride = p == RIDE and c == 0
                send = stage(blocks[p][c], order, here, riders if ride else (), ride_rows)
                blocks[p][c].append(swap(send, order[s], count))
                sends.append(send)
                if ride:
                    riders.append(blocks[p][c][-1])
            here = after(logical, *sends)
    slabs.append(load(w_out, after(first_tbls[1], *sends), wide, BUSY))

    gain_at, known = {0: (0, 0)}, [0]
    for t, bit in enumerate(orders[0]):
        gain_at.update({r ^ 1 << bit: (t + 1, ride_rows * k) for k, r in enumerate(known)})
        known += [r ^ 1 << bit for r in known]

    bf16, f32 = jnp.bfloat16, jnp.float32
    cut = blocks[0][0][0].shape[1]
    pieces = [(0, cut), (cut, depth - cut)]
    scale = head_signs.shape[0] ** -0.5
    *prevs, rot = project(
        [], slabs[0], pieces[:1], first_spans, wide, [f32] * colors, after(logical, slabs[1]),
        raws=blocks[0], orders=orders, scale=scale,
    )
    rots = [rot]
    *sends, rot = project(
        [], slabs[0], pieces[1:], first_spans, wide, [bf16] * colors, logical,
        [[p] for p in prevs], raws=blocks[1], orders=orders, scale=scale,
    )
    rots.append(rot)
    received = []
    for v in range(HALVES):
        if v:
            sends = project(
                rots, slabs[v], pieces, first_spans, wide, [bf16] * colors, logical
            )
        received.append([swap(send, order[0], count) for send, order in zip(sends, orders)])

    leads = []
    for s in later:
        for c in range(colors):
            n = len(lists[c][s])
            leads += [(c, k + n * (s < levels)) for k in range(n)]
    dtypes = [bf16 if s == 1 and levels > 1 else f32 for s in later for _ in range(colors)]

    def keys_and_values(run, running, last):
        v, arrays, run = run
        return kv_step(
            [plan for _, plan in run],
            arrays,
            riders,
            [gain_at[r] for r, _ in run],
            colors,
            w_kv,
            devices([r for r, _ in run]) * HALVES,
            v,
            half,
            running,
            kv_exps,
            channels * last,
        )

    resids, runs, running = [], [], None
    for v in range(HALVES):
        adds = [[r] for r in received[v]]
        slab = load(w_out, after(rest_tbls[v], *sends), wide)
        parts = project(
            rots, slab, pieces, rest_spans, wide, dtypes, logical, adds, leads
        )
        sends = parts[:colors]
        terms = []
        for c, order in enumerate(orders):
            recvs = []
            for s in range(1, levels):
                send = parts[(s - 1) * colors + c]
                if recvs:
                    size = send.shape[0]
                    for recv in recvs:
                        send = send + recv[size : 2 * size].astype(f32)
                    send = send.astype(bf16)
                recvs.append(swap(send, order[s], count))
            terms.append([parts[(levels - 1) * colors + c], *recvs])
        out = close(residual, exps, terms, v)
        resids += list(out)
        arrays, found = gather(out, orders, count)
        for far in (False, True):
            run = [b for b in found if (b[0].bit_count() > 1) == far]
            if run and not far:
                running = keys_and_values((v, arrays, run), running, False)
            elif run:
                runs.append((v, arrays, run))

    for k, run in enumerate(runs):
        running = keys_and_values(run, running, k == len(runs) - 1)
    return jnp.concatenate(resids, axis=1), running[0]


def solution(mesh):
    placed = (
        P("dp", "tensor"),
        P(),
        P("tensor", None),
        P("tensor"),
        P("dp", "tensor"),
        P("tensor"),
        P(None, "tensor"),
        P("tensor"),
    )
    return jax.shard_map(
        body,
        mesh=mesh,
        in_specs=placed,
        out_specs=(P("dp", "tensor"), P("dp", "tensor")),
        check_vma=False,
    )
```

```python
import functools

import jax
import jax.numpy as jnp
from jax import lax
from jax.experimental import pallas as pl
from jax.experimental.pallas import tpu as pltpu
from jax.sharding import PartitionSpec as P

HD = 128
EPS = 1e-05
QUARTERS = ((0, 1), (2, 3))
RIDE = 0
HALVES = 2
PIECES = 4
LOADS = 4
ROWS = 16
UNROLL = 2
VMEM = 4 * 1024 * 1024
PROJECT_FLOPS = 1e6
BUSY = 4e9


def cost(flops, nbytes):
    return pl.CostEstimate(flops=int(flops), bytes_accessed=int(nbytes), transcendentals=0)


def call(kernel, grid, scalars, in_specs, args, outs, estimate, scratch=(), kinds=None):
    kinds = kinds or [jax.ShapeDtypeStruct] * len(outs)
    return pl.pallas_call(
        kernel,
        grid_spec=pltpu.PrefetchScalarGridSpec(
            num_scalar_prefetch=len(scalars),
            grid=(grid,),
            in_specs=in_specs,
            out_specs=[spec for _, _, spec in outs],
            scratch_shapes=list(scratch),
        ),
        out_shape=[kind(shape, dtype) for (shape, dtype, _), kind in zip(outs, kinds)],
        compiler_params=pltpu.CompilerParams(vmem_limit_bytes=VMEM),
        cost_estimate=estimate,
    )(*scalars, *args)


def whole(shape):
    return pl.BlockSpec(shape, lambda *_: (0,) * len(shape))


IN_PLACE = pl.BlockSpec(memory_space=pl.ANY)
IN_VMEM = pl.BlockSpec(memory_space=pltpu.VMEM)


def in_hbm(array):
    return pltpu.with_memory_space_constraint(array, pltpu.HBM)


def after(value, *others):
    return lax.optimization_barrier((value, *others))[0]


def turned(bits, levels):
    by = levels // 2
    return (bits << by | bits >> levels - by) & (1 << levels) - 1


def swap(block, bit, count):
    levels = count.bit_length() - 1
    masks = (1 << bit, turned(1 << bit, levels))
    route = [
        (d * count + i, d * count + (i ^ masks[d % 2]))
        for d in range(lax.axis_size("dp"))
        for i in range(count)
    ]
    return lax.ppermute(block, ("dp", "tensor"), route)


def mix_rows(part, heads, c, i, size, signs, attn, sent):
    quarter = heads // 4
    at = pl.ds(pl.multiple_of(c * size + i * ROWS, ROWS), ROWS)
    rows = pl.ds(pl.multiple_of(i * ROWS, ROWS), ROWS)

    def head(h):
        return attn[at, pl.ds(h * HD, HD)].astype(jnp.float32) * signs[h]

    mixed = [[] for _ in QUARTERS[part]]
    for h in range(quarter):
        a, b, c2, d = [head(q * quarter + h) for q in range(4)]
        upper, lower = (a + c2, b + d), (a - c2, b - d)
        for k, q in enumerate(QUARTERS[part]):
            one, two = lower if q & 2 else upper
            mixed[k].append(one - two if q & 1 else one + two)
    for k, v in enumerate(mixed):
        step = 1
        while step < quarter:
            for lo in range(quarter):
                if not lo & step:
                    a, b = v[lo], v[lo | step]
                    v[lo], v[lo | step] = a + b, a - b
            step *= 2
        for h in range(quarter):
            cols = pl.ds((k * quarter + h) * HD, HD)
            sent[rows, cols] = v[h].astype(sent.dtype)


def mix_kernel(part, heads, me_ref, *refs):
    ride = part == RIDE
    attn, signs_ref, *refs = refs
    gain_hbm, *refs = refs if ride else (None, *refs)
    *outs, sem = refs
    gain, outs = (outs[-1], outs[:-1]) if ride else (None, outs)
    signs_mem, outs = outs[-1], outs[:-1]
    me = me_ref[0]
    get_signs = pltpu.make_async_copy(signs_ref, signs_mem, sem.at[0])
    get_signs.start()
    step = attn.shape[0] // PIECES
    pieces = []
    if part == 0:
        attn_hbm, attn, outs = attn, outs[-1], outs[:-1]
        for k in range(PIECES):
            rows = pl.ds(k * step, step)
            pieces.append(
                pltpu.make_async_copy(attn_hbm.at[rows, :], attn.at[rows, :], sem.at[2 + k])
            )
            pieces[k].start()
    size = attn.shape[0] // len(outs)
    if ride:
        get_gain = pltpu.make_async_copy(gain_hbm, gain, sem.at[1])
        get_gain.start()
        get_gain.wait()
        sent = outs[0]
        shape = (sent.shape[0] - size, sent.shape[1])
        row = lax.broadcasted_iota(jnp.int32, shape, 0)
        block = jnp.zeros(shape, jnp.float32)
        for k in range(gain.shape[0] // shape[1]):
            piece = gain[pl.ds(k * shape[1], shape[1])].astype(jnp.float32)
            block = jnp.where(row == k, jnp.broadcast_to(piece[None, :], shape), block)
        sent[size:, :] = block.astype(sent.dtype)
    get_signs.wait()
    signs = [(2 * signs_mem[me * heads + h] - 1).astype(jnp.float32) for h in range(heads)]
    for k in range(PIECES):
        if pieces:
            pieces[k].wait()
        c, first = k * step // size, k * step % size // ROWS

        @pl.loop(first, first + step // ROWS)
        def _(i):
            mix_rows(part, heads, c, i, size, signs, attn, outs[c])


def mix(attn, me, signs, gain, part, colors, count):
    rows, cols = attn.shape
    shape = (rows // colors, cols // 4 * len(QUARTERS[part]))
    riding = part == RIDE
    ride = -(-count // 2 * (gain.shape[0] // shape[1]) // ROWS) * ROWS
    outs = []
    for c in range(colors):
        sent = (shape[0] + ride * (riding and c == 0), shape[1])
        outs.append((sent, jnp.bfloat16, whole(sent)))
    kinds = [jax.ShapeDtypeStruct] * len(outs)
    specs, args = [IN_VMEM if part else IN_PLACE, IN_PLACE], [attn if part else in_hbm(attn), in_hbm(signs)]
    scratch = [pltpu.SMEM(signs.shape, signs.dtype)]
    if part == 0:
        outs.append((attn.shape, attn.dtype, IN_VMEM))
        kinds.append(pltpu.VMEM)
    if riding:
        specs.append(IN_PLACE)
        args.append(in_hbm(gain))
        scratch.append(pltpu.VMEM(gain.shape, gain.dtype))
    scratch.append(pltpu.SemaphoreType.DMA((2 + PIECES,)))
    return call(
        functools.partial(mix_kernel, part, cols // HD),
        1,
        [me],
        specs,
        args,
        outs,
        cost(6 * attn.size, 5 * attn.size),
        scratch,
        kinds,
    )


def load_kernel(tbl_ref, w_hbm, out, sem):
    depth, width = out.shape
    count, loads = sem.shape
    step, span = depth // loads, width // count
    copies = []
    for d in range(count):
        cols = pl.ds(pl.multiple_of(tbl_ref[d] * span, span), span)
        for k in range(loads):
            rows = pl.ds(k * step, step)
            to = out.at[rows, pl.ds(d * span, span)]
            copies.append(pltpu.make_async_copy(w_hbm.at[rows, cols], to, sem.at[d, k]))
    for copy in copies:
        copy.start()
    for copy in copies:
        copy.wait()


def load(w, tbl, width, flops=0):
    count = tbl.shape[0]
    return call(
        load_kernel,
        1,
        [tbl],
        [IN_PLACE],
        [in_hbm(w)],
        [((w.shape[0], count * width), w.dtype, IN_VMEM)],
        cost(flops, 0),
        [pltpu.SemaphoreType.DMA((count, LOADS))],
        [pltpu.VMEM],
    )[0]


def combine(order, me, own, recvs, rows):
    v = own[rows, :].astype(jnp.float32)
    for bit, recv in zip(order, recvs):
        flip = (1 - 2 * (me >> bit & 1)).astype(jnp.float32)
        v = recv[rows, :].astype(jnp.float32) + flip * v
    return v


def combine_into(out, orders, scale, me, size, ins):
    per = len(ins) // len(orders)
    for c, order in enumerate(orders):
        own, *recvs = ins[c * per : (c + 1) * per]

        @pl.loop(0, size // ROWS, unroll=UNROLL)
        def _(i):
            rows = pl.ds(pl.multiple_of(i * ROWS, ROWS), ROWS)
            to = pl.ds(pl.multiple_of(c * size + i * ROWS, ROWS), ROWS)
            out[to, :] = (combine(order, me, own, recvs, rows) * scale).astype(out.dtype)


def stage_kernel(order, size, ride, ride_rows, me_ref, *refs):
    riders, ins, out = refs[:ride], refs[ride:-1], refs[-1]
    combine_into(out, [order], 1.0, me_ref[0], size, ins)
    if ride:
        shape = (out.shape[0] - size, out.shape[1])
        row = lax.broadcasted_iota(jnp.int32, shape, 0)
        known = ride_rows
        block = riders[0][size:, :].astype(jnp.float32)
        for rider in riders[1:]:
            more = pltpu.roll(rider[size:, :].astype(jnp.float32), known, 0)
            block = jnp.where(row < known, block, more)
            known *= 2
        out[size:, :] = block.astype(out.dtype)


def stage(block, order, me, size, riders=(), ride_rows=0):
    flat = [*riders, *block]
    shape = riders[0].shape if riders else (size, block[0].shape[1])
    return call(
        functools.partial(stage_kernel, order, size, len(riders), ride_rows),
        1,
        [me],
        [whole(f.shape) for f in flat],
        flat,
        [(shape, jnp.bfloat16, whole(shape))],
        cost(4 * block[0].size * len(flat), 2 * block[0].size * (len(flat) + 2)),
    )[0]


def send_lists(order):
    lists = []
    for s, bit in enumerate(order):
        members = [1 << bit]
        for later in reversed(order[s + 1 :]):
            members = members + [m | 1 << later for m in members]
        lists.append(members)
    return lists + [[0]]


def project_kernel(plan, pieces, counts, adds, width, orders, scale, me_ref, *refs):
    added, refs = refs[: sum(adds)], refs[sum(adds) :]
    raws, rots = refs[: counts[0]], refs[counts[0] : sum(counts)]
    slab, outs = refs[sum(counts)], refs[sum(counts) + 1 :]
    if raws:
        size = outs[-1].shape[0] // len(orders)
        combine_into(outs[-1], orders, scale, me_ref[0], size, raws)
        rots = [outs[-1]]
    for step, (out, lead, add, add_lead) in enumerate(plan):
        acc = None
        for rot, (row, depth) in zip(rots, pieces):
            term = jnp.dot(
                rot[...],
                slab[row : row + depth, step * width : (step + 1) * width],
                preferred_element_type=jnp.float32,
            )
            acc = term if acc is None else acc + term
        if add is not None:
            first = sum(adds[:add])
            more = [a[add_lead].astype(jnp.float32) for a in added[first : first + adds[add]]]
            acc = acc + (more[0] if len(more) == 1 else jnp.concatenate(more, axis=1))
        outs[out][lead] = acc.astype(outs[out].dtype)


def project(
    rows, rots, slab, pieces, spans, width, dtypes, me, adds=(), leads=None, raws=(), orders=(), scale=1.0
):
    plan = [(k, n) for k, (_, count) in enumerate(spans) for n in range(count)]
    if leads is None:
        leads = plan if adds else [(None, None)] * len(plan)
    plan = [(*to, *add) for to, add in zip(plan, leads)]
    flat = [r for raw in raws for r in raw]
    args = [*[a for add in adds for a in add], *flat, *rots, slab]
    counts = [len(flat), len(rots)]
    shapes = [((n, rows, width), dtype) for (_, n), dtype in zip(spans, dtypes)]
    if raws:
        shapes.append(((rows, flat[0].shape[1]), jnp.bfloat16))
    return call(
        functools.partial(
            project_kernel, plan, pieces, counts, [len(a) for a in adds], width, orders, scale
        ),
        1,
        [me],
        [IN_VMEM] * len(args),
        args,
        [(shape, dtype, whole(shape)) for shape, dtype in shapes],
        cost(PROJECT_FLOPS, 0),
    )


def close_kernel(colors, residual, exps, *refs):
    terms, out = refs[:-1], refs[-1]
    per = len(terms) // colors
    width = residual.shape[1] // colors
    for c in range(colors):
        cols = pl.ds(c * width, width)
        own, *recvs = terms[c * per : (c + 1) * per]
        acc = own[0].astype(jnp.float32)
        for recv in recvs:
            acc = acc + recv[0].astype(jnp.float32)
        acc = acc * jnp.exp2(exps[:, cols].astype(jnp.float32))
        out[c] = (residual[:, cols].astype(jnp.float32) + acc).astype(jnp.bfloat16)


def close(residual, exps, terms, at):
    colors = len(terms)
    _, rows, width = terms[0][0].shape
    span = width * colors
    flat = [t for color in terms for t in color]
    shape = (colors, rows, width)
    return call(
        functools.partial(close_kernel, colors),
        1,
        [],
        [
            pl.BlockSpec((rows, span), lambda i: (0, at)),
            pl.BlockSpec((1, span), lambda i: (0, at)),
        ]
        + [whole((1, rows, width))] * len(flat),
        [residual, exps, *flat],
        [(shape, jnp.bfloat16, whole(shape))],
        cost(10 * rows * span, 2 * rows * width * (len(flat) + 2 * colors)),
    )[0]


def kv_kernel(plan, gain_at, counts, colors, has_prev, channels, at, span, tbl_ref, *refs):
    prevs, w, refs = refs[: 2 * has_prev], refs[2 * has_prev], refs[2 * has_prev + 1 :]
    xs, riders, rest = refs[: counts[0]], refs[counts[0] : sum(counts)], refs[sum(counts) :]
    rows, cols = xs[0].shape[-2], w.shape[1]
    product = prevs[0][...] if has_prev else jnp.zeros((rows, cols), jnp.float32)
    square = prevs[1][...] if has_prev else jnp.zeros((rows, HD), jnp.float32)
    for step, blocks in enumerate(plan):
        rider, row = gain_at[step]
        rider = riders[rider]
        for k, lead, c in blocks:
            hidden = xs[k][lead].astype(jnp.float32)
            depth = hidden.shape[1]
            part, col = divmod(at * span + c * depth, rider.shape[1])
            gain = rider[rows // colors :, col : col + depth].astype(jnp.float32)
            gain = gain[row + part : row + part + 1]
            scaled = (hidden * gain).astype(jnp.bfloat16)
            first = pl.multiple_of((tbl_ref[step] + at) * span + c * depth, depth)
            product = product + jnp.dot(
                scaled, w[pl.ds(first, depth), :], preferred_element_type=jnp.float32
            )
            hidden = hidden * hidden
            for b in range(depth // HD):
                square = square + hidden[:, b * HD : (b + 1) * HD]
    if channels:
        exps, out = rest
        mean = jnp.sum(square, axis=1, keepdims=True) / channels
        scale = jnp.exp2(exps[...].astype(jnp.float32))
        out[...] = (product * lax.rsqrt(mean + EPS) * scale).astype(out.dtype)
    else:
        rest[0][...], rest[1][...] = product, square


def kv_step(plan, arrays, riders, gain_at, colors, w_kv, tbl, at, span, prev, exps, channels):
    used = sorted({k for blocks in plan for k, _, _ in blocks})
    xs = [arrays[k] for k in used]
    plan = [[(used.index(k), lead, c) for k, lead, c in blocks] for blocks in plan]
    rows = xs[0].shape[1]
    cols = w_kv.shape[1]
    extra = []
    if channels:
        extra.append(exps)
        outs = [((rows, cols), jnp.bfloat16)]
    else:
        outs = [((rows, cols), jnp.float32), ((rows, HD), jnp.float32)]
    args = [*(prev or ()), w_kv, *xs, *riders, *extra]
    counts = [len(xs), len(riders)]
    return call(
        functools.partial(
            kv_kernel, plan, gain_at, counts, colors, prev is not None, channels, at, span
        ),
        1,
        [tbl],
        [IN_VMEM] * len(args),
        args,
        [(shape, dtype, whole(shape)) for shape, dtype in outs],
        cost(
            2 * rows * span * cols * len(plan), 2 * span * (rows + cols) * len(plan) + 4 * rows * cols
        ),
    )


def gather(x, orders, count):
    colors = x.shape[0]
    arrays, where = [x], {0: [(0, c) for c in range(colors)]}
    levels = len(orders[0])
    for bit in range(levels):
        arrays.append(swap(x, bit, count))
        where[1 << bit] = [(len(arrays) - 1, c) for c in range(colors)]
    for size in range(2, levels + 1):
        for r in range(count):
            if r.bit_count() == size:
                where[r] = []
                for c, order in enumerate(orders):
                    hop = max((b for b in range(levels) if r >> b & 1), key=order.index)
                    k, at = where[r ^ 1 << hop][c]
                    arrays.append(swap(arrays[k][at : at + 1], hop, count))
                    where[r].append((len(arrays) - 1, 0))
    plan = [[(k, at, c) for c, (k, at) in enumerate(blocks)] for blocks in where.values()]
    return arrays, list(zip(where, plan))


def body(attn_out, head_signs, w_out, out_exp, residual, norm_gain, w_kv, kv_exp):
    count = lax.axis_size("tensor")
    levels = count.bit_length() - 1
    me = lax.axis_index("tensor").astype(jnp.int32)
    odd = lax.axis_index("dp") % 2 == 1
    me_arr = me.reshape(1)
    by = levels // 2
    unturned = (me >> by | me << levels - by) & count - 1
    logical = jnp.where(odd, unturned, me).reshape(1)
    depth, (tokens, local) = w_out.shape[0], residual.shape
    channels = local * count
    orders = [list(range(levels))]
    orders.append(orders[0][levels // 2 :] + orders[0][: levels // 2])
    colors = len(orders)
    half = local // HALVES
    wide = half // colors

    def devices(rel):
        far = jnp.array([turned(r, levels) for r in rel], jnp.int32)
        return me ^ jnp.where(odd, far, jnp.array(rel, jnp.int32))

    lists = [send_lists(order) for order in orders]

    def blocks_of(stages, v):
        spans, rel, color = [], [], []
        for s in stages:
            for c in range(colors):
                spans.append((len(rel), len(lists[c][s])))
                rel += lists[c][s]
                color += [v * colors + c] * len(lists[c][s])
        return devices(rel) * (local // wide) + jnp.array(color, jnp.int32), spans

    later = range(1, levels + 1)
    first_tbls = [blocks_of([0], v)[0] for v in range(HALVES)]
    rest_tbls = [blocks_of(later, v)[0] for v in range(HALVES)]
    first_spans, rest_spans = blocks_of([0], 0)[1], blocks_of(later, 0)[1]

    exps = out_exp.reshape(1, -1)
    kv_exps = kv_exp.reshape(1, -1)

    blocks, riders = [], []
    attn = attn_out
    for p in range(len(QUARTERS)):
        mixed = mix(attn, me_arr, head_signs, norm_gain, p, colors, count)
        if p == 0:
            attn = mixed[-1]
        blocks.append([])
        for c, order in enumerate(orders):
            sent = mixed[c]
            blocks[p].append([sent, swap(sent, order[0], count)])
            if p == RIDE and c == 0:
                riders += [sent, blocks[p][c][1]]
    ride_rows = local // riders[0].shape[1]
    slabs = [load(w_out, after(first_tbls[0], sent), wide)]
    here = after(logical, slabs[0])
    for s in range(1, levels):
        sends = []
        for p in range(len(QUARTERS)):
            for c, order in enumerate(orders):
                ride = p == RIDE and c == 0
                send = stage(
                    blocks[p][c], order, here, tokens // colors, riders if ride else (), ride_rows
                )
                blocks[p][c].append(swap(send, order[s], count))
                sends.append(send)
                if ride:
                    riders.append(blocks[p][c][-1])
            here = after(logical, *sends)
    slabs.append(load(w_out, after(first_tbls[1], *sends), wide, BUSY))

    gain_at, known = {0: (0, 0)}, [0]
    for t, bit in enumerate(orders[0]):
        gain_at.update({r ^ 1 << bit: (t + 1, ride_rows * k) for k, r in enumerate(known)})
        known += [r ^ 1 << bit for r in known]

    bf16, f32 = jnp.bfloat16, jnp.float32
    cut = blocks[0][0][0].shape[1]
    pieces = [(0, cut), (cut, depth - cut)]
    scale = head_signs.shape[0] ** -0.5
    *prevs, rot = project(
        tokens, [], slabs[0], pieces[:1], first_spans, wide, [f32] * colors, after(logical, slabs[1]),
        raws=blocks[0], orders=orders, scale=scale,
    )
    rots = [rot]
    *sends, rot = project(
        tokens, [], slabs[0], pieces[1:], first_spans, wide, [bf16] * colors, logical,
        [[p] for p in prevs], raws=blocks[1], orders=orders, scale=scale,
    )
    rots.append(rot)
    received = []
    for v in range(HALVES):
        if v:
            sends = project(
                tokens, rots, slabs[v], pieces, first_spans, wide, [bf16] * colors, logical
            )
        received.append([swap(send, order[0], count) for send, order in zip(sends, orders)])

    leads = []
    for s in later:
        for c in range(colors):
            n = len(lists[c][s])
            leads += [(c, k + n * (s < levels)) for k in range(n)]
    dtypes = [bf16 if s == 1 and levels > 1 else f32 for s in later for _ in range(colors)]

    def keys_and_values(run, running, last):
        v, arrays, run = run
        return kv_step(
            [plan for _, plan in run],
            arrays,
            riders,
            [gain_at[r] for r, _ in run],
            colors,
            w_kv,
            devices([r for r, _ in run]) * HALVES,
            v,
            half,
            running,
            kv_exps,
            channels * last,
        )

    resids, runs, running = [], [], None
    for v in range(HALVES):
        adds = [[r] for r in received[v]]
        slab = load(w_out, after(rest_tbls[v], *sends), wide)
        parts = project(
            tokens, rots, slab, pieces, rest_spans, wide, dtypes, logical, adds, leads
        )
        sends = parts[:colors]
        terms = []
        for c, order in enumerate(orders):
            recvs = []
            for s in range(1, levels):
                send = parts[(s - 1) * colors + c]
                if recvs:
                    size = send.shape[0]
                    for recv in recvs:
                        send = send + recv[size : 2 * size].astype(f32)
                    send = send.astype(bf16)
                recvs.append(swap(send, order[s], count))
            terms.append([parts[(levels - 1) * colors + c], *recvs])
        out = close(residual, exps, terms, v)
        resids += list(out)
        arrays, found = gather(out, orders, count)
        for far in (False, True):
            run = [b for b in found if (b[0].bit_count() > 1) == far]
            if run and not far:
                running = keys_and_values((v, arrays, run), running, False)
            elif run:
                runs.append((v, arrays, run))

    for k, run in enumerate(runs):
        running = keys_and_values(run, running, k == len(runs) - 1)
    return jnp.concatenate(resids, axis=1), running[0]


def solution(mesh):
    placed = (
        P("dp", "tensor"),
        P(),
        P("tensor", None),
        P("tensor"),
        P("dp", "tensor"),
        P("tensor"),
        P(None, "tensor"),
        P("tensor"),
    )
    return jax.shard_map(
        body,
        mesh=mesh,
        in_specs=placed,
        out_specs=(P("dp", "tensor"), P("dp", "tensor")),
        check_vma=False,
    )
```

```python
import functools

import jax
import jax.numpy as jnp
from jax import lax
from jax.experimental import pallas as pl
from jax.experimental.pallas import tpu as pltpu
from jax.sharding import PartitionSpec as P

HD = 128
EPS = 1e-05
QUARTERS = ((0, 1), (2, 3))
RIDE = 0
HALVES = 2
PIECES = 4
LOADS = 4
ROWS = 16
UNROLL = 2
VMEM = 4 * 1024 * 1024
PROJECT_FLOPS = 1e6
BUSY = 4e9


def cost(flops, nbytes):
    return pl.CostEstimate(flops=int(flops), bytes_accessed=int(nbytes), transcendentals=0)


def call(kernel, grid, scalars, in_specs, args, outs, estimate, scratch=(), kinds=None):
    kinds = kinds or [jax.ShapeDtypeStruct] * len(outs)
    return pl.pallas_call(
        kernel,
        grid_spec=pltpu.PrefetchScalarGridSpec(
            num_scalar_prefetch=len(scalars),
            grid=(grid,),
            in_specs=in_specs,
            out_specs=[spec for _, _, spec in outs],
            scratch_shapes=list(scratch),
        ),
        out_shape=[kind(shape, dtype) for (shape, dtype, _), kind in zip(outs, kinds)],
        compiler_params=pltpu.CompilerParams(vmem_limit_bytes=VMEM),
        cost_estimate=estimate,
    )(*scalars, *args)


def whole(shape):
    return pl.BlockSpec(shape, lambda *_: (0,) * len(shape))


IN_PLACE = pl.BlockSpec(memory_space=pl.ANY)
IN_VMEM = pl.BlockSpec(memory_space=pltpu.VMEM)


def in_hbm(array):
    return pltpu.with_memory_space_constraint(array, pltpu.HBM)


def after(value, *others):
    return lax.optimization_barrier((value, *others))[0]


def turned(bits, levels):
    by = levels // 2
    return (bits << by | bits >> levels - by) & (1 << levels) - 1


def swap(block, bit, count):
    levels = count.bit_length() - 1
    masks = (1 << bit, turned(1 << bit, levels))
    route = [
        (d * count + i, d * count + (i ^ masks[d % 2]))
        for d in range(lax.axis_size("dp"))
        for i in range(count)
    ]
    return lax.ppermute(block, ("dp", "tensor"), route)


def mix_rows(part, heads, c, i, size, signs, attn, sent):
    quarter = heads // 4
    at = pl.ds(pl.multiple_of(c * size + i * ROWS, ROWS), ROWS)
    rows = pl.ds(pl.multiple_of(i * ROWS, ROWS), ROWS)

    def head(h):
        return attn[at, pl.ds(h * HD, HD)].astype(jnp.float32) * signs[h]

    mixed = [[] for _ in QUARTERS[part]]
    for h in range(quarter):
        a, b, c2, d = [head(q * quarter + h) for q in range(4)]
        upper, lower = (a + c2, b + d), (a - c2, b - d)
        for k, q in enumerate(QUARTERS[part]):
            one, two = lower if q & 2 else upper
            mixed[k].append(one - two if q & 1 else one + two)
    for k, v in enumerate(mixed):
        step = 1
        while step < quarter:
            for lo in range(quarter):
                if not lo & step:
                    a, b = v[lo], v[lo | step]
                    v[lo], v[lo | step] = a + b, a - b
            step *= 2
        for h in range(quarter):
            cols = pl.ds((k * quarter + h) * HD, HD)
            sent[rows, cols] = v[h].astype(sent.dtype)


def mix_kernel(part, heads, me_ref, *refs):
    ride = part == RIDE
    attn, signs_ref, *refs = refs
    gain_hbm, *refs = refs if ride else (None, *refs)
    *outs, sem = refs
    gain, outs = (outs[-1], outs[:-1]) if ride else (None, outs)
    signs_mem, outs = outs[-1], outs[:-1]
    me = me_ref[0]
    get_signs = pltpu.make_async_copy(signs_ref, signs_mem, sem.at[0])
    get_signs.start()
    step = attn.shape[0] // PIECES
    pieces = []
    if part == 0:
        attn_hbm, attn, outs = attn, outs[-1], outs[:-1]
        for k in range(PIECES):
            rows = pl.ds(k * step, step)
            pieces.append(
                pltpu.make_async_copy(attn_hbm.at[rows, :], attn.at[rows, :], sem.at[2 + k])
            )
            pieces[k].start()
    size = attn.shape[0] // len(outs)
    if ride:
        get_gain = pltpu.make_async_copy(gain_hbm, gain, sem.at[1])
        get_gain.start()
        get_gain.wait()
        sent = outs[0]
        shape = (sent.shape[0] - size, sent.shape[1])
        row = lax.broadcasted_iota(jnp.int32, shape, 0)
        block = jnp.zeros(shape, jnp.float32)
        for k in range(gain.shape[0] // shape[1]):
            piece = gain[pl.ds(k * shape[1], shape[1])].astype(jnp.float32)
            block = jnp.where(row == k, jnp.broadcast_to(piece[None, :], shape), block)
        sent[size:, :] = block.astype(sent.dtype)
    get_signs.wait()
    signs = [(2 * signs_mem[me * heads + h] - 1).astype(jnp.float32) for h in range(heads)]
    for k in range(PIECES):
        if pieces:
            pieces[k].wait()
        c, first = k * step // size, k * step % size // ROWS

        @pl.loop(first, first + step // ROWS)
        def _(i):
            mix_rows(part, heads, c, i, size, signs, attn, outs[c])


def mix(attn, me, signs, gain, part, colors, count):
    rows, cols = attn.shape
    shape = (rows // colors, cols // 4 * len(QUARTERS[part]))
    riding = part == RIDE
    ride = -(-count // 2 * (gain.shape[0] // shape[1]) // ROWS) * ROWS
    outs = []
    for c in range(colors):
        sent = (shape[0] + ride * (riding and c == 0), shape[1])
        outs.append((sent, jnp.bfloat16, whole(sent)))
    kinds = [jax.ShapeDtypeStruct] * len(outs)
    specs, args = [IN_VMEM if part else IN_PLACE, IN_PLACE], [attn if part else in_hbm(attn), in_hbm(signs)]
    scratch = [pltpu.SMEM(signs.shape, signs.dtype)]
    if part == 0:
        outs.append((attn.shape, attn.dtype, IN_VMEM))
        kinds.append(pltpu.VMEM)
    if riding:
        specs.append(IN_PLACE)
        args.append(in_hbm(gain))
        scratch.append(pltpu.VMEM(gain.shape, gain.dtype))
    scratch.append(pltpu.SemaphoreType.DMA((2 + PIECES,)))
    return call(
        functools.partial(mix_kernel, part, cols // HD),
        1,
        [me],
        specs,
        args,
        outs,
        cost(6 * attn.size, 5 * attn.size),
        scratch,
        kinds,
    )


def load_kernel(tbl_ref, w_hbm, out, sem):
    depth, width = out.shape
    count, loads = sem.shape
    step, span = depth // loads, width // count
    copies = []
    for d in range(count):
        cols = pl.ds(pl.multiple_of(tbl_ref[d] * span, span), span)
        for k in range(loads):
            rows = pl.ds(k * step, step)
            to = out.at[rows, pl.ds(d * span, span)]
            copies.append(pltpu.make_async_copy(w_hbm.at[rows, cols], to, sem.at[d, k]))
    for copy in copies:
        copy.start()
    for copy in copies:
        copy.wait()


def load(w, tbl, width, flops=0):
    count = tbl.shape[0]
    return call(
        load_kernel,
        1,
        [tbl],
        [IN_PLACE],
        [in_hbm(w)],
        [((w.shape[0], count * width), w.dtype, IN_VMEM)],
        cost(flops, 0),
        [pltpu.SemaphoreType.DMA((count, LOADS))],
        [pltpu.VMEM],
    )[0]


def combine(order, me, own, recvs, rows):
    v = own[rows, :].astype(jnp.float32)
    for bit, recv in zip(order, recvs):
        flip = (1 - 2 * (me >> bit & 1)).astype(jnp.float32)
        v = recv[rows, :].astype(jnp.float32) + flip * v
    return v


def combine_into(out, orders, scale, me, size, ins):
    per = len(ins) // len(orders)
    for c, order in enumerate(orders):
        own, *recvs = ins[c * per : (c + 1) * per]

        @pl.loop(0, size // ROWS, unroll=UNROLL)
        def _(i):
            rows = pl.ds(pl.multiple_of(i * ROWS, ROWS), ROWS)
            to = pl.ds(pl.multiple_of(c * size + i * ROWS, ROWS), ROWS)
            out[to, :] = (combine(order, me, own, recvs, rows) * scale).astype(out.dtype)


def stage_kernel(order, size, ride, ride_rows, me_ref, *refs):
    riders, ins, out = refs[:ride], refs[ride:-1], refs[-1]
    combine_into(out, [order], 1.0, me_ref[0], size, ins)
    if ride:
        shape = (out.shape[0] - size, out.shape[1])
        row = lax.broadcasted_iota(jnp.int32, shape, 0)
        known = ride_rows
        block = riders[0][size:, :].astype(jnp.float32)
        for rider in riders[1:]:
            more = pltpu.roll(rider[size:, :].astype(jnp.float32), known, 0)
            block = jnp.where(row < known, block, more)
            known *= 2
        out[size:, :] = block.astype(out.dtype)


def stage(block, order, me, size, riders=(), ride_rows=0):
    flat = [*riders, *block]
    shape = riders[0].shape if riders else (size, block[0].shape[1])
    return call(
        functools.partial(stage_kernel, order, size, len(riders), ride_rows),
        1,
        [me],
        [whole(f.shape) for f in flat],
        flat,
        [(shape, jnp.bfloat16, whole(shape))],
        cost(4 * block[0].size * len(flat), 2 * block[0].size * (len(flat) + 2)),
    )[0]


def send_lists(order):
    lists = []
    for s, bit in enumerate(order):
        members = [1 << bit]
        for later in reversed(order[s + 1 :]):
            members = members + [m | 1 << later for m in members]
        lists.append(members)
    return lists + [[0]]


def project_kernel(plan, pieces, counts, adds, width, orders, scale, me_ref, *refs):
    added, refs = refs[: sum(adds)], refs[sum(adds) :]
    raws, rots = refs[: counts[0]], refs[counts[0] : sum(counts)]
    slab, outs = refs[sum(counts)], refs[sum(counts) + 1 :]
    if raws:
        size = outs[-1].shape[0] // len(orders)
        combine_into(outs[-1], orders, scale, me_ref[0], size, raws)
        rots = [outs[-1]]
    for step, (out, lead, add, add_lead) in enumerate(plan):
        acc = None
        for rot, (row, depth) in zip(rots, pieces):
            term = jnp.dot(
                rot[...],
                slab[row : row + depth, step * width : (step + 1) * width],
                preferred_element_type=jnp.float32,
            )
            acc = term if acc is None else acc + term
        if add is not None:
            first = sum(adds[:add])
            more = [a[add_lead].astype(jnp.float32) for a in added[first : first + adds[add]]]
            acc = acc + (more[0] if len(more) == 1 else jnp.concatenate(more, axis=1))
        outs[out][lead] = acc.astype(outs[out].dtype)


def project(
    rows, rots, slab, pieces, spans, width, dtypes, me, adds=(), leads=None, raws=(), orders=(), scale=1.0
):
    plan = [(k, n) for k, (_, count) in enumerate(spans) for n in range(count)]
    if leads is None:
        leads = plan if adds else [(None, None)] * len(plan)
    plan = [(*to, *add) for to, add in zip(plan, leads)]
    flat = [r for raw in raws for r in raw]
    args = [*[a for add in adds for a in add], *flat, *rots, slab]
    counts = [len(flat), len(rots)]
    shapes = [((n, rows, width), dtype) for (_, n), dtype in zip(spans, dtypes)]
    if raws:
        shapes.append(((rows, flat[0].shape[1]), jnp.bfloat16))
    return call(
        functools.partial(
            project_kernel, plan, pieces, counts, [len(a) for a in adds], width, orders, scale
        ),
        1,
        [me],
        [IN_VMEM] * len(args),
        args,
        [(shape, dtype, whole(shape)) for shape, dtype in shapes],
        cost(PROJECT_FLOPS, 0),
    )


def close_kernel(colors, residual, exps, *refs):
    terms, out = refs[:-1], refs[-1]
    per = len(terms) // colors
    width = residual.shape[1] // colors
    for c in range(colors):
        cols = pl.ds(c * width, width)
        own, *recvs = terms[c * per : (c + 1) * per]
        acc = own[0].astype(jnp.float32)
        for recv in recvs:
            acc = acc + recv[0].astype(jnp.float32)
        acc = acc * jnp.exp2(exps[:, cols].astype(jnp.float32))
        out[c] = (residual[:, cols].astype(jnp.float32) + acc).astype(jnp.bfloat16)


def close(residual, exps, terms, at):
    colors = len(terms)
    _, rows, width = terms[0][0].shape
    span = width * colors
    flat = [t for color in terms for t in color]
    shape = (colors, rows, width)
    return call(
        functools.partial(close_kernel, colors),
        1,
        [],
        [
            pl.BlockSpec((rows, span), lambda i: (0, at)),
            pl.BlockSpec((1, span), lambda i: (0, at)),
        ]
        + [whole((1, rows, width))] * len(flat),
        [residual, exps, *flat],
        [(shape, jnp.bfloat16, whole(shape))],
        cost(10 * rows * span, 2 * rows * width * (len(flat) + 2 * colors)),
    )[0]


def kv_kernel(plan, gain_at, counts, colors, has_prev, channels, at, span, tbl_ref, *refs):
    prevs, w, refs = refs[: 2 * has_prev], refs[2 * has_prev], refs[2 * has_prev + 1 :]
    xs, riders, rest = refs[: counts[0]], refs[counts[0] : sum(counts)], refs[sum(counts) :]
    rows, cols = xs[0].shape[-2], w.shape[1]
    product = prevs[0][...] if has_prev else jnp.zeros((rows, cols), jnp.float32)
    square = prevs[1][...] if has_prev else jnp.zeros((rows, HD), jnp.float32)
    for step, blocks in enumerate(plan):
        rider, row = gain_at[step]
        rider = riders[rider]
        for k, lead, c in blocks:
            hidden = xs[k][lead].astype(jnp.float32)
            depth = hidden.shape[1]
            part, col = divmod(at * span + c * depth, rider.shape[1])
            gain = rider[rows // colors :, col : col + depth].astype(jnp.float32)
            gain = gain[row + part : row + part + 1]
            scaled = (hidden * gain).astype(jnp.bfloat16)
            first = pl.multiple_of((tbl_ref[step] + at) * span + c * depth, depth)
            product = product + jnp.dot(
                scaled, w[pl.ds(first, depth), :], preferred_element_type=jnp.float32
            )
            hidden = hidden * hidden
            for b in range(depth // HD):
                square = square + hidden[:, b * HD : (b + 1) * HD]
    if channels:
        exps, out = rest
        mean = jnp.sum(square, axis=1, keepdims=True) / channels
        scale = jnp.exp2(exps[...].astype(jnp.float32))
        out[...] = (product * lax.rsqrt(mean + EPS) * scale).astype(out.dtype)
    else:
        rest[0][...], rest[1][...] = product, square


def kv_step(plan, arrays, riders, gain_at, colors, w_kv, tbl, at, span, prev, exps, channels):
    used = sorted({k for blocks in plan for k, _, _ in blocks})
    xs = [arrays[k] for k in used]
    plan = [[(used.index(k), lead, c) for k, lead, c in blocks] for blocks in plan]
    rows = xs[0].shape[1]
    cols = w_kv.shape[1]
    extra = []
    if channels:
        extra.append(exps)
        outs = [((rows, cols), jnp.bfloat16)]
    else:
        outs = [((rows, cols), jnp.float32), ((rows, HD), jnp.float32)]
    args = [*(prev or ()), w_kv, *xs, *riders, *extra]
    counts = [len(xs), len(riders)]
    return call(
        functools.partial(
            kv_kernel, plan, gain_at, counts, colors, prev is not None, channels, at, span
        ),
        1,
        [tbl],
        [IN_VMEM] * len(args),
        args,
        [(shape, dtype, whole(shape)) for shape, dtype in outs],
        cost(
            2 * rows * span * cols * len(plan), 2 * span * (rows + cols) * len(plan) + 4 * rows * cols
        ),
    )


def gather(x, orders, count):
    colors = x.shape[0]
    arrays, where = [x], {0: [(0, c) for c in range(colors)]}
    levels = len(orders[0])
    for bit in range(levels):
        arrays.append(swap(x, bit, count))
        where[1 << bit] = [(len(arrays) - 1, c) for c in range(colors)]
    for size in range(2, levels + 1):
        for r in range(count):
            if r.bit_count() == size:
                where[r] = []
                for c, order in enumerate(orders):
                    hop = max((b for b in range(levels) if r >> b & 1), key=order.index)
                    k, at = where[r ^ 1 << hop][c]
                    arrays.append(swap(arrays[k][at : at + 1], hop, count))
                    where[r].append((len(arrays) - 1, 0))
    plan = [[(k, at, c) for c, (k, at) in enumerate(blocks)] for blocks in where.values()]
    return arrays, list(zip(where, plan))


def body(attn_out, head_signs, w_out, out_exp, residual, norm_gain, w_kv, kv_exp):
    count = lax.axis_size("tensor")
    levels = count.bit_length() - 1
    me = lax.axis_index("tensor").astype(jnp.int32)
    odd = lax.axis_index("dp") % 2 == 1
    me_arr = me.reshape(1)
    by = levels // 2
    unturned = (me >> by | me << levels - by) & count - 1
    logical = jnp.where(odd, unturned, me).reshape(1)
    depth, (tokens, local) = w_out.shape[0], residual.shape
    channels = local * count
    orders = [list(range(levels))]
    orders.append(orders[0][levels // 2 :] + orders[0][: levels // 2])
    colors = len(orders)
    half = local // HALVES
    wide = half // colors

    def devices(rel):
        far = jnp.array([turned(r, levels) for r in rel], jnp.int32)
        return me ^ jnp.where(odd, far, jnp.array(rel, jnp.int32))

    lists = [send_lists(order) for order in orders]

    def blocks_of(stages, v):
        spans, rel, color = [], [], []
        for s in stages:
            for c in range(colors):
                spans.append((len(rel), len(lists[c][s])))
                rel += lists[c][s]
                color += [v * colors + c] * len(lists[c][s])
        return devices(rel) * (local // wide) + jnp.array(color, jnp.int32), spans

    later = range(1, levels + 1)
    first_tbls = [blocks_of([0], v)[0] for v in range(HALVES)]
    rest_tbls = [blocks_of(later, v)[0] for v in range(HALVES)]
    first_spans, rest_spans = blocks_of([0], 0)[1], blocks_of(later, 0)[1]

    exps = out_exp.reshape(1, -1)
    kv_exps = kv_exp.reshape(1, -1)

    blocks, riders = [], []
    attn = attn_out
    for p in range(len(QUARTERS)):
        gate = after(me_arr, *slabs) if p else me_arr
        mixed = mix(attn, gate, head_signs, norm_gain, p, colors, count)
        if p == 0:
            attn = mixed[-1]
            slabs = [load(w_out, after(first_tbls[0], *mixed[:colors]), wide)]
        blocks.append([])
        for c, order in enumerate(orders):
            sent = mixed[c]
            blocks[p].append([sent, swap(sent, order[0], count)])
            if p == RIDE and c == 0:
                riders += [sent, blocks[p][c][1]]
    ride_rows = local // riders[0].shape[1]
    here = logical
    for s in range(1, levels):
        sends = []
        for p in range(len(QUARTERS)):
            for c, order in enumerate(orders):
                ride = p == RIDE and c == 0
                send = stage(
                    blocks[p][c], order, here, tokens // colors, riders if ride else (), ride_rows
                )
                blocks[p][c].append(swap(send, order[s], count))
                sends.append(send)
                if ride:
                    riders.append(blocks[p][c][-1])
            here = after(logical, *sends)
    slabs.append(load(w_out, after(first_tbls[1], *sends), wide, BUSY))

    gain_at, known = {0: (0, 0)}, [0]
    for t, bit in enumerate(orders[0]):
        gain_at.update({r ^ 1 << bit: (t + 1, ride_rows * k) for k, r in enumerate(known)})
        known += [r ^ 1 << bit for r in known]

    bf16, f32 = jnp.bfloat16, jnp.float32
    cut = blocks[0][0][0].shape[1]
    pieces = [(0, cut), (cut, depth - cut)]
    scale = head_signs.shape[0] ** -0.5
    *prevs, rot = project(
        tokens, [], slabs[0], pieces[:1], first_spans, wide, [f32] * colors, after(logical, slabs[1]),
        raws=blocks[0], orders=orders, scale=scale,
    )
    rots = [rot]
    *sends, rot = project(
        tokens, [], slabs[0], pieces[1:], first_spans, wide, [bf16] * colors, logical,
        [[p] for p in prevs], raws=blocks[1], orders=orders, scale=scale,
    )
    rots.append(rot)
    received = []
    for v in range(HALVES):
        if v:
            sends = project(
                tokens, rots, slabs[v], pieces, first_spans, wide, [bf16] * colors, logical
            )
        received.append([swap(send, order[0], count) for send, order in zip(sends, orders)])

    leads = []
    for s in later:
        for c in range(colors):
            n = len(lists[c][s])
            leads += [(c, k + n * (s < levels)) for k in range(n)]
    dtypes = [bf16 if s == 1 and levels > 1 else f32 for s in later for _ in range(colors)]

    def keys_and_values(run, running, last):
        v, arrays, run = run
        return kv_step(
            [plan for _, plan in run],
            arrays,
            riders,
            [gain_at[r] for r, _ in run],
            colors,
            w_kv,
            devices([r for r, _ in run]) * HALVES,
            v,
            half,
            running,
            kv_exps,
            channels * last,
        )

    resids, runs, running = [], [], None
    for v in range(HALVES):
        adds = [[r] for r in received[v]]
        slab = load(w_out, after(rest_tbls[v], *sends), wide)
        parts = project(
            tokens, rots, slab, pieces, rest_spans, wide, dtypes, logical, adds, leads
        )
        sends = parts[:colors]
        terms = []
        for c, order in enumerate(orders):
            recvs = []
            for s in range(1, levels):
                send = parts[(s - 1) * colors + c]
                if recvs:
                    size = send.shape[0]
                    for recv in recvs:
                        send = send + recv[size : 2 * size].astype(f32)
                    send = send.astype(bf16)
                recvs.append(swap(send, order[s], count))
            terms.append([parts[(levels - 1) * colors + c], *recvs])
        out = close(residual, exps, terms, v)
        resids += list(out)
        arrays, found = gather(out, orders, count)
        for far in (False, True):
            run = [b for b in found if (b[0].bit_count() > 1) == far]
            if run and not far:
                running = keys_and_values((v, arrays, run), running, False)
            elif run:
                runs.append((v, arrays, run))

    for k, run in enumerate(runs):
        running = keys_and_values(run, running, k == len(runs) - 1)
    return jnp.concatenate(resids, axis=1), running[0]


def solution(mesh):
    placed = (
        P("dp", "tensor"),
        P(),
        P("tensor", None),
        P("tensor"),
        P("dp", "tensor"),
        P("tensor"),
        P(None, "tensor"),
        P("tensor"),
    )
    return jax.shard_map(
        body,
        mesh=mesh,
        in_specs=placed,
        out_specs=(P("dp", "tensor"), P("dp", "tensor")),
        check_vma=False,
    )
```

```python
import functools

import jax
import jax.numpy as jnp
from jax import lax
from jax.experimental import pallas as pl
from jax.experimental.pallas import tpu as pltpu
from jax.sharding import PartitionSpec as P

HD = 128
EPS = 1e-05
QUARTERS = ((0, 1, 2), (3,))
RIDE = 1
HALVES = 2
PIECES = 4
LOADS = 4
ROWS = 16
UNROLL = 2
VMEM = 4 * 1024 * 1024
PROJECT_FLOPS = 1e6
BUSY = 4e9


def cost(flops, nbytes):
    return pl.CostEstimate(flops=int(flops), bytes_accessed=int(nbytes), transcendentals=0)


def call(kernel, grid, scalars, in_specs, args, outs, estimate, scratch=(), kinds=None):
    kinds = kinds or [jax.ShapeDtypeStruct] * len(outs)
    return pl.pallas_call(
        kernel,
        grid_spec=pltpu.PrefetchScalarGridSpec(
            num_scalar_prefetch=len(scalars),
            grid=(grid,),
            in_specs=in_specs,
            out_specs=[spec for _, _, spec in outs],
            scratch_shapes=list(scratch),
        ),
        out_shape=[kind(shape, dtype) for (shape, dtype, _), kind in zip(outs, kinds)],
        compiler_params=pltpu.CompilerParams(vmem_limit_bytes=VMEM),
        cost_estimate=estimate,
    )(*scalars, *args)


def whole(shape):
    return pl.BlockSpec(shape, lambda *_: (0,) * len(shape))


IN_PLACE = pl.BlockSpec(memory_space=pl.ANY)
IN_VMEM = pl.BlockSpec(memory_space=pltpu.VMEM)


def in_hbm(array):
    return pltpu.with_memory_space_constraint(array, pltpu.HBM)


def after(value, *others):
    return lax.optimization_barrier((value, *others))[0]


def turned(bits, levels):
    by = levels // 2
    return (bits << by | bits >> levels - by) & (1 << levels) - 1


def swap(block, bit, count):
    levels = count.bit_length() - 1
    masks = (1 << bit, turned(1 << bit, levels))
    route = [
        (d * count + i, d * count + (i ^ masks[d % 2]))
        for d in range(lax.axis_size("dp"))
        for i in range(count)
    ]
    return lax.ppermute(block, ("dp", "tensor"), route)


def mix_rows(part, heads, c, i, size, signs, attn, sent):
    quarter = heads // 4
    at = pl.ds(pl.multiple_of(c * size + i * ROWS, ROWS), ROWS)
    rows = pl.ds(pl.multiple_of(i * ROWS, ROWS), ROWS)

    def head(h):
        return attn[at, pl.ds(h * HD, HD)].astype(jnp.float32) * signs[h]

    mixed = [[] for _ in QUARTERS[part]]
    for h in range(quarter):
        a, b, c2, d = [head(q * quarter + h) for q in range(4)]
        upper, lower = (a + c2, b + d), (a - c2, b - d)
        for k, q in enumerate(QUARTERS[part]):
            one, two = lower if q & 2 else upper
            mixed[k].append(one - two if q & 1 else one + two)
    for k, v in enumerate(mixed):
        step = 1
        while step < quarter:
            for lo in range(quarter):
                if not lo & step:
                    a, b = v[lo], v[lo | step]
                    v[lo], v[lo | step] = a + b, a - b
            step *= 2
        for h in range(quarter):
            cols = pl.ds((k * quarter + h) * HD, HD)
            sent[rows, cols] = v[h].astype(sent.dtype)


def mix_kernel(part, heads, me_ref, *refs):
    ride = part == RIDE
    attn, signs_ref, *refs = refs
    gain_hbm, *refs = refs if ride else (None, *refs)
    *outs, sem = refs
    gain, outs = (outs[-1], outs[:-1]) if ride else (None, outs)
    signs_mem, outs = outs[-1], outs[:-1]
    me = me_ref[0]
    get_signs = pltpu.make_async_copy(signs_ref, signs_mem, sem.at[0])
    get_signs.start()
    step = attn.shape[0] // PIECES
    pieces = []
    if part == 0:
        attn_hbm, attn, outs = attn, outs[-1], outs[:-1]
        for k in range(PIECES):
            rows = pl.ds(k * step, step)
            pieces.append(
                pltpu.make_async_copy(attn_hbm.at[rows, :], attn.at[rows, :], sem.at[2 + k])
            )
            pieces[k].start()
    size = attn.shape[0] // len(outs)
    if ride:
        get_gain = pltpu.make_async_copy(gain_hbm, gain, sem.at[1])
        get_gain.start()
        get_gain.wait()
        sent = outs[0]
        shape = (sent.shape[0] - size, sent.shape[1])
        row = lax.broadcasted_iota(jnp.int32, shape, 0)
        block = jnp.zeros(shape, jnp.float32)
        for k in range(gain.shape[0] // shape[1]):
            piece = gain[pl.ds(k * shape[1], shape[1])].astype(jnp.float32)
            block = jnp.where(row == k, jnp.broadcast_to(piece[None, :], shape), block)
        sent[size:, :] = block.astype(sent.dtype)
    get_signs.wait()
    signs = [(2 * signs_mem[me * heads + h] - 1).astype(jnp.float32) for h in range(heads)]
    for k in range(PIECES):
        if pieces:
            pieces[k].wait()
        c, first = k * step // size, k * step % size // ROWS

        @pl.loop(first, first + step // ROWS)
        def _(i):
            mix_rows(part, heads, c, i, size, signs, attn, outs[c])


def mix(attn, me, signs, gain, part, colors, count):
    rows, cols = attn.shape
    shape = (rows // colors, cols // 4 * len(QUARTERS[part]))
    riding = part == RIDE
    ride = -(-count // 2 * (gain.shape[0] // shape[1]) // ROWS) * ROWS
    outs = []
    for c in range(colors):
        sent = (shape[0] + ride * (riding and c == 0), shape[1])
        outs.append((sent, jnp.bfloat16, whole(sent)))
    kinds = [jax.ShapeDtypeStruct] * len(outs)
    specs, args = [IN_VMEM if part else IN_PLACE, IN_PLACE], [attn if part else in_hbm(attn), in_hbm(signs)]
    scratch = [pltpu.SMEM(signs.shape, signs.dtype)]
    if part == 0:
        outs.append((attn.shape, attn.dtype, IN_VMEM))
        kinds.append(pltpu.VMEM)
    if riding:
        specs.append(IN_PLACE)
        args.append(in_hbm(gain))
        scratch.append(pltpu.VMEM(gain.shape, gain.dtype))
    scratch.append(pltpu.SemaphoreType.DMA((2 + PIECES,)))
    return call(
        functools.partial(mix_kernel, part, cols // HD),
        1,
        [me],
        specs,
        args,
        outs,
        cost(6 * attn.size, 5 * attn.size),
        scratch,
        kinds,
    )


def load_kernel(tbl_ref, w_hbm, out, sem):
    depth, width = out.shape
    count, loads = sem.shape
    step, span = depth // loads, width // count
    copies = []
    for d in range(count):
        cols = pl.ds(pl.multiple_of(tbl_ref[d] * span, span), span)
        for k in range(loads):
            rows = pl.ds(k * step, step)
            to = out.at[rows, pl.ds(d * span, span)]
            copies.append(pltpu.make_async_copy(w_hbm.at[rows, cols], to, sem.at[d, k]))
    for copy in copies:
        copy.start()
    for copy in copies:
        copy.wait()


def load(w, tbl, width, flops=0):
    count = tbl.shape[0]
    return call(
        load_kernel,
        1,
        [tbl],
        [IN_PLACE],
        [in_hbm(w)],
        [((w.shape[0], count * width), w.dtype, IN_VMEM)],
        cost(flops, 0),
        [pltpu.SemaphoreType.DMA((count, LOADS))],
        [pltpu.VMEM],
    )[0]


def combine(order, me, own, recvs, rows):
    v = own[rows, :].astype(jnp.float32)
    for bit, recv in zip(order, recvs):
        flip = (1 - 2 * (me >> bit & 1)).astype(jnp.float32)
        v = recv[rows, :].astype(jnp.float32) + flip * v
    return v


def combine_into(out, orders, scale, me, size, ins):
    per = len(ins) // len(orders)
    for c, order in enumerate(orders):
        own, *recvs = ins[c * per : (c + 1) * per]

        @pl.loop(0, size // ROWS, unroll=UNROLL)
        def _(i):
            rows = pl.ds(pl.multiple_of(i * ROWS, ROWS), ROWS)
            to = pl.ds(pl.multiple_of(c * size + i * ROWS, ROWS), ROWS)
            out[to, :] = (combine(order, me, own, recvs, rows) * scale).astype(out.dtype)


def stage_kernel(order, size, ride, ride_rows, me_ref, *refs):
    riders, ins, out = refs[:ride], refs[ride:-1], refs[-1]
    combine_into(out, [order], 1.0, me_ref[0], size, ins)
    if ride:
        shape = (out.shape[0] - size, out.shape[1])
        row = lax.broadcasted_iota(jnp.int32, shape, 0)
        known = ride_rows
        block = riders[0][size:, :].astype(jnp.float32)
        for rider in riders[1:]:
            more = pltpu.roll(rider[size:, :].astype(jnp.float32), known, 0)
            block = jnp.where(row < known, block, more)
            known *= 2
        out[size:, :] = block.astype(out.dtype)


def stage(block, order, me, size, riders=(), ride_rows=0):
    flat = [*riders, *block]
    shape = riders[0].shape if riders else (size, block[0].shape[1])
    return call(
        functools.partial(stage_kernel, order, size, len(riders), ride_rows),
        1,
        [me],
        [whole(f.shape) for f in flat],
        flat,
        [(shape, jnp.bfloat16, whole(shape))],
        cost(4 * block[0].size * len(flat), 2 * block[0].size * (len(flat) + 2)),
    )[0]


def send_lists(order):
    lists = []
    for s, bit in enumerate(order):
        members = [1 << bit]
        for later in reversed(order[s + 1 :]):
            members = members + [m | 1 << later for m in members]
        lists.append(members)
    return lists + [[0]]


def project_kernel(plan, pieces, counts, adds, width, orders, scale, me_ref, *refs):
    added, refs = refs[: sum(adds)], refs[sum(adds) :]
    raws, rots = refs[: counts[0]], refs[counts[0] : sum(counts)]
    slab, outs = refs[sum(counts)], refs[sum(counts) + 1 :]
    if raws:
        size = outs[-1].shape[0] // len(orders)
        combine_into(outs[-1], orders, scale, me_ref[0], size, raws)
        rots = [outs[-1]]
    for step, (out, lead, add, add_lead) in enumerate(plan):
        acc = None
        for rot, (row, depth) in zip(rots, pieces):
            term = jnp.dot(
                rot[...],
                slab[row : row + depth, step * width : (step + 1) * width],
                preferred_element_type=jnp.float32,
            )
            acc = term if acc is None else acc + term
        if add is not None:
            first = sum(adds[:add])
            more = [a[add_lead].astype(jnp.float32) for a in added[first : first + adds[add]]]
            acc = acc + (more[0] if len(more) == 1 else jnp.concatenate(more, axis=1))
        outs[out][lead] = acc.astype(outs[out].dtype)


def project(
    rows, rots, slab, pieces, spans, width, dtypes, me, adds=(), leads=None, raws=(), orders=(), scale=1.0
):
    plan = [(k, n) for k, (_, count) in enumerate(spans) for n in range(count)]
    if leads is None:
        leads = plan if adds else [(None, None)] * len(plan)
    plan = [(*to, *add) for to, add in zip(plan, leads)]
    flat = [r for raw in raws for r in raw]
    args = [*[a for add in adds for a in add], *flat, *rots, slab]
    counts = [len(flat), len(rots)]
    shapes = [((n, rows, width), dtype) for (_, n), dtype in zip(spans, dtypes)]
    if raws:
        shapes.append(((rows, flat[0].shape[1]), jnp.bfloat16))
    return call(
        functools.partial(
            project_kernel, plan, pieces, counts, [len(a) for a in adds], width, orders, scale
        ),
        1,
        [me],
        [IN_VMEM] * len(args),
        args,
        [(shape, dtype, whole(shape)) for shape, dtype in shapes],
        cost(PROJECT_FLOPS, 0),
    )


def close_kernel(colors, residual, exps, *refs):
    terms, out = refs[:-1], refs[-1]
    per = len(terms) // colors
    width = residual.shape[1] // colors
    for c in range(colors):
        cols = pl.ds(c * width, width)
        own, *recvs = terms[c * per : (c + 1) * per]
        acc = own[0].astype(jnp.float32)
        for recv in recvs:
            acc = acc + recv[0].astype(jnp.float32)
        acc = acc * jnp.exp2(exps[:, cols].astype(jnp.float32))
        out[c] = (residual[:, cols].astype(jnp.float32) + acc).astype(jnp.bfloat16)


def close(residual, exps, terms, at):
    colors = len(terms)
    _, rows, width = terms[0][0].shape
    span = width * colors
    flat = [t for color in terms for t in color]
    shape = (colors, rows, width)
    return call(
        functools.partial(close_kernel, colors),
        1,
        [],
        [
            pl.BlockSpec((rows, span), lambda i: (0, at)),
            pl.BlockSpec((1, span), lambda i: (0, at)),
        ]
        + [whole((1, rows, width))] * len(flat),
        [residual, exps, *flat],
        [(shape, jnp.bfloat16, whole(shape))],
        cost(10 * rows * span, 2 * rows * width * (len(flat) + 2 * colors)),
    )[0]


def kv_kernel(plan, gain_at, counts, colors, has_prev, channels, at, span, tbl_ref, *refs):
    prevs, w, refs = refs[: 2 * has_prev], refs[2 * has_prev], refs[2 * has_prev + 1 :]
    xs, riders, rest = refs[: counts[0]], refs[counts[0] : sum(counts)], refs[sum(counts) :]
    rows, cols = xs[0].shape[-2], w.shape[1]
    product = prevs[0][...] if has_prev else jnp.zeros((rows, cols), jnp.float32)
    square = prevs[1][...] if has_prev else jnp.zeros((rows, HD), jnp.float32)
    for step, blocks in enumerate(plan):
        rider, row = gain_at[step]
        rider = riders[rider]
        for k, lead, c in blocks:
            hidden = xs[k][lead].astype(jnp.float32)
            depth = hidden.shape[1]
            part, col = divmod(at * span + c * depth, rider.shape[1])
            gain = rider[rows // colors :, col : col + depth].astype(jnp.float32)
            gain = gain[row + part : row + part + 1]
            scaled = (hidden * gain).astype(jnp.bfloat16)
            first = pl.multiple_of((tbl_ref[step] + at) * span + c * depth, depth)
            product = product + jnp.dot(
                scaled, w[pl.ds(first, depth), :], preferred_element_type=jnp.float32
            )
            hidden = hidden * hidden
            for b in range(depth // HD):
                square = square + hidden[:, b * HD : (b + 1) * HD]
    if channels:
        exps, out = rest
        mean = jnp.sum(square, axis=1, keepdims=True) / channels
        scale = jnp.exp2(exps[...].astype(jnp.float32))
        out[...] = (product * lax.rsqrt(mean + EPS) * scale).astype(out.dtype)
    else:
        rest[0][...], rest[1][...] = product, square


def kv_step(plan, arrays, riders, gain_at, colors, w_kv, tbl, at, span, prev, exps, channels):
    used = sorted({k for blocks in plan for k, _, _ in blocks})
    xs = [arrays[k] for k in used]
    plan = [[(used.index(k), lead, c) for k, lead, c in blocks] for blocks in plan]
    rows = xs[0].shape[1]
    cols = w_kv.shape[1]
    extra = []
    if channels:
        extra.append(exps)
        outs = [((rows, cols), jnp.bfloat16)]
    else:
        outs = [((rows, cols), jnp.float32), ((rows, HD), jnp.float32)]
    args = [*(prev or ()), w_kv, *xs, *riders, *extra]
    counts = [len(xs), len(riders)]
    return call(
        functools.partial(
            kv_kernel, plan, gain_at, counts, colors, prev is not None, channels, at, span
        ),
        1,
        [tbl],
        [IN_VMEM] * len(args),
        args,
        [(shape, dtype, whole(shape)) for shape, dtype in outs],
        cost(
            2 * rows * span * cols * len(plan), 2 * span * (rows + cols) * len(plan) + 4 * rows * cols
        ),
    )


def gather(x, orders, count):
    colors = x.shape[0]
    arrays, where = [x], {0: [(0, c) for c in range(colors)]}
    levels = len(orders[0])
    for bit in range(levels):
        arrays.append(swap(x, bit, count))
        where[1 << bit] = [(len(arrays) - 1, c) for c in range(colors)]
    for size in range(2, levels + 1):
        for r in range(count):
            if r.bit_count() == size:
                where[r] = []
                for c, order in enumerate(orders):
                    hop = max((b for b in range(levels) if r >> b & 1), key=order.index)
                    k, at = where[r ^ 1 << hop][c]
                    arrays.append(swap(arrays[k][at : at + 1], hop, count))
                    where[r].append((len(arrays) - 1, 0))
    plan = [[(k, at, c) for c, (k, at) in enumerate(blocks)] for blocks in where.values()]
    return arrays, list(zip(where, plan))


def body(attn_out, head_signs, w_out, out_exp, residual, norm_gain, w_kv, kv_exp):
    count = lax.axis_size("tensor")
    levels = count.bit_length() - 1
    me = lax.axis_index("tensor").astype(jnp.int32)
    odd = lax.axis_index("dp") % 2 == 1
    me_arr = me.reshape(1)
    by = levels // 2
    unturned = (me >> by | me << levels - by) & count - 1
    logical = jnp.where(odd, unturned, me).reshape(1)
    depth, (tokens, local) = w_out.shape[0], residual.shape
    channels = local * count
    orders = [list(range(levels))]
    orders.append(orders[0][levels // 2 :] + orders[0][: levels // 2])
    colors = len(orders)
    half = local // HALVES
    wide = half // colors

    def devices(rel):
        far = jnp.array([turned(r, levels) for r in rel], jnp.int32)
        return me ^ jnp.where(odd, far, jnp.array(rel, jnp.int32))

    lists = [send_lists(order) for order in orders]

    def blocks_of(stages, v):
        spans, rel, color = [], [], []
        for s in stages:
            for c in range(colors):
                spans.append((len(rel), len(lists[c][s])))
                rel += lists[c][s]
                color += [v * colors + c] * len(lists[c][s])
        return devices(rel) * (local // wide) + jnp.array(color, jnp.int32), spans

    later = range(1, levels + 1)
    first_tbls = [blocks_of([0], v)[0] for v in range(HALVES)]
    rest_tbls = [blocks_of(later, v)[0] for v in range(HALVES)]
    first_spans, rest_spans = blocks_of([0], 0)[1], blocks_of(later, 0)[1]

    exps = out_exp.reshape(1, -1)
    kv_exps = kv_exp.reshape(1, -1)

    blocks, riders = [], []
    attn = attn_out
    for p in range(len(QUARTERS)):
        mixed = mix(attn, me_arr, head_signs, norm_gain, p, colors, count)
        if p == 0:
            attn = mixed[-1]
        blocks.append([])
        for c, order in enumerate(orders):
            sent = mixed[c]
            blocks[p].append([sent, swap(sent, order[0], count)])
            if p == RIDE and c == 0:
                riders += [sent, blocks[p][c][1]]
    ride_rows = local // riders[0].shape[1]
    slabs = [load(w_out, after(first_tbls[0], sent), wide)]
    here = after(logical, slabs[0])
    for s in range(1, levels):
        sends = []
        for p in range(len(QUARTERS)):
            for c, order in enumerate(orders):
                ride = p == RIDE and c == 0
                send = stage(
                    blocks[p][c], order, here, tokens // colors, riders if ride else (), ride_rows
                )
                blocks[p][c].append(swap(send, order[s], count))
                sends.append(send)
                if ride:
                    riders.append(blocks[p][c][-1])
            here = after(logical, *sends)
    slabs.append(load(w_out, after(first_tbls[1], *sends), wide, BUSY))

    gain_at, known = {0: (0, 0)}, [0]
    for t, bit in enumerate(orders[0]):
        gain_at.update({r ^ 1 << bit: (t + 1, ride_rows * k) for k, r in enumerate(known)})
        known += [r ^ 1 << bit for r in known]

    bf16, f32 = jnp.bfloat16, jnp.float32
    cut = blocks[0][0][0].shape[1]
    pieces = [(0, cut), (cut, depth - cut)]
    scale = head_signs.shape[0] ** -0.5
    *prevs, rot = project(
        tokens, [], slabs[0], pieces[:1], first_spans, wide, [f32] * colors, after(logical, slabs[1]),
        raws=blocks[0], orders=orders, scale=scale,
    )
    rots = [rot]
    *sends, rot = project(
        tokens, [], slabs[0], pieces[1:], first_spans, wide, [bf16] * colors, logical,
        [[p] for p in prevs], raws=blocks[1], orders=orders, scale=scale,
    )
    rots.append(rot)
    received = []
    for v in range(HALVES):
        if v:
            sends = project(
                tokens, rots, slabs[v], pieces, first_spans, wide, [bf16] * colors, logical
            )
        received.append([swap(send, order[0], count) for send, order in zip(sends, orders)])

    leads = []
    for s in later:
        for c in range(colors):
            n = len(lists[c][s])
            leads += [(c, k + n * (s < levels)) for k in range(n)]
    dtypes = [bf16 if s == 1 and levels > 1 else f32 for s in later for _ in range(colors)]

    def keys_and_values(run, running, last):
        v, arrays, run = run
        return kv_step(
            [plan for _, plan in run],
            arrays,
            riders,
            [gain_at[r] for r, _ in run],
            colors,
            w_kv,
            devices([r for r, _ in run]) * HALVES,
            v,
            half,
            running,
            kv_exps,
            channels * last,
        )

    resids, runs, running = [], [], None
    for v in range(HALVES):
        adds = [[r] for r in received[v]]
        slab = load(w_out, after(rest_tbls[v], *sends), wide)
        parts = project(
            tokens, rots, slab, pieces, rest_spans, wide, dtypes, logical, adds, leads
        )
        sends = parts[:colors]
        terms = []
        for c, order in enumerate(orders):
            recvs = []
            for s in range(1, levels):
                send = parts[(s - 1) * colors + c]
                if recvs:
                    size = send.shape[0]
                    for recv in recvs:
                        send = send + recv[size : 2 * size].astype(f32)
                    send = send.astype(bf16)
                recvs.append(swap(send, order[s], count))
            terms.append([parts[(levels - 1) * colors + c], *recvs])
        out = close(residual, exps, terms, v)
        resids += list(out)
        arrays, found = gather(out, orders, count)
        for far in (False, True):
            run = [b for b in found if (b[0].bit_count() > 1) == far]
            if run and not far:
                running = keys_and_values((v, arrays, run), running, False)
            elif run:
                runs.append((v, arrays, run))

    for k, run in enumerate(runs):
        running = keys_and_values(run, running, k == len(runs) - 1)
    return jnp.concatenate(resids, axis=1), running[0]


def solution(mesh):
    placed = (
        P("dp", "tensor"),
        P(),
        P("tensor", None),
        P("tensor"),
        P("dp", "tensor"),
        P("tensor"),
        P(None, "tensor"),
        P("tensor"),
    )
    return jax.shard_map(
        body,
        mesh=mesh,
        in_specs=placed,
        out_specs=(P("dp", "tensor"), P("dp", "tensor")),
        check_vma=False,
    )
```

```python
import functools

import jax
import jax.numpy as jnp
from jax import lax
from jax.experimental import pallas as pl
from jax.experimental.pallas import tpu as pltpu
from jax.sharding import PartitionSpec as P

HD = 128
EPS = 1e-05
QUARTERS = ((0, 1, 2), (3,))
RIDE = 1
HALVES = 2
PIECES = 8
LOADS = 4
ROWS = 16
UNROLL = 2
VMEM = 4 * 1024 * 1024
PROJECT_FLOPS = 1e6
BUSY = 4e9


def cost(flops, nbytes):
    return pl.CostEstimate(flops=int(flops), bytes_accessed=int(nbytes), transcendentals=0)


def call(kernel, grid, scalars, in_specs, args, outs, estimate, scratch=(), kinds=None):
    kinds = kinds or [jax.ShapeDtypeStruct] * len(outs)
    return pl.pallas_call(
        kernel,
        grid_spec=pltpu.PrefetchScalarGridSpec(
            num_scalar_prefetch=len(scalars),
            grid=(grid,),
            in_specs=in_specs,
            out_specs=[spec for _, _, spec in outs],
            scratch_shapes=list(scratch),
        ),
        out_shape=[kind(shape, dtype) for (shape, dtype, _), kind in zip(outs, kinds)],
        compiler_params=pltpu.CompilerParams(vmem_limit_bytes=VMEM),
        cost_estimate=estimate,
    )(*scalars, *args)


def whole(shape):
    return pl.BlockSpec(shape, lambda *_: (0,) * len(shape))


IN_PLACE = pl.BlockSpec(memory_space=pl.ANY)
IN_VMEM = pl.BlockSpec(memory_space=pltpu.VMEM)


def in_hbm(array):
    return pltpu.with_memory_space_constraint(array, pltpu.HBM)


def after(value, *others):
    return lax.optimization_barrier((value, *others))[0]


def turned(bits, levels):
    by = levels // 2
    return (bits << by | bits >> levels - by) & (1 << levels) - 1


def swap(block, bit, count):
    levels = count.bit_length() - 1
    masks = (1 << bit, turned(1 << bit, levels))
    route = [
        (d * count + i, d * count + (i ^ masks[d % 2]))
        for d in range(lax.axis_size("dp"))
        for i in range(count)
    ]
    return lax.ppermute(block, ("dp", "tensor"), route)


def mix_rows(part, heads, c, i, size, signs, attn, sent):
    quarter = heads // 4
    at = pl.ds(pl.multiple_of(c * size + i * ROWS, ROWS), ROWS)
    rows = pl.ds(pl.multiple_of(i * ROWS, ROWS), ROWS)

    def head(h):
        return attn[at, pl.ds(h * HD, HD)].astype(jnp.float32) * signs[h]

    mixed = [[] for _ in QUARTERS[part]]
    for h in range(quarter):
        a, b, c2, d = [head(q * quarter + h) for q in range(4)]
        upper, lower = (a + c2, b + d), (a - c2, b - d)
        for k, q in enumerate(QUARTERS[part]):
            one, two = lower if q & 2 else upper
            mixed[k].append(one - two if q & 1 else one + two)
    for k, v in enumerate(mixed):
        step = 1
        while step < quarter:
            for lo in range(quarter):
                if not lo & step:
                    a, b = v[lo], v[lo | step]
                    v[lo], v[lo | step] = a + b, a - b
            step *= 2
        for h in range(quarter):
            cols = pl.ds((k * quarter + h) * HD, HD)
            sent[rows, cols] = v[h].astype(sent.dtype)


def mix_kernel(part, heads, me_ref, *refs):
    ride = part == RIDE
    attn, signs_ref, *refs = refs
    gain_hbm, *refs = refs if ride else (None, *refs)
    *outs, sem = refs
    gain, outs = (outs[-1], outs[:-1]) if ride else (None, outs)
    signs_mem, outs = outs[-1], outs[:-1]
    me = me_ref[0]
    get_signs = pltpu.make_async_copy(signs_ref, signs_mem, sem.at[0])
    get_signs.start()
    step = attn.shape[0] // PIECES
    pieces = []
    if part == 0:
        attn_hbm, attn, outs = attn, outs[-1], outs[:-1]
        for k in range(PIECES):
            rows = pl.ds(k * step, step)
            pieces.append(
                pltpu.make_async_copy(attn_hbm.at[rows, :], attn.at[rows, :], sem.at[2 + k])
            )
            pieces[k].start()
    size = attn.shape[0] // len(outs)
    if ride:
        get_gain = pltpu.make_async_copy(gain_hbm, gain, sem.at[1])
        get_gain.start()
        get_gain.wait()
        sent = outs[0]
        shape = (sent.shape[0] - size, sent.shape[1])
        row = lax.broadcasted_iota(jnp.int32, shape, 0)
        block = jnp.zeros(shape, jnp.float32)
        for k in range(gain.shape[0] // shape[1]):
            piece = gain[pl.ds(k * shape[1], shape[1])].astype(jnp.float32)
            block = jnp.where(row == k, jnp.broadcast_to(piece[None, :], shape), block)
        sent[size:, :] = block.astype(sent.dtype)
    get_signs.wait()
    signs = [(2 * signs_mem[me * heads + h] - 1).astype(jnp.float32) for h in range(heads)]
    for k in range(PIECES):
        if pieces:
            pieces[k].wait()
        c, first = k * step // size, k * step % size // ROWS

        @pl.loop(first, first + step // ROWS)
        def _(i):
            mix_rows(part, heads, c, i, size, signs, attn, outs[c])


def mix(attn, me, signs, gain, part, colors, count):
    rows, cols = attn.shape
    shape = (rows // colors, cols // 4 * len(QUARTERS[part]))
    riding = part == RIDE
    ride = -(-count // 2 * (gain.shape[0] // shape[1]) // ROWS) * ROWS
    outs = []
    for c in range(colors):
        sent = (shape[0] + ride * (riding and c == 0), shape[1])
        outs.append((sent, jnp.bfloat16, whole(sent)))
    kinds = [jax.ShapeDtypeStruct] * len(outs)
    specs, args = [IN_VMEM if part else IN_PLACE, IN_PLACE], [attn if part else in_hbm(attn), in_hbm(signs)]
    scratch = [pltpu.SMEM(signs.shape, signs.dtype)]
    if part == 0:
        outs.append((attn.shape, attn.dtype, IN_VMEM))
        kinds.append(pltpu.VMEM)
    if riding:
        specs.append(IN_PLACE)
        args.append(in_hbm(gain))
        scratch.append(pltpu.VMEM(gain.shape, gain.dtype))
    scratch.append(pltpu.SemaphoreType.DMA((2 + PIECES,)))
    return call(
        functools.partial(mix_kernel, part, cols // HD),
        1,
        [me],
        specs,
        args,
        outs,
        cost(6 * attn.size, 5 * attn.size),
        scratch,
        kinds,
    )


def load_kernel(tbl_ref, w_hbm, out, sem):
    depth, width = out.shape
    count, loads = sem.shape
    step, span = depth // loads, width // count
    copies = []
    for d in range(count):
        cols = pl.ds(pl.multiple_of(tbl_ref[d] * span, span), span)
        for k in range(loads):
            rows = pl.ds(k * step, step)
            to = out.at[rows, pl.ds(d * span, span)]
            copies.append(pltpu.make_async_copy(w_hbm.at[rows, cols], to, sem.at[d, k]))
    for copy in copies:
        copy.start()
    for copy in copies:
        copy.wait()


def load(w, tbl, width, flops=0):
    count = tbl.shape[0]
    return call(
        load_kernel,
        1,
        [tbl],
        [IN_PLACE],
        [in_hbm(w)],
        [((w.shape[0], count * width), w.dtype, IN_VMEM)],
        cost(flops, 0),
        [pltpu.SemaphoreType.DMA((count, LOADS))],
        [pltpu.VMEM],
    )[0]


def combine(order, me, own, recvs, rows):
    v = own[rows, :].astype(jnp.float32)
    for bit, recv in zip(order, recvs):
        flip = (1 - 2 * (me >> bit & 1)).astype(jnp.float32)
        v = recv[rows, :].astype(jnp.float32) + flip * v
    return v


def combine_into(out, orders, scale, me, size, ins):
    per = len(ins) // len(orders)
    for c, order in enumerate(orders):
        own, *recvs = ins[c * per : (c + 1) * per]

        @pl.loop(0, size // ROWS, unroll=UNROLL)
        def _(i):
            rows = pl.ds(pl.multiple_of(i * ROWS, ROWS), ROWS)
            to = pl.ds(pl.multiple_of(c * size + i * ROWS, ROWS), ROWS)
            out[to, :] = (combine(order, me, own, recvs, rows) * scale).astype(out.dtype)


def stage_kernel(order, size, ride, ride_rows, me_ref, *refs):
    riders, ins, out = refs[:ride], refs[ride:-1], refs[-1]
    combine_into(out, [order], 1.0, me_ref[0], size, ins)
    if ride:
        shape = (out.shape[0] - size, out.shape[1])
        row = lax.broadcasted_iota(jnp.int32, shape, 0)
        known = ride_rows
        block = riders[0][size:, :].astype(jnp.float32)
        for rider in riders[1:]:
            more = pltpu.roll(rider[size:, :].astype(jnp.float32), known, 0)
            block = jnp.where(row < known, block, more)
            known *= 2
        out[size:, :] = block.astype(out.dtype)


def stage(block, order, me, size, riders=(), ride_rows=0):
    flat = [*riders, *block]
    shape = riders[0].shape if riders else (size, block[0].shape[1])
    return call(
        functools.partial(stage_kernel, order, size, len(riders), ride_rows),
        1,
        [me],
        [whole(f.shape) for f in flat],
        flat,
        [(shape, jnp.bfloat16, whole(shape))],
        cost(4 * block[0].size * len(flat), 2 * block[0].size * (len(flat) + 2)),
    )[0]


def send_lists(order):
    lists = []
    for s, bit in enumerate(order):
        members = [1 << bit]
        for later in reversed(order[s + 1 :]):
            members = members + [m | 1 << later for m in members]
        lists.append(members)
    return lists + [[0]]


def project_kernel(plan, pieces, counts, adds, width, orders, scale, me_ref, *refs):
    added, refs = refs[: sum(adds)], refs[sum(adds) :]
    raws, rots = refs[: counts[0]], refs[counts[0] : sum(counts)]
    slab, outs = refs[sum(counts)], refs[sum(counts) + 1 :]
    if raws:
        size = outs[-1].shape[0] // len(orders)
        combine_into(outs[-1], orders, scale, me_ref[0], size, raws)
        rots = [outs[-1]]
    for step, (out, lead, add, add_lead) in enumerate(plan):
        acc = None
        for rot, (row, depth) in zip(rots, pieces):
            term = jnp.dot(
                rot[...],
                slab[row : row + depth, step * width : (step + 1) * width],
                preferred_element_type=jnp.float32,
            )
            acc = term if acc is None else acc + term
        if add is not None:
            first = sum(adds[:add])
            more = [a[add_lead].astype(jnp.float32) for a in added[first : first + adds[add]]]
            acc = acc + (more[0] if len(more) == 1 else jnp.concatenate(more, axis=1))
        outs[out][lead] = acc.astype(outs[out].dtype)


def project(
    rows, rots, slab, pieces, spans, width, dtypes, me, adds=(), leads=None, raws=(), orders=(), scale=1.0
):
    plan = [(k, n) for k, (_, count) in enumerate(spans) for n in range(count)]
    if leads is None:
        leads = plan if adds else [(None, None)] * len(plan)
    plan = [(*to, *add) for to, add in zip(plan, leads)]
    flat = [r for raw in raws for r in raw]
    args = [*[a for add in adds for a in add], *flat, *rots, slab]
    counts = [len(flat), len(rots)]
    shapes = [((n, rows, width), dtype) for (_, n), dtype in zip(spans, dtypes)]
    if raws:
        shapes.append(((rows, flat[0].shape[1]), jnp.bfloat16))
    return call(
        functools.partial(
            project_kernel, plan, pieces, counts, [len(a) for a in adds], width, orders, scale
        ),
        1,
        [me],
        [IN_VMEM] * len(args),
        args,
        [(shape, dtype, whole(shape)) for shape, dtype in shapes],
        cost(PROJECT_FLOPS, 0),
    )


def close_kernel(colors, residual, exps, *refs):
    terms, out = refs[:-1], refs[-1]
    per = len(terms) // colors
    width = residual.shape[1] // colors
    for c in range(colors):
        cols = pl.ds(c * width, width)
        own, *recvs = terms[c * per : (c + 1) * per]
        acc = own[0].astype(jnp.float32)
        for recv in recvs:
            acc = acc + recv[0].astype(jnp.float32)
        acc = acc * jnp.exp2(exps[:, cols].astype(jnp.float32))
        out[c] = (residual[:, cols].astype(jnp.float32) + acc).astype(jnp.bfloat16)


def close(residual, exps, terms, at):
    colors = len(terms)
    _, rows, width = terms[0][0].shape
    span = width * colors
    flat = [t for color in terms for t in color]
    shape = (colors, rows, width)
    return call(
        functools.partial(close_kernel, colors),
        1,
        [],
        [
            pl.BlockSpec((rows, span), lambda i: (0, at)),
            pl.BlockSpec((1, span), lambda i: (0, at)),
        ]
        + [whole((1, rows, width))] * len(flat),
        [residual, exps, *flat],
        [(shape, jnp.bfloat16, whole(shape))],
        cost(10 * rows * span, 2 * rows * width * (len(flat) + 2 * colors)),
    )[0]


def kv_kernel(plan, gain_at, counts, colors, has_prev, channels, at, span, tbl_ref, *refs):
    prevs, w, refs = refs[: 2 * has_prev], refs[2 * has_prev], refs[2 * has_prev + 1 :]
    xs, riders, rest = refs[: counts[0]], refs[counts[0] : sum(counts)], refs[sum(counts) :]
    rows, cols = xs[0].shape[-2], w.shape[1]
    product = prevs[0][...] if has_prev else jnp.zeros((rows, cols), jnp.float32)
    square = prevs[1][...] if has_prev else jnp.zeros((rows, HD), jnp.float32)
    for step, blocks in enumerate(plan):
        rider, row = gain_at[step]
        rider = riders[rider]
        for k, lead, c in blocks:
            hidden = xs[k][lead].astype(jnp.float32)
            depth = hidden.shape[1]
            part, col = divmod(at * span + c * depth, rider.shape[1])
            gain = rider[rows // colors :, col : col + depth].astype(jnp.float32)
            gain = gain[row + part : row + part + 1]
            scaled = (hidden * gain).astype(jnp.bfloat16)
            first = pl.multiple_of((tbl_ref[step] + at) * span + c * depth, depth)
            product = product + jnp.dot(
                scaled, w[pl.ds(first, depth), :], preferred_element_type=jnp.float32
            )
            hidden = hidden * hidden
            for b in range(depth // HD):
                square = square + hidden[:, b * HD : (b + 1) * HD]
    if channels:
        exps, out = rest
        mean = jnp.sum(square, axis=1, keepdims=True) / channels
        scale = jnp.exp2(exps[...].astype(jnp.float32))
        out[...] = (product * lax.rsqrt(mean + EPS) * scale).astype(out.dtype)
    else:
        rest[0][...], rest[1][...] = product, square


def kv_step(plan, arrays, riders, gain_at, colors, w_kv, tbl, at, span, prev, exps, channels):
    used = sorted({k for blocks in plan for k, _, _ in blocks})
    xs = [arrays[k] for k in used]
    plan = [[(used.index(k), lead, c) for k, lead, c in blocks] for blocks in plan]
    rows = xs[0].shape[1]
    cols = w_kv.shape[1]
    extra = []
    if channels:
        extra.append(exps)
        outs = [((rows, cols), jnp.bfloat16)]
    else:
        outs = [((rows, cols), jnp.float32), ((rows, HD), jnp.float32)]
    args = [*(prev or ()), w_kv, *xs, *riders, *extra]
    counts = [len(xs), len(riders)]
    return call(
        functools.partial(
            kv_kernel, plan, gain_at, counts, colors, prev is not None, channels, at, span
        ),
        1,
        [tbl],
        [IN_VMEM] * len(args),
        args,
        [(shape, dtype, whole(shape)) for shape, dtype in outs],
        cost(
            2 * rows * span * cols * len(plan), 2 * span * (rows + cols) * len(plan) + 4 * rows * cols
        ),
    )


def gather(x, orders, count):
    colors = x.shape[0]
    arrays, where = [x], {0: [(0, c) for c in range(colors)]}
    levels = len(orders[0])
    for bit in range(levels):
        arrays.append(swap(x, bit, count))
        where[1 << bit] = [(len(arrays) - 1, c) for c in range(colors)]
    for size in range(2, levels + 1):
        for r in range(count):
            if r.bit_count() == size:
                where[r] = []
                for c, order in enumerate(orders):
                    hop = max((b for b in range(levels) if r >> b & 1), key=order.index)
                    k, at = where[r ^ 1 << hop][c]
                    arrays.append(swap(arrays[k][at : at + 1], hop, count))
                    where[r].append((len(arrays) - 1, 0))
    plan = [[(k, at, c) for c, (k, at) in enumerate(blocks)] for blocks in where.values()]
    return arrays, list(zip(where, plan))


def body(attn_out, head_signs, w_out, out_exp, residual, norm_gain, w_kv, kv_exp):
    count = lax.axis_size("tensor")
    levels = count.bit_length() - 1
    me = lax.axis_index("tensor").astype(jnp.int32)
    odd = lax.axis_index("dp") % 2 == 1
    me_arr = me.reshape(1)
    by = levels // 2
    unturned = (me >> by | me << levels - by) & count - 1
    logical = jnp.where(odd, unturned, me).reshape(1)
    depth, (tokens, local) = w_out.shape[0], residual.shape
    channels = local * count
    orders = [list(range(levels))]
    orders.append(orders[0][levels // 2 :] + orders[0][: levels // 2])
    colors = len(orders)
    half = local // HALVES
    wide = half // colors

    def devices(rel):
        far = jnp.array([turned(r, levels) for r in rel], jnp.int32)
        return me ^ jnp.where(odd, far, jnp.array(rel, jnp.int32))

    lists = [send_lists(order) for order in orders]

    def blocks_of(stages, v):
        spans, rel, color = [], [], []
        for s in stages:
            for c in range(colors):
                spans.append((len(rel), len(lists[c][s])))
                rel += lists[c][s]
                color += [v * colors + c] * len(lists[c][s])
        return devices(rel) * (local // wide) + jnp.array(color, jnp.int32), spans

    later = range(1, levels + 1)
    first_tbls = [blocks_of([0], v)[0] for v in range(HALVES)]
    rest_tbls = [blocks_of(later, v)[0] for v in range(HALVES)]
    first_spans, rest_spans = blocks_of([0], 0)[1], blocks_of(later, 0)[1]

    exps = out_exp.reshape(1, -1)
    kv_exps = kv_exp.reshape(1, -1)

    blocks, riders = [], []
    attn = attn_out
    for p in range(len(QUARTERS)):
        mixed = mix(attn, me_arr, head_signs, norm_gain, p, colors, count)
        if p == 0:
            attn = mixed[-1]
        blocks.append([])
        for c, order in enumerate(orders):
            sent = mixed[c]
            blocks[p].append([sent, swap(sent, order[0], count)])
            if p == RIDE and c == 0:
                riders += [sent, blocks[p][c][1]]
    ride_rows = local // riders[0].shape[1]
    slabs = [load(w_out, after(first_tbls[0], sent), wide)]
    here = after(logical, slabs[0])
    for s in range(1, levels):
        sends = []
        for p in range(len(QUARTERS)):
            for c, order in enumerate(orders):
                ride = p == RIDE and c == 0
                send = stage(
                    blocks[p][c], order[s - 1 : s], here, tokens // colors, riders if ride else (), ride_rows
                )
                blocks[p][c] = [send, swap(send, order[s], count)]
                sends.append(send)
                if ride:
                    riders.append(blocks[p][c][-1])
            here = after(logical, *sends)
    slabs.append(load(w_out, after(first_tbls[1], *sends), wide, BUSY))

    gain_at, known = {0: (0, 0)}, [0]
    for t, bit in enumerate(orders[0]):
        gain_at.update({r ^ 1 << bit: (t + 1, ride_rows * k) for k, r in enumerate(known)})
        known += [r ^ 1 << bit for r in known]

    bf16, f32 = jnp.bfloat16, jnp.float32
    cut = blocks[0][0][0].shape[1]
    pieces = [(0, cut), (cut, depth - cut)]
    scale = head_signs.shape[0] ** -0.5
    closing = [order[levels - 1 :] for order in orders]
    *prevs, rot = project(
        tokens, [], slabs[0], pieces[:1], first_spans, wide, [f32] * colors, after(logical, slabs[1]),
        raws=blocks[0], orders=closing, scale=scale,
    )
    rots = [rot]
    *sends, rot = project(
        tokens, [], slabs[0], pieces[1:], first_spans, wide, [bf16] * colors, logical,
        [[p] for p in prevs], raws=blocks[1], orders=closing, scale=scale,
    )
    rots.append(rot)
    received = []
    for v in range(HALVES):
        if v:
            sends = project(
                tokens, rots, slabs[v], pieces, first_spans, wide, [bf16] * colors, logical
            )
        received.append([swap(send, order[0], count) for send, order in zip(sends, orders)])

    leads = []
    for s in later:
        for c in range(colors):
            n = len(lists[c][s])
            leads += [(c, k + n * (s < levels)) for k in range(n)]
    dtypes = [bf16 if s == 1 and levels > 1 else f32 for s in later for _ in range(colors)]

    def keys_and_values(run, running, last):
        v, arrays, run = run
        return kv_step(
            [plan for _, plan in run],
            arrays,
            riders,
            [gain_at[r] for r, _ in run],
            colors,
            w_kv,
            devices([r for r, _ in run]) * HALVES,
            v,
            half,
            running,
            kv_exps,
            channels * last,
        )

    resids, runs, running = [], [], None
    for v in range(HALVES):
        adds = [[r] for r in received[v]]
        slab = load(w_out, after(rest_tbls[v], *sends), wide)
        parts = project(
            tokens, rots, slab, pieces, rest_spans, wide, dtypes, logical, adds, leads
        )
        sends = parts[:colors]
        terms = []
        for c, order in enumerate(orders):
            recvs = []
            for s in range(1, levels):
                send = parts[(s - 1) * colors + c]
                if recvs:
                    size = send.shape[0]
                    for recv in recvs:
                        send = send + recv[size : 2 * size].astype(f32)
                    send = send.astype(bf16)
                recvs.append(swap(send, order[s], count))
            terms.append([parts[(levels - 1) * colors + c], *recvs])
        out = close(residual, exps, terms, v)
        resids += list(out)
        arrays, found = gather(out, orders, count)
        for far in (False, True):
            run = [b for b in found if (b[0].bit_count() > 1) == far]
            if run and not far:
                running = keys_and_values((v, arrays, run), running, False)
            elif run:
                runs.append((v, arrays, run))

    for k, run in enumerate(runs):
        running = keys_and_values(run, running, k == len(runs) - 1)
    return jnp.concatenate(resids, axis=1), running[0]


def solution(mesh):
    placed = (
        P("dp", "tensor"),
        P(),
        P("tensor", None),
        P("tensor"),
        P("dp", "tensor"),
        P("tensor"),
        P(None, "tensor"),
        P("tensor"),
    )
    return jax.shard_map(
        body,
        mesh=mesh,
        in_specs=placed,
        out_specs=(P("dp", "tensor"), P("dp", "tensor")),
        check_vma=False,
    )
```

```python
import functools

import jax
import jax.numpy as jnp
from jax import lax
from jax.experimental import pallas as pl
from jax.experimental.pallas import tpu as pltpu
from jax.sharding import PartitionSpec as P

HD = 128
EPS = 1e-05
QUARTERS = ((0, 1, 2), (3,))
RIDE = 1
HALVES = 2
PIECES = 8
LOADS = 4
ROWS = 16
UNROLL = 4
VMEM = 4 * 1024 * 1024
PROJECT_FLOPS = 1e6
BUSY = 4e9


def cost(flops, nbytes):
    return pl.CostEstimate(flops=int(flops), bytes_accessed=int(nbytes), transcendentals=0)


def call(kernel, grid, scalars, in_specs, args, outs, estimate, scratch=(), kinds=None):
    kinds = kinds or [jax.ShapeDtypeStruct] * len(outs)
    return pl.pallas_call(
        kernel,
        grid_spec=pltpu.PrefetchScalarGridSpec(
            num_scalar_prefetch=len(scalars),
            grid=(grid,),
            in_specs=in_specs,
            out_specs=[spec for _, _, spec in outs],
            scratch_shapes=list(scratch),
        ),
        out_shape=[kind(shape, dtype) for (shape, dtype, _), kind in zip(outs, kinds)],
        compiler_params=pltpu.CompilerParams(vmem_limit_bytes=VMEM),
        cost_estimate=estimate,
    )(*scalars, *args)


def whole(shape):
    return pl.BlockSpec(shape, lambda *_: (0,) * len(shape))


IN_PLACE = pl.BlockSpec(memory_space=pl.ANY)
IN_VMEM = pl.BlockSpec(memory_space=pltpu.VMEM)


def in_hbm(array):
    return pltpu.with_memory_space_constraint(array, pltpu.HBM)


def after(value, *others):
    return lax.optimization_barrier((value, *others))[0]


def turned(bits, levels):
    by = levels // 2
    return (bits << by | bits >> levels - by) & (1 << levels) - 1


def swap(block, bit, count):
    levels = count.bit_length() - 1
    masks = (1 << bit, turned(1 << bit, levels))
    route = [
        (d * count + i, d * count + (i ^ masks[d % 2]))
        for d in range(lax.axis_size("dp"))
        for i in range(count)
    ]
    return lax.ppermute(block, ("dp", "tensor"), route)


def mix_rows(part, heads, c, i, size, signs, attn, sent):
    quarter = heads // 4
    at = pl.ds(pl.multiple_of(c * size + i * ROWS, ROWS), ROWS)
    rows = pl.ds(pl.multiple_of(i * ROWS, ROWS), ROWS)

    def head(h):
        return attn[at, pl.ds(h * HD, HD)].astype(jnp.float32) * signs[h]

    mixed = [[] for _ in QUARTERS[part]]
    for h in range(quarter):
        a, b, c2, d = [head(q * quarter + h) for q in range(4)]
        upper, lower = (a + c2, b + d), (a - c2, b - d)
        for k, q in enumerate(QUARTERS[part]):
            one, two = lower if q & 2 else upper
            mixed[k].append(one - two if q & 1 else one + two)
    for k, v in enumerate(mixed):
        step = 1
        while step < quarter:
            for lo in range(quarter):
                if not lo & step:
                    a, b = v[lo], v[lo | step]
                    v[lo], v[lo | step] = a + b, a - b
            step *= 2
        for h in range(quarter):
            cols = pl.ds((k * quarter + h) * HD, HD)
            sent[rows, cols] = v[h].astype(sent.dtype)


def mix_kernel(part, heads, me_ref, *refs):
    ride = part == RIDE
    attn, signs_ref, *refs = refs
    gain_hbm, *refs = refs if ride else (None, *refs)
    *outs, sem = refs
    gain, outs = (outs[-1], outs[:-1]) if ride else (None, outs)
    signs_mem, outs = outs[-1], outs[:-1]
    me = me_ref[0]
    get_signs = pltpu.make_async_copy(signs_ref, signs_mem, sem.at[0])
    get_signs.start()
    step = attn.shape[0] // PIECES
    pieces = []
    if part == 0:
        attn_hbm, attn, outs = attn, outs[-1], outs[:-1]
        for k in range(PIECES):
            rows = pl.ds(k * step, step)
            pieces.append(
                pltpu.make_async_copy(attn_hbm.at[rows, :], attn.at[rows, :], sem.at[2 + k])
            )
            pieces[k].start()
    size = attn.shape[0] // len(outs)
    if ride:
        get_gain = pltpu.make_async_copy(gain_hbm, gain, sem.at[1])
        get_gain.start()
        get_gain.wait()
        sent = outs[0]
        shape = (sent.shape[0] - size, sent.shape[1])
        row = lax.broadcasted_iota(jnp.int32, shape, 0)
        block = jnp.zeros(shape, jnp.float32)
        for k in range(gain.shape[0] // shape[1]):
            piece = gain[pl.ds(k * shape[1], shape[1])].astype(jnp.float32)
            block = jnp.where(row == k, jnp.broadcast_to(piece[None, :], shape), block)
        sent[size:, :] = block.astype(sent.dtype)
    get_signs.wait()
    signs = [(2 * signs_mem[me * heads + h] - 1).astype(jnp.float32) for h in range(heads)]
    for k in range(PIECES):
        if pieces:
            pieces[k].wait()
        c, first = k * step // size, k * step % size // ROWS

        @pl.loop(first, first + step // ROWS)
        def _(i):
            mix_rows(part, heads, c, i, size, signs, attn, outs[c])


def mix(attn, me, signs, gain, part, colors, count):
    rows, cols = attn.shape
    shape = (rows // colors, cols // 4 * len(QUARTERS[part]))
    riding = part == RIDE
    ride = -(-count // 2 * (gain.shape[0] // shape[1]) // ROWS) * ROWS
    outs = []
    for c in range(colors):
        sent = (shape[0] + ride * (riding and c == 0), shape[1])
        outs.append((sent, jnp.bfloat16, whole(sent)))
    kinds = [jax.ShapeDtypeStruct] * len(outs)
    specs, args = [IN_VMEM if part else IN_PLACE, IN_PLACE], [attn if part else in_hbm(attn), in_hbm(signs)]
    scratch = [pltpu.SMEM(signs.shape, signs.dtype)]
    if part == 0:
        outs.append((attn.shape, attn.dtype, IN_VMEM))
        kinds.append(pltpu.VMEM)
    if riding:
        specs.append(IN_PLACE)
        args.append(in_hbm(gain))
        scratch.append(pltpu.VMEM(gain.shape, gain.dtype))
    scratch.append(pltpu.SemaphoreType.DMA((2 + PIECES,)))
    return call(
        functools.partial(mix_kernel, part, cols // HD),
        1,
        [me],
        specs,
        args,
        outs,
        cost(6 * attn.size, 5 * attn.size),
        scratch,
        kinds,
    )


def load_kernel(tbl_ref, w_hbm, out, sem):
    depth, width = out.shape
    count, loads = sem.shape
    step, span = depth // loads, width // count
    copies = []
    for d in range(count):
        cols = pl.ds(pl.multiple_of(tbl_ref[d] * span, span), span)
        for k in range(loads):
            rows = pl.ds(k * step, step)
            to = out.at[rows, pl.ds(d * span, span)]
            copies.append(pltpu.make_async_copy(w_hbm.at[rows, cols], to, sem.at[d, k]))
    for copy in copies:
        copy.start()
    for copy in copies:
        copy.wait()


def load(w, tbl, width, flops=0):
    count = tbl.shape[0]
    return call(
        load_kernel,
        1,
        [tbl],
        [IN_PLACE],
        [in_hbm(w)],
        [((w.shape[0], count * width), w.dtype, IN_VMEM)],
        cost(flops, 0),
        [pltpu.SemaphoreType.DMA((count, LOADS))],
        [pltpu.VMEM],
    )[0]


def combine(order, me, own, recvs, rows):
    v = own[rows, :].astype(jnp.float32)
    for bit, recv in zip(order, recvs):
        flip = (1 - 2 * (me >> bit & 1)).astype(jnp.float32)
        v = recv[rows, :].astype(jnp.float32) + flip * v
    return v


def combine_into(out, orders, scale, me, size, ins):
    per = len(ins) // len(orders)
    for c, order in enumerate(orders):
        own, *recvs = ins[c * per : (c + 1) * per]

        @pl.loop(0, size // ROWS, unroll=UNROLL)
        def _(i):
            rows = pl.ds(pl.multiple_of(i * ROWS, ROWS), ROWS)
            to = pl.ds(pl.multiple_of(c * size + i * ROWS, ROWS), ROWS)
            out[to, :] = (combine(order, me, own, recvs, rows) * scale).astype(out.dtype)


def stage_kernel(order, size, ride, ride_rows, me_ref, *refs):
    riders, ins, out = refs[:ride], refs[ride:-1], refs[-1]
    combine_into(out, [order], 1.0, me_ref[0], size, ins)
    if ride:
        shape = (out.shape[0] - size, out.shape[1])
        row = lax.broadcasted_iota(jnp.int32, shape, 0)
        known = ride_rows
        block = riders[0][size:, :].astype(jnp.float32)
        for rider in riders[1:]:
            more = pltpu.roll(rider[size:, :].astype(jnp.float32), known, 0)
            block = jnp.where(row < known, block, more)
            known *= 2
        out[size:, :] = block.astype(out.dtype)


def stage(block, order, me, size, riders=(), ride_rows=0):
    flat = [*riders, *block]
    shape = riders[0].shape if riders else (size, block[0].shape[1])
    return call(
        functools.partial(stage_kernel, order, size, len(riders), ride_rows),
        1,
        [me],
        [whole(f.shape) for f in flat],
        flat,
        [(shape, jnp.bfloat16, whole(shape))],
        cost(4 * block[0].size * len(flat), 2 * block[0].size * (len(flat) + 2)),
    )[0]


def send_lists(order):
    lists = []
    for s, bit in enumerate(order):
        members = [1 << bit]
        for later in reversed(order[s + 1 :]):
            members = members + [m | 1 << later for m in members]
        lists.append(members)
    return lists + [[0]]


def project_kernel(plan, pieces, counts, adds, width, orders, scale, me_ref, *refs):
    added, refs = refs[: sum(adds)], refs[sum(adds) :]
    raws, rots = refs[: counts[0]], refs[counts[0] : sum(counts)]
    slab, outs = refs[sum(counts)], refs[sum(counts) + 1 :]
    if raws:
        size = outs[-1].shape[0] // len(orders)
        combine_into(outs[-1], orders, scale, me_ref[0], size, raws)
        rots = [outs[-1]]
    for step, (out, lead, add, add_lead) in enumerate(plan):
        acc = None
        for rot, (row, depth) in zip(rots, pieces):
            term = jnp.dot(
                rot[...],
                slab[row : row + depth, step * width : (step + 1) * width],
                preferred_element_type=jnp.float32,
            )
            acc = term if acc is None else acc + term
        if add is not None:
            first = sum(adds[:add])
            more = [a[add_lead].astype(jnp.float32) for a in added[first : first + adds[add]]]
            acc = acc + (more[0] if len(more) == 1 else jnp.concatenate(more, axis=1))
        outs[out][lead] = acc.astype(outs[out].dtype)


def project(
    rows, rots, slab, pieces, spans, width, dtypes, me, adds=(), leads=None, raws=(), orders=(), scale=1.0
):
    plan = [(k, n) for k, (_, count) in enumerate(spans) for n in range(count)]
    if leads is None:
        leads = plan if adds else [(None, None)] * len(plan)
    plan = [(*to, *add) for to, add in zip(plan, leads)]
    flat = [r for raw in raws for r in raw]
    args = [*[a for add in adds for a in add], *flat, *rots, slab]
    counts = [len(flat), len(rots)]
    shapes = [((n, rows, width), dtype) for (_, n), dtype in zip(spans, dtypes)]
    if raws:
        shapes.append(((rows, flat[0].shape[1]), jnp.bfloat16))
    return call(
        functools.partial(
            project_kernel, plan, pieces, counts, [len(a) for a in adds], width, orders, scale
        ),
        1,
        [me],
        [IN_VMEM] * len(args),
        args,
        [(shape, dtype, whole(shape)) for shape, dtype in shapes],
        cost(PROJECT_FLOPS, 0),
    )


def close_kernel(colors, residual, exps, *refs):
    terms, out = refs[:-1], refs[-1]
    per = len(terms) // colors
    width = residual.shape[1] // colors
    for c in range(colors):
        cols = pl.ds(c * width, width)
        own, *recvs = terms[c * per : (c + 1) * per]
        acc = own[0].astype(jnp.float32)
        for recv in recvs:
            acc = acc + recv[0].astype(jnp.float32)
        acc = acc * jnp.exp2(exps[:, cols].astype(jnp.float32))
        out[c] = (residual[:, cols].astype(jnp.float32) + acc).astype(jnp.bfloat16)


def close(residual, exps, terms, at):
    colors = len(terms)
    _, rows, width = terms[0][0].shape
    span = width * colors
    flat = [t for color in terms for t in color]
    shape = (colors, rows, width)
    return call(
        functools.partial(close_kernel, colors),
        1,
        [],
        [
            pl.BlockSpec((rows, span), lambda i: (0, at)),
            pl.BlockSpec((1, span), lambda i: (0, at)),
        ]
        + [whole((1, rows, width))] * len(flat),
        [residual, exps, *flat],
        [(shape, jnp.bfloat16, whole(shape))],
        cost(10 * rows * span, 2 * rows * width * (len(flat) + 2 * colors)),
    )[0]


def kv_kernel(plan, gain_at, counts, colors, has_prev, channels, at, span, tbl_ref, *refs):
    prevs, w, refs = refs[: 2 * has_prev], refs[2 * has_prev], refs[2 * has_prev + 1 :]
    xs, riders, rest = refs[: counts[0]], refs[counts[0] : sum(counts)], refs[sum(counts) :]
    rows, cols = xs[0].shape[-2], w.shape[1]
    product = prevs[0][...] if has_prev else jnp.zeros((rows, cols), jnp.float32)
    square = prevs[1][...] if has_prev else jnp.zeros((rows, HD), jnp.float32)
    for step, blocks in enumerate(plan):
        rider, row = gain_at[step]
        rider = riders[rider]
        for k, lead, c in blocks:
            hidden = xs[k][lead].astype(jnp.float32)
            depth = hidden.shape[1]
            part, col = divmod(at * span + c * depth, rider.shape[1])
            gain = rider[rows // colors :, col : col + depth].astype(jnp.float32)
            gain = gain[row + part : row + part + 1]
            scaled = (hidden * gain).astype(jnp.bfloat16)
            first = pl.multiple_of((tbl_ref[step] + at) * span + c * depth, depth)
            product = product + jnp.dot(
                scaled, w[pl.ds(first, depth), :], preferred_element_type=jnp.float32
            )
            hidden = hidden * hidden
            for b in range(depth // HD):
                square = square + hidden[:, b * HD : (b + 1) * HD]
    if channels:
        exps, out = rest
        mean = jnp.sum(square, axis=1, keepdims=True) / channels
        scale = jnp.exp2(exps[...].astype(jnp.float32))
        out[...] = (product * lax.rsqrt(mean + EPS) * scale).astype(out.dtype)
    else:
        rest[0][...], rest[1][...] = product, square


def kv_step(plan, arrays, riders, gain_at, colors, w_kv, tbl, at, span, prev, exps, channels):
    used = sorted({k for blocks in plan for k, _, _ in blocks})
    xs = [arrays[k] for k in used]
    plan = [[(used.index(k), lead, c) for k, lead, c in blocks] for blocks in plan]
    rows = xs[0].shape[1]
    cols = w_kv.shape[1]
    extra = []
    if channels:
        extra.append(exps)
        outs = [((rows, cols), jnp.bfloat16)]
    else:
        outs = [((rows, cols), jnp.float32), ((rows, HD), jnp.float32)]
    args = [*(prev or ()), w_kv, *xs, *riders, *extra]
    counts = [len(xs), len(riders)]
    return call(
        functools.partial(
            kv_kernel, plan, gain_at, counts, colors, prev is not None, channels, at, span
        ),
        1,
        [tbl],
        [IN_VMEM] * len(args),
        args,
        [(shape, dtype, whole(shape)) for shape, dtype in outs],
        cost(
            2 * rows * span * cols * len(plan), 2 * span * (rows + cols) * len(plan) + 4 * rows * cols
        ),
    )


def gather(x, orders, count):
    colors = x.shape[0]
    arrays, where = [x], {0: [(0, c) for c in range(colors)]}
    levels = len(orders[0])
    for bit in range(levels):
        arrays.append(swap(x, bit, count))
        where[1 << bit] = [(len(arrays) - 1, c) for c in range(colors)]
    for size in range(2, levels + 1):
        for r in range(count):
            if r.bit_count() == size:
                where[r] = []
                for c, order in enumerate(orders):
                    hop = max((b for b in range(levels) if r >> b & 1), key=order.index)
                    k, at = where[r ^ 1 << hop][c]
                    arrays.append(swap(arrays[k][at : at + 1], hop, count))
                    where[r].append((len(arrays) - 1, 0))
    plan = [[(k, at, c) for c, (k, at) in enumerate(blocks)] for blocks in where.values()]
    return arrays, list(zip(where, plan))


def body(attn_out, head_signs, w_out, out_exp, residual, norm_gain, w_kv, kv_exp):
    count = lax.axis_size("tensor")
    levels = count.bit_length() - 1
    me = lax.axis_index("tensor").astype(jnp.int32)
    odd = lax.axis_index("dp") % 2 == 1
    me_arr = me.reshape(1)
    by = levels // 2
    unturned = (me >> by | me << levels - by) & count - 1
    logical = jnp.where(odd, unturned, me).reshape(1)
    depth, (tokens, local) = w_out.shape[0], residual.shape
    channels = local * count
    orders = [list(range(levels))]
    orders.append(orders[0][levels // 2 :] + orders[0][: levels // 2])
    colors = len(orders)
    half = local // HALVES
    wide = half // colors

    def devices(rel):
        far = jnp.array([turned(r, levels) for r in rel], jnp.int32)
        return me ^ jnp.where(odd, far, jnp.array(rel, jnp.int32))

    lists = [send_lists(order) for order in orders]

    def blocks_of(stages, v):
        spans, rel, color = [], [], []
        for s in stages:
            for c in range(colors):
                spans.append((len(rel), len(lists[c][s])))
                rel += lists[c][s]
                color += [v * colors + c] * len(lists[c][s])
        return devices(rel) * (local // wide) + jnp.array(color, jnp.int32), spans

    later = range(1, levels + 1)
    first_tbls = [blocks_of([0], v)[0] for v in range(HALVES)]
    rest_tbls = [blocks_of(later, v)[0] for v in range(HALVES)]
    first_spans, rest_spans = blocks_of([0], 0)[1], blocks_of(later, 0)[1]

    exps = out_exp.reshape(1, -1)
    kv_exps = kv_exp.reshape(1, -1)

    blocks, riders = [], []
    attn = attn_out
    for p in range(len(QUARTERS)):
        mixed = mix(attn, me_arr, head_signs, norm_gain, p, colors, count)
        if p == 0:
            attn = mixed[-1]
        blocks.append([])
        for c, order in enumerate(orders):
            sent = mixed[c]
            blocks[p].append([sent, swap(sent, order[0], count)])
            if p == RIDE and c == 0:
                riders += [sent, blocks[p][c][1]]
    ride_rows = local // riders[0].shape[1]
    slabs = [load(w_out, after(first_tbls[0], sent), wide)]
    here = after(logical, slabs[0])
    for s in range(1, levels):
        sends = []
        for p in range(len(QUARTERS)):
            for c, order in enumerate(orders):
                ride = p == RIDE and c == 0
                send = stage(
                    blocks[p][c], order[s - 1 : s], here, tokens // colors, riders if ride else (), ride_rows
                )
                blocks[p][c] = [send, swap(send, order[s], count)]
                sends.append(send)
                if ride:
                    riders.append(blocks[p][c][-1])
            here = after(logical, *sends)
    slabs.append(load(w_out, after(first_tbls[1], *sends), wide, BUSY))

    gain_at, known = {0: (0, 0)}, [0]
    for t, bit in enumerate(orders[0]):
        gain_at.update({r ^ 1 << bit: (t + 1, ride_rows * k) for k, r in enumerate(known)})
        known += [r ^ 1 << bit for r in known]

    bf16, f32 = jnp.bfloat16, jnp.float32
    cut = blocks[0][0][0].shape[1]
    pieces = [(0, cut), (cut, depth - cut)]
    scale = head_signs.shape[0] ** -0.5
    closing = [order[levels - 1 :] for order in orders]
    *prevs, rot = project(
        tokens, [], slabs[0], pieces[:1], first_spans, wide, [f32] * colors, after(logical, slabs[1]),
        raws=blocks[0], orders=closing, scale=scale,
    )
    rots = [rot]
    *sends, rot = project(
        tokens, [], slabs[0], pieces[1:], first_spans, wide, [bf16] * colors, logical,
        [[p] for p in prevs], raws=blocks[1], orders=closing, scale=scale,
    )
    rots.append(rot)
    received = []
    for v in range(HALVES):
        if v:
            sends = project(
                tokens, rots, slabs[v], pieces, first_spans, wide, [bf16] * colors, logical
            )
        received.append([swap(send, order[0], count) for send, order in zip(sends, orders)])

    leads = []
    for s in later:
        for c in range(colors):
            n = len(lists[c][s])
            leads += [(c, k + n * (s < levels)) for k in range(n)]
    dtypes = [bf16 if s == 1 and levels > 1 else f32 for s in later for _ in range(colors)]

    def keys_and_values(run, running, last):
        v, arrays, run = run
        return kv_step(
            [plan for _, plan in run],
            arrays,
            riders,
            [gain_at[r] for r, _ in run],
            colors,
            w_kv,
            devices([r for r, _ in run]) * HALVES,
            v,
            half,
            running,
            kv_exps,
            channels * last,
        )

    resids, runs, running = [], [], None
    for v in range(HALVES):
        adds = [[r] for r in received[v]]
        slab = load(w_out, after(rest_tbls[v], *sends), wide)
        parts = project(
            tokens, rots, slab, pieces, rest_spans, wide, dtypes, logical, adds, leads
        )
        sends = parts[:colors]
        terms = []
        for c, order in enumerate(orders):
            recvs = []
            for s in range(1, levels):
                send = parts[(s - 1) * colors + c]
                if recvs:
                    size = send.shape[0]
                    for recv in recvs:
                        send = send + recv[size : 2 * size].astype(f32)
                    send = send.astype(bf16)
                recvs.append(swap(send, order[s], count))
            terms.append([parts[(levels - 1) * colors + c], *recvs])
        out = close(residual, exps, terms, v)
        resids += list(out)
        arrays, found = gather(out, orders, count)
        for far in (False, True):
            run = [b for b in found if (b[0].bit_count() > 1) == far]
            if run and not far:
                running = keys_and_values((v, arrays, run), running, False)
            elif run:
                runs.append((v, arrays, run))

    for k, run in enumerate(runs):
        running = keys_and_values(run, running, k == len(runs) - 1)
    return jnp.concatenate(resids, axis=1), running[0]


def solution(mesh):
    placed = (
        P("dp", "tensor"),
        P(),
        P("tensor", None),
        P("tensor"),
        P("dp", "tensor"),
        P("tensor"),
        P(None, "tensor"),
        P("tensor"),
    )
    return jax.shard_map(
        body,
        mesh=mesh,
        in_specs=placed,
        out_specs=(P("dp", "tensor"), P("dp", "tensor")),
        check_vma=False,
    )
```
